32 devices in a mesh: stream: 2 (over x), dp: 16 (over z, y, core).
Axes of the slice: x: 2, y: 2, z: 4, core: 2. Of those that a mesh axis runs over, the one named last changes fastest.
Arguments:
- tokens: bfloat16 [2, 8192, 1152], P('stream', 'dp'), may hold values from -6 to 6
- condition: bfloat16 [2, 48, 1152], P('stream', 'dp'), may hold values from -6 to 6
- segments: int32 [2, 8192], P('stream', 'dp'), may hold values from 0 to 2, as said below
- positions: int32 [2, 8192], P('stream', 'dp'), may hold values from 0 to 255, as said below
- buckets: int32 [256, 256], replicated, may hold values from 0 to 960
- modulator: bfloat16 [1152, 6912], P('dp'), may hold values from -0.1875 to 0.1875
- modulator_bias: bfloat16 [6912], P('dp'), may hold values from -3 to 3
- projector: bfloat16 [1152, 3456], P('dp'), may hold values from -0.1875 to 0.1875
- projector_bias: bfloat16 [2304], P('dp'), may hold values from -3 to 3
- position_table: bfloat16 [16, 961], replicated, may hold values from -6 to 6
- output_weight: bfloat16 [1152, 1152], P('dp'), may hold values from -0.75 to 0.75
- output_bias: bfloat16 [1152], P('dp'), may hold values from -3 to 3
- up_weight: bfloat16 [1152, 4608], P('dp'), may hold values from -0.1875 to 0.1875
- up_bias: bfloat16 [4608], P('dp'), may hold values from -3 to 3
- down_weight: bfloat16 [4608, 1152], P('dp'), may hold values from -0.09375 to 0.09375
- down_bias: bfloat16 [1152], P('dp'), may hold values from -3 to 3
- cotangent: bfloat16 [2, 8192, 1152], P('stream', 'dp'), may hold values from -6 to 6
Outputs:
- result: bfloat16 [2, 8192, 1152], P('stream', 'dp')
- grad_tokens: float32 [2, 8192, 1152], P('stream', 'dp')
- grad_condition: float32 [2, 48, 1152], P('stream', 'dp')
- grad_modulator: float32 [1152, 6912], P('dp')
- grad_modulator_bias: float32 [6912], P('dp')
- grad_projector: float32 [1152, 3456], P('dp')
- grad_projector_bias: float32 [2304], P('dp')
- grad_position_table: float32 [16, 961], replicated
- grad_output_weight: float32 [1152, 1152], P('dp')
- grad_output_bias: float32 [1152], P('dp')
- grad_up_weight: float32 [1152, 4608], P('dp')
- grad_up_bias: float32 [4608], P('dp')
- grad_down_weight: float32 [4608, 1152], P('dp')
- grad_down_bias: float32 [1152], P('dp')
The draws below stay inside these ranges and needn't reach their ends.
Inputs may be any that keep to these rules, and one draw needn't show every extreme that they name: `segments`: rows come in aligned blocks of 512, each holding image slots 0, 1, 2 in this order, an image's rows together. In the first pass each slot holds 1 to 256 rows; in the second pass slots 0 and 1 hold 256 rows each and slot 2 none. `positions`: A row's place among its image's 256 tokens, rising within an image; in the second pass every place in order.
All inputs are finite; a program needn't handle non-finite values.
Results may differ from the reference program's by a relative error of at most 0.014.
The reference program's roundings to bfloat16 on the way count: a program that leaves them out, or rounds other values in their place, can miss the bound.
Values may be sent and summed in bfloat16 or wider, within the bound.
A program may use at most 512 MiB of HBM per device.

```python
from functools import partial
import jax
import jax.numpy as jnp
from jax import lax

D = 1152
H = 16
FF = 4608
HEAD = 72
P_SIZE = 256
BUCKETS = 961
TOKENS = 8192
IMAGES = 48


def pack_layout(key):
    blocks = TOKENS // (2 * P_SIZE)
    breakpoints = jax.random.randint(jax.random.fold_in(key, 11), (blocks, 2), 1, P_SIZE)
    lower = jnp.min(breakpoints, axis=1)
    upper = jnp.max(breakpoints, axis=1)
    sizes = jnp.stack([P_SIZE - lower, P_SIZE - upper + lower, upper], axis=1).astype(jnp.int32)
    second = sizes[:, 0:1]
    third = sizes[:, 0:1] + sizes[:, 1:2]
    rows_all = jnp.arange(2 * P_SIZE, dtype=jnp.int32)[None, :]
    slot_ids = (rows_all >= second).astype(jnp.int32) + (rows_all >= third).astype(jnp.int32)
    starts = jnp.concatenate([jnp.zeros((blocks, 1), jnp.int32), second, third], axis=1)
    offsets = rows_all - jnp.take_along_axis(starts, slot_ids, axis=1)
    key_list = jax.random.split(jax.random.fold_in(key, 12), blocks * 3)
    orders = jax.vmap(lambda one_key: jax.random.permutation(one_key, P_SIZE))(key_list).reshape(blocks, 3, P_SIZE)
    ranks = jnp.argsort(orders, axis=-1).astype(jnp.int32)
    places = jnp.arange(P_SIZE, dtype=jnp.int32)
    ordering = jnp.where(ranks < sizes[:, :, None], places, P_SIZE + places)
    kept_places = jnp.argsort(ordering, axis=-1).astype(jnp.int32).reshape(blocks, 3 * P_SIZE)
    masked_places = jnp.take_along_axis(kept_places, slot_ids * P_SIZE + offsets, axis=1)
    full_slots = jnp.broadcast_to(rows_all // P_SIZE, (blocks, 2 * P_SIZE))
    full_places = jnp.broadcast_to(rows_all % P_SIZE, (blocks, 2 * P_SIZE))
    segment_rows = jnp.stack([slot_ids.reshape(-1), full_slots.reshape(-1)]).astype(jnp.int32)
    place_rows = jnp.stack([masked_places.reshape(-1), full_places.reshape(-1)]).astype(jnp.int32)
    return (segment_rows, place_rows)


def draw_segments(key, part):
    layout = pack_layout(key)
    return layout[0]


def draw_positions(key, part):
    layout = pack_layout(key)
    return layout[1]


def set_ends(drawn, key, low, high):
    index_at = [jax.random.randint(jax.random.fold_in(key, axis), (), 0, length) for axis, length in enumerate(drawn.shape)]
    longest = drawn.shape.index(max(drawn.shape))
    beside = index_at[:longest] + [(index_at[longest] + 1) % drawn.shape[longest]] + index_at[longest + 1:]
    return drawn.at[tuple(index_at)].set(low).at[tuple(beside)].set(high)


def raised(result, rng, source, target, shards_of, factor):
    owner, partner = [(jnp.arange(result.shape[axis_at]) // (result.shape[axis_at] // shards_of)).reshape([-1 if axis == axis_at else 1 for axis in range(result.ndim)]) for axis_at in (source, target)]
    chosen = jax.random.permutation(rng, shards_of)[partner]
    strong = (owner == chosen) | (owner == (partner + shards_of // 2) % shards_of)
    return jnp.where(strong, factor * result, result)


def steps_of(key, dims, pieces, smallest, top_value):
    gain = 1.0
    for position, parts in pieces:
        steps = jax.random.uniform(jax.random.fold_in(jax.random.fold_in(key, 6), position), (parts,), jnp.float32, smallest / len(pieces), top_value / len(pieces))
        gain = gain * jnp.repeat(jnp.exp(steps), dims[position] // parts).reshape((-1,) + (1,) * (len(dims) - 1 - position))
    return gain


def normal_values(key, shape, deviation, limit, cuts=(), kind=jnp.bfloat16):
    drawn = jax.random.normal(key, shape, jnp.float32) * deviation
    if len(cuts) > 0:
        drawn = steps_of(key, shape, cuts, -0.22, 0.18) * drawn
    return jnp.clip(drawn, min=-limit, max=limit).astype(kind)


def gaussian_with(key, dims, scale, reach, cuts, heavy, held_as=jnp.bfloat16):
    entries = scale * jax.random.normal(key, dims, jnp.float32)
    if cuts:
        entries = entries * steps_of(key, dims, cuts, -0.22, 0.18)
    return jnp.clip(raised(entries, jax.random.fold_in(key, 3), *heavy), -reach, reach).astype(held_as)


def setup_inputs(seed: int = 0) -> dict:
    keys = jax.random.split(jax.random.key(seed), 18)
    return {
        "tokens": normal_values(keys[0], (2, TOKENS, D), 1.0, 6.0, ((0, 2), (1, 16))),
        "condition": normal_values(keys[1], (2, IMAGES, D), 1.0, 6.0, ((0, 2), (1, 16))),
        "segments": draw_segments(jax.random.fold_in(keys[17], 71), 0),
        "positions": draw_positions(jax.random.fold_in(keys[17], 71), 0),
        "buckets": set_ends(jax.random.randint(keys[4], (P_SIZE, P_SIZE), 0, BUCKETS), jax.random.fold_in(keys[4], 1), 0, BUCKETS - 1).astype(jnp.int32),
        "modulator": normal_values(keys[5], (D, 6 * D), D ** -0.5, 0.1875, ((0, 16),)),
        "modulator_bias": normal_values(keys[6], (6 * D,), 0.5, 3.0, ((0, 16),)),
        "projector": normal_values(keys[7], (D, 3 * D), D ** -0.5, 0.1875, ((0, 16),)),
        "projector_bias": normal_values(keys[8], (2 * D,), 0.5, 3.0, ((0, 16),)),
        "position_table": normal_values(keys[9], (H, BUCKETS), 1.0, 6.0),
        "output_weight": normal_values(keys[10], (D, D), (D // 16) ** -0.5, 0.75, ((0, 16),)),
        "output_bias": normal_values(keys[11], (D,), 0.5, 3.0, ((0, 16),)),
        "up_weight": normal_values(keys[12], (D, FF), D ** -0.5, 0.1875, ((0, 16),)),
        "up_bias": normal_values(keys[13], (FF,), 0.5, 3.0, ((0, 16),)),
        "down_weight": normal_values(keys[14], (FF, D), FF ** -0.5, 0.09375, ((0, 16),)),
        "down_bias": normal_values(keys[15], (D,), 0.5, 3.0, ((0, 16),)),
        "cotangent": gaussian_with(keys[16], (2, TOKENS, D), 1.0, 6.0, ((0, 2), (1, 16)), (1, 2, 16, 2.0)),
    }


norm_epsilon = 1e-06
masked_score = -1000000000.0

@jax.custom_vjp
def low(v):
    return lax.optimization_barrier(v.astype(jnp.bfloat16)).astype(jnp.float32)

@jax.custom_vjp
def low_back(v):
    return v

def low_keep(v):
    return (low(v), None)

def low_pass(kept, grad):
    return (grad,)

def back_keep(v):
    return (v, None)

def back_low(kept, grad):
    return (low(grad),)
low.defvjp(low_keep, low_pass)
low_back.defvjp(back_keep, back_low)

def normalize(values):
    center = values - lax.optimization_barrier(jnp.mean(values, axis=-1, keepdims=True))
    return center * lax.rsqrt(lax.optimization_barrier(jnp.mean(center * center, axis=-1, keepdims=True)) + norm_epsilon)

def product(left, right):
    return jnp.dot(left, right, precision=lax.Precision.HIGHEST)

def layer_pack(weight_set, item_set):
    projector, projector_bias, output_weight, output_bias, up_weight, up_bias, down_weight, down_bias, pos_grid = weight_set
    inputs, slot_ids, places, pack_mod = item_set
    per_token = jnp.take(pack_mod, slot_ids, axis=0)
    shift_attn, scale_attn, gate_attn, shift_mlp, scale_mlp, gate_mlp = jnp.split(per_token, 6, axis=1)
    hidden_one = low(normalize(inputs) * (1.0 + scale_attn) + shift_attn)
    zero_middle = jnp.zeros((D,), inputs.dtype)
    full_bias = jnp.concatenate([projector_bias[:D], zero_middle, projector_bias[D:]])
    packed = low(low_back(product(hidden_one, projector) + full_bias))
    shaped = packed.reshape(packed.shape[0], 3, H, HEAD)
    queries, keys_all, values_all = (shaped[:, 0], shaped[:, 1], shaped[:, 2])
    pair_index = places[:, None] * P_SIZE + places[None, :]
    bias_grid = jnp.take(pos_grid, pair_index, axis=1)
    scores = jnp.einsum('qhd,khd->hqk', queries, keys_all, precision=lax.Precision.HIGHEST) * HEAD ** (-0.5)
    scores = low_back(scores + bias_grid)
    same_image = slot_ids[:, None] == slot_ids[None, :]
    scores = jnp.where(same_image[None], scores, masked_score)
    maximum = lax.optimization_barrier(jnp.max(scores, axis=-1, keepdims=True))
    exponent = jnp.exp(scores - maximum)
    weights = low(exponent / lax.optimization_barrier(jnp.sum(exponent, axis=-1, keepdims=True)))
    attended = jnp.einsum('hqk,khd->qhd', weights, values_all, precision=lax.Precision.HIGHEST)
    attended = low(low_back(attended.reshape(inputs.shape[0], D)))
    branch_attn = low_back(product(attended, output_weight) + output_bias)
    middle = inputs + gate_attn * branch_attn
    hidden_two = low(normalize(middle) * (1.0 + scale_mlp) + shift_mlp)
    up_output = low_back(product(hidden_two, up_weight) + up_bias)
    activation = low(jax.nn.gelu(up_output, approximate=True))
    branch_mlp = low_back(product(activation, down_weight) + down_bias)
    return middle + gate_mlp * branch_mlp

def forward(tokens, condition, modulator, modulator_bias, projector, projector_bias, position_table, output_weight, output_bias, up_weight, up_bias, down_weight, down_bias, segments, positions, buckets):
    activated = low(jax.nn.silu(condition))
    modulation = low_back(jnp.einsum('sid,de->sie', activated, modulator, precision=lax.Precision.HIGHEST) + modulator_bias)
    pos_grid = jnp.take(position_table, buckets.reshape(-1), axis=1)
    block_count = TOKENS // P_SIZE
    item_set = (tokens.reshape(block_count, 2 * P_SIZE, D), segments.reshape(block_count, 2 * P_SIZE), positions.reshape(block_count, 2 * P_SIZE), modulation.reshape(block_count, 3, 6 * D))
    weight_set = (projector, projector_bias, output_weight, output_bias, up_weight, up_bias, down_weight, down_bias, pos_grid)
    pack_step = jax.checkpoint(partial(layer_pack, weight_set))
    out_blocks = lax.map(pack_step, item_set)
    return out_blocks.reshape(2, TOKENS, D)

def reference(tokens, condition, segments, positions, buckets, modulator, modulator_bias, projector, projector_bias, position_table, output_weight, output_bias, up_weight, up_bias, down_weight, down_bias, cotangent):
    floats = tuple((item.astype(jnp.float32) for item in (tokens, condition, modulator, modulator_bias, projector, projector_bias, position_table, output_weight, output_bias, up_weight, up_bias, down_weight, down_bias)))

    def forward_fn(tokens_f, condition_f, modulator_f, modulator_bias_f, projector_f, projector_bias_f, table_f, output_f, output_bias_f, up_f, up_bias_f, down_f, down_bias_f):
        return forward(tokens_f, condition_f, modulator_f, modulator_bias_f, projector_f, projector_bias_f, table_f, output_f, output_bias_f, up_f, up_bias_f, down_f, down_bias_f, segments, positions, buckets)
    output, pullback = jax.vjp(forward_fn, *floats)
    grads = pullback(cotangent.astype(jnp.float32))
    return (output.astype(jnp.bfloat16), grads[0], grads[1], grads[2], grads[3], grads[4], grads[5], grads[6], grads[7], grads[8], grads[9], grads[10], grads[11], grads[12])
```

```python
import functools

import jax
import jax.numpy as jnp
from jax import lax
from jax.experimental import pallas as pl
from jax.experimental.pallas import tpu as pltpu
from jax.sharding import PartitionSpec as P

norm_epsilon = 1e-06
masked_score=-1000000000.0

def grid_kernel(table_ref, buckets_ref, grid_ref):
    chunks = table_ref.shape[1]
    for half in range(buckets_ref.shape[1] // 128):
        span = slice(128 * half, 128 * half + 128)
        index = buckets_ref[:, span]
        low, high = index & 127, index >> 7
        total = jnp.zeros(index.shape, jnp.float32)
        for chunk in range(chunks):
            row = jnp.broadcast_to(table_ref[0, chunk : chunk + 1], index.shape)
            found = jnp.take_along_axis(row, low, axis=1)
            total = jnp.where(high == chunk, found, total)
        grid_ref[0, :, span] = total.astype(jnp.bfloat16)

def bias_grid(table, buckets):
    heads, count = table.shape
    chunks = -(-count // 128)
    wide = jnp.pad(table.astype(jnp.float32), ((0, 0), (0, chunks * 128 - count)))
    return pl.pallas_call(
        grid_kernel,
        grid=(heads,),
        in_specs=[pl.BlockSpec((1, chunks, 128), lambda h: (h, 0, 0)),
                  pl.BlockSpec(buckets.shape, lambda h: (0, 0))],
        out_specs=pl.BlockSpec((1,) + buckets.shape, lambda h: (h, 0, 0)),
        out_shape=jax.ShapeDtypeStruct((heads,) + buckets.shape, jnp.bfloat16),
    )(wide.reshape(heads, chunks, 128), buckets)

def hist_kernel(grad_ref, buckets_ref, out_ref):
    rows, heads, width = grad_ref.shape
    chunks = out_ref.shape[0] // heads
    @pl.when(pl.program_id(0) == 0)
    def _():
        out_ref[...] = jnp.zeros_like(out_ref)
    total = out_ref[...]
    for row in range(rows):
        index = buckets_ref[row : row + 1, :]
        low, high = index & 127, index >> 7
        mask = lax.broadcasted_iota(jnp.int32, (chunks, width), 0) == high
        values = jnp.where(mask[None], grad_ref[row][:, None, :], 0.0)
        left = values.reshape(heads * chunks, width).astype(jnp.bfloat16)
        right = (lax.broadcasted_iota(jnp.int32, (128, width), 0) == low).astype(jnp.float32).astype(jnp.bfloat16)
        total += lax.dot_general(left, right, (((1,), (1,)), ((), ())), preferred_element_type=jnp.float32)
    out_ref[...] = total

def table_histogram(grad, buckets, count):
    places, heads, width = grad.shape
    chunks = -(-count // 128)
    step = 16
    out = pl.pallas_call(
        hist_kernel,
        grid=(places // step,),
        in_specs=[pl.BlockSpec((step, heads, width), lambda a: (a, 0, 0)),
                  pl.BlockSpec((step, width), lambda a: (a, 0))],
        out_specs=pl.BlockSpec((heads * chunks, 128), lambda a: (0, 0)),
        out_shape=jax.ShapeDtypeStruct((heads * chunks, 128), jnp.float32),
    )(grad, buckets)
    return out.reshape(heads, chunks * 128)[:, :count]

def head_windows(heads, head_width):
    found = []
    for head in range(heads):
        start = head * head_width
        base = start // 128 * 128
        stop = -(-(start + head_width) // 128) * 128
        found.append((base, stop - base, start - base))
    return found

def lane_mask(rows, width, offset, head_width):
    lane = lax.broadcasted_iota(jnp.int32, (rows, width), 1)
    return (lane >= offset) & (lane < offset + head_width)

def nt(left, right):
    return lax.dot_general(left, right, (((1,), (1,)), ((), ())), preferred_element_type=jnp.float32)
def tn(left, right):
    return lax.dot_general(left, right, (((0,), (0,)), ((), ())), preferred_element_type=jnp.float32)
def nn(left, right):
    return lax.dot_general(left, right, (((1,), (0,)), ((), ())), preferred_element_type=jnp.float32)

def attend_forward_kernel(heads, packed_ref, frame_row_ref, frame_column_ref, grid_ref, attended_ref, placed_ref, weights_ref, mixed_ref):
    rows, width3 = packed_ref.shape
    frames = placed_ref.shape[0]
    places = grid_ref.shape[1]
    width = width3 // 3
    head_width = width // heads
    scale = head_width ** (-0.5)
    place = (lax.broadcasted_iota(jnp.int32, (frames, rows), 0) == frame_row_ref[...]).astype(jnp.float32).astype(jnp.bfloat16)
    for part in range(3):
        span = slice(part * width, part * width + width)
        placed_ref[:, span] = nn(place, packed_ref[:, span]).astype(jnp.bfloat16)
    filled = nt(jnp.ones((8, rows), jnp.bfloat16), place)[0:1] > 0.5
    filled_f = jnp.where(filled, 0.0, masked_score)
    mixed_ref[...] = jnp.zeros_like(mixed_ref)
    for image in range(frames // places):
        span_rows = slice(image * places, image * places + places)
        offset_row = filled_f[:, span_rows]
        for head, (base, wide, offset) in enumerate(head_windows(heads, head_width)):
            mask = lane_mask(places, wide, offset, head_width)
            query = placed_ref[span_rows, base : base + wide]
            key = placed_ref[span_rows, width + base : width + base + wide]
            value = placed_ref[span_rows, 2 * width + base : 2 * width + base + wide]
            query = jnp.where(mask, query, jnp.zeros_like(query))
            scores = nt(query, key) * scale + grid_ref[head].astype(jnp.float32)
            scores = jnp.where(offset_row < 0.0, masked_score, scores)
            exponent = jnp.exp(scores - jnp.max(scores, axis=-1, keepdims=True))
            weights = (exponent / jnp.sum(exponent, axis=-1, keepdims=True)).astype(jnp.bfloat16)
            weights_ref[image, head] = weights
            mixture = nn(weights, value).astype(jnp.bfloat16)
            before = mixed_ref[span_rows, base : base + wide]
            mixed_ref[span_rows, base : base + wide] = jnp.where(mask, mixture, before)
    back = (lax.broadcasted_iota(jnp.int32, (rows, frames), 1) == frame_column_ref[...]).astype(jnp.float32).astype(jnp.bfloat16)
    attended_ref[...] = nn(back, mixed_ref[...]).astype(jnp.bfloat16)

def attend_forward(packed, slots, places, grid):
    rows = packed.shape[0]
    heads, image, _ = grid.shape
    frame = slots * image + places
    frames = 3 * image
    width = packed.shape[1] // 3
    return pl.pallas_call(
        functools.partial(attend_forward_kernel, heads),
        out_shape=(jax.ShapeDtypeStruct((rows, width), jnp.bfloat16),
                   jax.ShapeDtypeStruct((frames, 3 * width), jnp.bfloat16),
                   jax.ShapeDtypeStruct((3, heads, image, image), jnp.bfloat16)),
        scratch_shapes=[pltpu.VMEM((frames, width), jnp.bfloat16)],
        compiler_params=pltpu.CompilerParams(vmem_limit_bytes=48 * 2**20),
    )(packed, frame[None, :], frame[:, None], grid)

def attend_backward_kernel(heads, placed_ref, weights_ref, upstream_ref, frame_row_ref, frame_column_ref, packed_grad_ref, grid_grad_ref, up_ref, grad_ref, bias_ref):
    frames, width3 = placed_ref.shape
    rows = upstream_ref.shape[0]
    places = weights_ref.shape[2]
    width = width3 // 3
    head_width = width // heads
    scale = head_width ** (-0.5)
    place = (lax.broadcasted_iota(jnp.int32, (frames, rows), 0) == frame_row_ref[...]).astype(jnp.float32).astype(jnp.bfloat16)
    up_ref[...] = nn(place, upstream_ref[...]).astype(jnp.bfloat16)
    grad_ref[...] = jnp.zeros_like(grad_ref)
    for head, (base, wide, offset) in enumerate(head_windows(heads, head_width)):
        mask = lane_mask(places, wide, offset, head_width)
        for image in range(frames // places):
            span_rows = slice(image * places, image * places + places)
            spans = [slice(part * width + base, part * width + base + wide) for part in range(3)]
            query, key = [jnp.where(mask, t, jnp.zeros_like(t)) for t in (placed_ref[span_rows, spans[0]], placed_ref[span_rows, spans[1]])]
            value = placed_ref[span_rows, spans[2]]
            upstream = up_ref[span_rows, spans[0]]
            upstream = jnp.where(mask, upstream, jnp.zeros_like(upstream))
            weights = weights_ref[image, head]
            weights_f = weights.astype(jnp.float32)
            weight_grads = nt(upstream, value)
            inner = jnp.sum(weight_grads * weights_f, axis=-1, keepdims=True)
            score_grads_f = weights_f * (weight_grads - inner)
            score_grads = score_grads_f.astype(jnp.bfloat16)
            if image == 0:
                bias_ref[...] = score_grads_f
            else:
                bias_ref[...] += score_grads_f
            grad_ref[span_rows, spans[0]] += (nn(score_grads, key) * scale).astype(jnp.bfloat16)
            grad_ref[span_rows, spans[1]] += (tn(score_grads, query) * scale).astype(jnp.bfloat16)
            grad_ref[span_rows, spans[2]] += tn(weights, upstream).astype(jnp.bfloat16)
        grid_grad_ref[:, head, :] = bias_ref[...]
    back = (lax.broadcasted_iota(jnp.int32, (rows, frames), 1) == frame_column_ref[...]).astype(jnp.float32).astype(jnp.bfloat16)
    for part in range(3):
        span = slice(part * width, part * width + width)
        packed_grad_ref[:, span] = nn(back, grad_ref[:, span]).astype(jnp.bfloat16)

def attend_backward(placed, weights, upstream, slots, places):
    rows, width = upstream.shape
    _, heads, image, _ = weights.shape
    frame = slots * image + places
    frames = 3 * image
    return pl.pallas_call(
        functools.partial(attend_backward_kernel, heads),
        out_shape=(jax.ShapeDtypeStruct((rows, 3 * width), jnp.bfloat16),
                   jax.ShapeDtypeStruct((image, heads, image), jnp.float32)),
        scratch_shapes=[pltpu.VMEM((frames, width), jnp.bfloat16),
                        pltpu.VMEM((frames, 3 * width), jnp.bfloat16),
                        pltpu.VMEM((image, image), jnp.float32)],
        compiler_params=pltpu.CompilerParams(vmem_limit_bytes=56 * 2**20),
    )(placed, weights, upstream, frame[None, :], frame[:, None])

def normalize(values):
    center = values - jnp.mean(values, axis=-1, keepdims=True)
    inverse = lax.rsqrt(jnp.mean(center * center, axis=-1, keepdims=True) + norm_epsilon)
    return (center * inverse, inverse)


def normalize_back(normed, inverse, upstream):
    return inverse * (
        upstream
        - jnp.mean(upstream, axis=-1, keepdims=True)
        - normed * jnp.mean(upstream * normed, axis=-1, keepdims=True)
    )


def smooth_gelu(values):
    return jax.nn.gelu(values, approximate=True)


def shards(
    tokens,
    condition,
    segments,
    positions,
    buckets,
    modulator,
    modulator_bias,
    projector,
    projector_bias,
    position_table,
    output_weight,
    output_bias,
    up_weight,
    up_bias,
    down_weight,
    down_bias,
    cotangent,
):
    heads, bucket_count = position_table.shape
    image_tokens = buckets.shape[0]
    rows, model_width = tokens.shape[1], tokens.shape[2]
    images = condition.shape[1]
    shard = modulator.shape[0]
    feed_width = up_weight.shape[1]
    dp_index = lax.axis_index("dp")
    stream_index = lax.axis_index("stream")
    low = jnp.bfloat16
    full = jnp.float32

    def gather(part):
        return lax.all_gather(part, "dp", axis=0, tiled=True)

    inputs = tokens[0].astype(full)
    slot_ids, places = segments[0], positions[0]
    silu_value, silu_back = jax.vjp(jax.nn.silu, condition[0].astype(full))
    activated = silu_value.astype(low)
    activated_both = lax.all_gather(activated, ("stream", "dp"), axis=0, tiled=True)
    slots = activated_both.shape[0]
    activated_own = lax.dynamic_slice(activated_both, (0, dp_index * shard), (slots, shard))
    stream_slots = slots // 2
    partial = jnp.dot(
        lax.dynamic_slice(activated_own, (stream_index * stream_slots, 0), (stream_slots, shard)),
        modulator,
        preferred_element_type=full,
    )
    bias_parts = (modulator_bias, projector_bias, output_bias, up_bias, down_bias)
    bias_all = lax.all_gather(jnp.concatenate(bias_parts), "dp", axis=0)
    bias_full = []
    start = 0
    for part in bias_parts:
        bias_full.append(bias_all[:, start : start + part.shape[0]].reshape(-1).astype(full))
        start += part.shape[0]
    modulation = (
        lax.psum_scatter(partial, "dp", scatter_dimension=0, tiled=True) + bias_full[0]
    )
    projector_all = gather(projector)
    output_all = gather(output_weight)
    up_all = gather(up_weight)
    down_all = gather(down_weight)
    grid = bias_grid(position_table, buckets)
    local = slot_ids[:, None]
    per_token = jnp.where(
        local == 0, modulation[0:1], jnp.where(local == 1, modulation[1:2], modulation[2:3])
    )
    shift_attn, scale_attn, gate_attn, shift_mlp, scale_mlp, gate_mlp = jnp.split(
        per_token, 6, axis=1
    )
    normed_one, inverse_one = normalize(inputs)
    hidden_one = (normed_one * (1.0 + scale_attn) + shift_attn).astype(low)
    packed_bias = jnp.concatenate(
        [bias_full[1][:model_width], jnp.zeros((model_width,), full), bias_full[1][model_width:]]
    )
    packed = (
        jnp.dot(hidden_one, projector_all, preferred_element_type=full) + packed_bias
    ).astype(low)
    attended, placed, weights = attend_forward(packed, slot_ids, places, grid)
    branch_attn = jnp.dot(attended, output_all, preferred_element_type=full) + bias_full[2]
    middle = inputs + gate_attn * branch_attn
    normed_two, inverse_two = normalize(middle)
    hidden_two = (normed_two * (1.0 + scale_mlp) + shift_mlp).astype(low)
    up_output = jnp.dot(hidden_two, up_all, preferred_element_type=full) + bias_full[3]
    activation, gelu_back = jax.vjp(lambda v: jax.nn.gelu(v, approximate=True), up_output)
    activation_low = activation.astype(low)
    branch_mlp = jnp.dot(activation_low, down_all, preferred_element_type=full) + bias_full[4]
    result = (middle + gate_mlp * branch_mlp).astype(low)

    upstream = cotangent[0].astype(full)
    mlp_grad = (gate_mlp * upstream).astype(low)
    gate_mlp_grad = branch_mlp * upstream

    def scatter(grad):
        part = lax.psum_scatter(grad.astype(low), "dp", scatter_dimension=0, tiled=True)
        return lax.psum(part, "stream").astype(full)

    down_grad = scatter(
        jnp.einsum("tf,td->fd", activation_low, mlp_grad, preferred_element_type=full)
    )
    activation_grad = jnp.einsum("td,fd->tf", mlp_grad, down_all, preferred_element_type=full)
    up_grad_low = gelu_back(activation_grad)[0].astype(low)
    up_grad = scatter(
        jnp.einsum("td,tf->df", hidden_two, up_grad_low, preferred_element_type=full)
    )
    hidden_two_grad = jnp.einsum(
        "tf,df->td", up_grad_low, up_all, preferred_element_type=full
    )
    middle_grad = upstream + normalize_back(
        normed_two, inverse_two, hidden_two_grad * (1.0 + scale_mlp)
    )
    attn_grad = (gate_attn * middle_grad).astype(low)
    gate_attn_grad = branch_attn * middle_grad
    output_grad = scatter(
        jnp.einsum("td,te->de", attended, attn_grad, preferred_element_type=full)
    )
    attended_grad = jnp.einsum(
        "te,de->td", attn_grad, output_all, preferred_element_type=full
    ).astype(low)
    packed_grad, grid_grad = attend_backward(placed, weights, attended_grad, slot_ids, places)
    projector_grad = scatter(
        jnp.einsum("td,te->de", hidden_one, packed_grad, preferred_element_type=full)
    )
    table_grad = table_histogram(grid_grad, buckets, bucket_count)
    packed_sums = jnp.sum(packed_grad.astype(full), axis=0)
    sums = (
        table_grad.reshape(-1),
        packed_sums[:model_width],
        packed_sums[2 * model_width :],
        jnp.sum(attn_grad.astype(full), axis=0),
        jnp.sum(up_grad_low.astype(full), axis=0),
        jnp.sum(mlp_grad.astype(full), axis=0),
    )
    small = lax.psum(jnp.concatenate(sums), ("stream", "dp"))
    table_count = heads * bucket_count
    table_total = small[:table_count].reshape(heads, bucket_count)
    bias_grads = []
    start = table_count
    for part in bias_parts[1:]:
        size = part.shape[0]
        bias_grads.append(lax.dynamic_slice(small, (start + dp_index * size,), (size,)))
        start += size * (model_width // shard)
    hidden_one_grad = jnp.einsum(
        "te,de->td", packed_grad, projector_all, preferred_element_type=full
    )
    inputs_grad = middle_grad + normalize_back(
        normed_one, inverse_one, hidden_one_grad * (1.0 + scale_attn)
    )
    token_mod_grad = jnp.concatenate(
        [
            hidden_one_grad,
            hidden_one_grad * normed_one,
            gate_attn_grad,
            hidden_two_grad,
            hidden_two_grad * normed_two,
            gate_mlp_grad,
        ],
        axis=1,
    )
    modulation_grad = jnp.stack(
        [jnp.sum(jnp.where(local == slot, token_mod_grad, 0.0), axis=0) for slot in range(images)]
    ).astype(low)
    modulation_grad_both = lax.all_gather(modulation_grad, ("stream", "dp"), axis=0, tiled=True)
    modulator_grad = jnp.einsum(
        "id,ie->de", activated_own, modulation_grad_both, preferred_element_type=full
    )
    bias_width = modulator_bias.shape[0]
    modulator_bias_grad = jnp.sum(
        lax.dynamic_slice(
            modulation_grad_both, (0, dp_index * bias_width), (slots, bias_width)
        ).astype(full),
        axis=0,
    )
    activated_part = jnp.einsum(
        "ie,de->id",
        lax.dynamic_slice(
            modulation_grad_both, (stream_index * stream_slots, 0), (stream_slots, 6 * model_width)
        ),
        modulator,
        preferred_element_type=full,
    )
    activated_grad = (
        lax.all_to_all(
            activated_part.reshape(-1, images, shard), "dp", split_axis=0, concat_axis=0, tiled=True
        )
        .transpose(1, 0, 2)
        .reshape(images, model_width)
    )
    condition_grad = silu_back(activated_grad)[0]
    return (
        result[None],
        inputs_grad[None],
        condition_grad[None],
        modulator_grad,
        modulator_bias_grad,
        projector_grad,
        bias_grads[0],
        table_total,
        output_grad,
        bias_grads[1],
        up_grad,
        bias_grads[2],
        down_grad,
        bias_grads[3],
    )


def solution(mesh):
    in_specs = (
        P("stream", "dp", None),
        P("stream", "dp", None),
        P("stream", "dp"),
        P("stream", "dp"),
        P(),
        P("dp", None),
        P("dp"),
        P("dp", None),
        P("dp"),
        P(),
        P("dp", None),
        P("dp"),
        P("dp", None),
        P("dp"),
        P("dp", None),
        P("dp"),
        P("stream", "dp", None),
    )
    out_specs = (
        P("stream", "dp", None),
        P("stream", "dp", None),
        P("stream", "dp", None),
        P("dp", None),
        P("dp"),
        P("dp", None),
        P("dp"),
        P(),
        P("dp", None),
        P("dp"),
        P("dp", None),
        P("dp"),
        P("dp", None),
        P("dp"),
    )
    return jax.shard_map(shards, mesh=mesh, in_specs=in_specs, out_specs=out_specs, check_vma=False)
```

```python
import functools

import jax
import jax.numpy as jnp
from jax import lax
from jax.experimental import pallas as pl
from jax.experimental.pallas import tpu as pltpu
from jax.sharding import PartitionSpec as P

norm_epsilon = 1e-06
masked_score=-1000000000.0

def grid_kernel(table_ref, buckets_ref, grid_ref):
    chunks = table_ref.shape[1]
    for half in range(buckets_ref.shape[1] // 128):
        span = slice(128 * half, 128 * half + 128)
        index = buckets_ref[:, span]
        low, high = index & 127, index >> 7
        total = jnp.zeros(index.shape, jnp.float32)
        for chunk in range(chunks):
            row = jnp.broadcast_to(table_ref[0, chunk : chunk + 1], index.shape)
            found = jnp.take_along_axis(row, low, axis=1)
            total = jnp.where(high == chunk, found, total)
        grid_ref[0, :, span] = total.astype(jnp.bfloat16)

def bias_grid(table, buckets):
    heads, count = table.shape
    chunks = -(-count // 128)
    wide = jnp.pad(table.astype(jnp.float32), ((0, 0), (0, chunks * 128 - count)))
    return pl.pallas_call(
        grid_kernel,
        grid=(heads,),
        in_specs=[pl.BlockSpec((1, chunks, 128), lambda h: (h, 0, 0)),
                  pl.BlockSpec(buckets.shape, lambda h: (0, 0))],
        out_specs=pl.BlockSpec((1,) + buckets.shape, lambda h: (h, 0, 0)),
        out_shape=jax.ShapeDtypeStruct((heads,) + buckets.shape, jnp.bfloat16),
    )(wide.reshape(heads, chunks, 128), buckets)

def hist_kernel(grad_ref, buckets_ref, out_ref):
    rows, heads, width = grad_ref.shape
    chunks = out_ref.shape[0] // heads
    @pl.when(pl.program_id(0) == 0)
    def _():
        out_ref[...] = jnp.zeros_like(out_ref)
    total = out_ref[...]
    for row in range(rows):
        index = buckets_ref[row : row + 1, :]
        low, high = index & 127, index >> 7
        mask = lax.broadcasted_iota(jnp.int32, (chunks, width), 0) == high
        values = jnp.where(mask[None], grad_ref[row][:, None, :], 0.0)
        left = values.reshape(heads * chunks, width).astype(jnp.bfloat16)
        right = (lax.broadcasted_iota(jnp.int32, (128, width), 0) == low).astype(jnp.float32).astype(jnp.bfloat16)
        total += lax.dot_general(left, right, (((1,), (1,)), ((), ())), preferred_element_type=jnp.float32)
    out_ref[...] = total

def table_histogram(grad, buckets, count):
    places, heads, width = grad.shape
    chunks = -(-count // 128)
    step = 16
    out = pl.pallas_call(
        hist_kernel,
        grid=(places // step,),
        in_specs=[pl.BlockSpec((step, heads, width), lambda a: (a, 0, 0)),
                  pl.BlockSpec((step, width), lambda a: (a, 0))],
        out_specs=pl.BlockSpec((heads * chunks, 128), lambda a: (0, 0)),
        out_shape=jax.ShapeDtypeStruct((heads * chunks, 128), jnp.float32),
    )(grad, buckets)
    return out.reshape(heads, chunks * 128)[:, :count]

def head_windows(heads, head_width):
    found = []
    for head in range(heads):
        start = head * head_width
        base = start // 128 * 128
        stop = -(-(start + head_width) // 128) * 128
        found.append((base, stop - base, start - base))
    return found

def lane_mask(rows, width, offset, head_width):
    lane = lax.broadcasted_iota(jnp.int32, (rows, width), 1)
    return (lane >= offset) & (lane < offset + head_width)

def nt(left, right):
    return lax.dot_general(left, right, (((1,), (1,)), ((), ())), preferred_element_type=jnp.float32)
def tn(left, right):
    return lax.dot_general(left, right, (((0,), (0,)), ((), ())), preferred_element_type=jnp.float32)
def nn(left, right):
    return lax.dot_general(left, right, (((1,), (0,)), ((), ())), preferred_element_type=jnp.float32)

def attend_forward_kernel(heads, packed_ref, frame_row_ref, frame_column_ref, grid_ref, attended_ref, placed_ref, weights_ref, mixed_ref):
    rows, width3 = packed_ref.shape
    frames = placed_ref.shape[0]
    places = grid_ref.shape[1]
    width = width3 // 3
    head_width = width // heads
    scale = head_width ** (-0.5)
    place = (lax.broadcasted_iota(jnp.int32, (frames, rows), 0) == frame_row_ref[...]).astype(jnp.float32).astype(jnp.bfloat16)
    for part in range(3):
        span = slice(part * width, part * width + width)
        placed_ref[:, span] = nn(place, packed_ref[:, span]).astype(jnp.bfloat16)
    filled = nt(jnp.ones((8, rows), jnp.bfloat16), place)[0:1] > 0.5
    filled_f = jnp.where(filled, 0.0, masked_score)
    mixed_ref[...] = jnp.zeros_like(mixed_ref)
    for image in range(frames // places):
        span_rows = slice(image * places, image * places + places)
        offset_row = filled_f[:, span_rows]
        for head, (base, wide, offset) in enumerate(head_windows(heads, head_width)):
            mask = lane_mask(places, wide, offset, head_width)
            query = placed_ref[span_rows, base : base + wide]
            key = placed_ref[span_rows, width + base : width + base + wide]
            value = placed_ref[span_rows, 2 * width + base : 2 * width + base + wide]
            query = jnp.where(mask, query, jnp.zeros_like(query))
            scores = nt(query, key) * scale + grid_ref[head].astype(jnp.float32)
            scores = jnp.where(offset_row < 0.0, masked_score, scores)
            exponent = jnp.exp(scores - jnp.max(scores, axis=-1, keepdims=True))
            weights = (exponent / jnp.sum(exponent, axis=-1, keepdims=True)).astype(jnp.bfloat16)
            weights_ref[image, head] = weights
            mixture = nn(weights, value).astype(jnp.bfloat16)
            before = mixed_ref[span_rows, base : base + wide]
            mixed_ref[span_rows, base : base + wide] = jnp.where(mask, mixture, before)
    back = (lax.broadcasted_iota(jnp.int32, (rows, frames), 1) == frame_column_ref[...]).astype(jnp.float32).astype(jnp.bfloat16)
    attended_ref[...] = nn(back, mixed_ref[...]).astype(jnp.bfloat16)

def attend_forward(packed, slots, places, grid):
    rows = packed.shape[0]
    heads, image, _ = grid.shape
    frame = slots * image + places
    frames = 3 * image
    width = packed.shape[1] // 3
    return pl.pallas_call(
        functools.partial(attend_forward_kernel, heads),
        out_shape=(jax.ShapeDtypeStruct((rows, width), jnp.bfloat16),
                   jax.ShapeDtypeStruct((frames, 3 * width), jnp.bfloat16),
                   jax.ShapeDtypeStruct((3, heads, image, image), jnp.bfloat16)),
        scratch_shapes=[pltpu.VMEM((frames, width), jnp.bfloat16)],
        compiler_params=pltpu.CompilerParams(vmem_limit_bytes=48 * 2**20),
    )(packed, frame[None, :], frame[:, None], grid)

def attend_backward_kernel(heads, placed_ref, weights_ref, upstream_ref, frame_row_ref, frame_column_ref, packed_grad_ref, grid_grad_ref, up_ref, grad_ref, bias_ref):
    frames, width3 = placed_ref.shape
    rows = upstream_ref.shape[0]
    places = weights_ref.shape[2]
    width = width3 // 3
    head_width = width // heads
    scale = head_width ** (-0.5)
    place = (lax.broadcasted_iota(jnp.int32, (frames, rows), 0) == frame_row_ref[...]).astype(jnp.float32).astype(jnp.bfloat16)
    up_ref[...] = nn(place, upstream_ref[...]).astype(jnp.bfloat16)
    grad_ref[...] = jnp.zeros_like(grad_ref)
    for head, (base, wide, offset) in enumerate(head_windows(heads, head_width)):
        mask = lane_mask(places, wide, offset, head_width)
        for image in range(frames // places):
            span_rows = slice(image * places, image * places + places)
            spans = [slice(part * width + base, part * width + base + wide) for part in range(3)]
            query, key = [jnp.where(mask, t, jnp.zeros_like(t)) for t in (placed_ref[span_rows, spans[0]], placed_ref[span_rows, spans[1]])]
            value = placed_ref[span_rows, spans[2]]
            upstream = up_ref[span_rows, spans[0]]
            upstream = jnp.where(mask, upstream, jnp.zeros_like(upstream))
            weights = weights_ref[image, head]
            weights_f = weights.astype(jnp.float32)
            weight_grads = nt(upstream, value)
            inner = jnp.sum(weight_grads * weights_f, axis=-1, keepdims=True)
            score_grads_f = weights_f * (weight_grads - inner)
            score_grads = score_grads_f.astype(jnp.bfloat16)
            if image == 0:
                bias_ref[...] = score_grads_f
            else:
                bias_ref[...] += score_grads_f
            grad_ref[span_rows, spans[0]] += (nn(score_grads, key) * scale).astype(jnp.bfloat16)
            grad_ref[span_rows, spans[1]] += (tn(score_grads, query) * scale).astype(jnp.bfloat16)
            grad_ref[span_rows, spans[2]] += tn(weights, upstream).astype(jnp.bfloat16)
        grid_grad_ref[:, head, :] = bias_ref[...]
    back = (lax.broadcasted_iota(jnp.int32, (rows, frames), 1) == frame_column_ref[...]).astype(jnp.float32).astype(jnp.bfloat16)
    for part in range(3):
        span = slice(part * width, part * width + width)
        packed_grad_ref[:, span] = nn(back, grad_ref[:, span]).astype(jnp.bfloat16)

def attend_backward(placed, weights, upstream, slots, places):
    rows, width = upstream.shape
    _, heads, image, _ = weights.shape
    frame = slots * image + places
    frames = 3 * image
    return pl.pallas_call(
        functools.partial(attend_backward_kernel, heads),
        out_shape=(jax.ShapeDtypeStruct((rows, 3 * width), jnp.bfloat16),
                   jax.ShapeDtypeStruct((image, heads, image), jnp.float32)),
        scratch_shapes=[pltpu.VMEM((frames, width), jnp.bfloat16),
                        pltpu.VMEM((frames, 3 * width), jnp.bfloat16),
                        pltpu.VMEM((image, image), jnp.float32)],
        compiler_params=pltpu.CompilerParams(vmem_limit_bytes=56 * 2**20),
    )(placed, weights, upstream, frame[None, :], frame[:, None])

def normalize(values):
    center = values - jnp.mean(values, axis=-1, keepdims=True)
    inverse = lax.rsqrt(jnp.mean(center * center, axis=-1, keepdims=True) + norm_epsilon)
    return (center * inverse, inverse)


def normalize_back(normed, inverse, upstream):
    return inverse * (
        upstream
        - jnp.mean(upstream, axis=-1, keepdims=True)
        - normed * jnp.mean(upstream * normed, axis=-1, keepdims=True)
    )


def smooth_gelu(values):
    return jax.nn.gelu(values, approximate=True)


MESH = pl.DeviceIdType.MESH
low = jnp.bfloat16
full = jnp.float32


class Place:
    def __init__(self):
        self.x = lax.axis_index("stream")
        self.d = lax.axis_index("dp")
        self.z = self.d // 4
        self.y = (self.d // 2) % 2
        self.c = self.d % 2
    def zz(self, j):
        return (self.z, self.z + 1 - 2 * (self.z % 2), self.z + 2 - 4 * (self.z // 2), 3 - self.z)[j]
    def chip(self, j=0, yy=0):
        return self.zz(j) * 2 + (self.y if yy == 0 else 1 - self.y)
    def at(self, x=0, y=0, j=0, core=0):
        xx = self.x if x == 0 else 1 - self.x
        cc = self.c if core == 0 else 1 - self.c
        return (xx, self.chip(j, y) * 2 + cc)

def gather_region(place, full_ref, w, chip, part):
    c, x = place.c, place.x
    if w < 2:
        off, size = {"all": (0, 2304), "ad": (1024 * x, 1280), "a": (1280 * x, 1024)}[part]
        col = pl.multiple_of(4608 * w + 2304 * c + off, 128)
        return full_ref[0].at[pl.ds(pl.multiple_of(chip * 144, 16), 144), pl.ds(col, size)]
    off, size = {"all": (0, 288), "ad": (128 * x, 160), "a": (160 * x, 128)}[part]
    row = pl.multiple_of(c * 2304 + chip * 288 + off, 16)
    return full_ref[1].at[pl.ds(row, size), :]

class Gather:
    def __init__(self, place, full_ref, send, recv):
        self.place, self.full, self.send, self.recv = place, full_ref, send, recv
    def copy(self, w, slot, region_src, device):
        return pltpu.make_async_remote_copy(src_ref=region_src, dst_ref=region_src, send_sem=self.send.at[w, slot],
            recv_sem=self.recv.at[w, slot], device_id=device, device_id_type=MESH)
    def region(self, w, chip, part):
        return gather_region(self.place, self.full, w, chip, part)
    def desc(self, w, kind, j=0, yy=0, recv=False):
        p = self.place
        if kind == "z":
            return self.copy(w, j - 1, self.region(w, p.chip(j if recv else 0), "ad"), p.at(j=j))
        if kind == "y":
            part = "all" if j == 0 else "ad"
            return self.copy(w, 3 + j, self.region(w, p.chip(j, 1 if recv else 0), part), p.at(y=1))
        if kind == "x":
            if recv:
                return self.copy(w, 7 + 2 * (j - 1) + yy, self.other_a(w, p.chip(j, yy)), p.at(x=1))
            return self.copy(w, 7 + 2 * (j - 1) + yy, self.region(w, p.chip(j, yy), "a"), p.at(x=1))
        if kind == "s":
            slot = 13 + 2 * j + yy - 1
            if recv:
                return self.copy(w, slot, self.other_half(w, p.chip(j, yy)), p.at(core=1))
            return self.copy(w, slot, self.region(w, p.chip(j, yy), "all"), p.at(core=1))
    def other_a(self, w, chip):
        q = type("Q", (), {})(); q.c, q.x = self.place.c, 1 - self.place.x
        return gather_region(q, self.full, w, chip, "a")
    def other_half(self, w, chip):
        q = type("Q", (), {})(); q.c, q.x = 1 - self.place.c, self.place.x
        return gather_region(q, self.full, w, chip, "all")
    def start(self, w):
        for j in (1, 2, 3):
            self.desc(w, "z", j).start()
        self.desc(w, "y", 0).start()
    def on_z(self, w, j):
        self.desc(w, "z", j, recv=True).wait_recv()
        self.desc(w, "x", j, 0).start()
        self.desc(w, "y", j).start()
    def on_y(self, w, j):
        self.desc(w, "y", j, recv=True).wait_recv()
        if j == 0:
            self.desc(w, "s", 0, 1).start()
        else:
            self.desc(w, "x", j, 1).start()
    def on_x(self, w, j, yy):
        self.desc(w, "x", j, yy, recv=True).wait_recv()
        self.desc(w, "s", j, yy).start()
    def on_s(self, w, j, yy):
        self.desc(w, "s", j, yy, recv=True).wait_recv()
    def finish(self, w):
        for j in (1, 2, 3):
            self.desc(w, "z", j).wait_send()
            self.desc(w, "y", j).wait_send()
            for yy in (0, 1):
                self.desc(w, "x", j, yy).wait_send()
                self.desc(w, "s", j, yy).wait_send()
        self.desc(w, "y", 0).wait_send()
        self.desc(w, "s", 0, 1).wait_send()

def gather_kernel(note_ref, mod_ref, shard_ref, down_ref, full12_ref, full3_ref, inbox_ref, modulation_ref,
                  sib, chip, msend, mrecv, csem, csend, crecv, send, recv, part, got0, got1, psend, precv):
    place = Place()
    x, d, c = place.x, place.d, place.c
    barrier = pltpu.get_barrier_semaphore()
    def peer(t, k):
        return (x if t == 0 else 1 - x, (d + k) % 16)
    for t in (0, 1):
        for k in range(16):
            if (t, k) != (0, 0):
                pl.semaphore_signal(barrier, inc=1, device_id=peer(t, k), device_id_type=MESH)
    pl.semaphore_wait(barrier, 31)
    sib_copy = pltpu.make_async_remote_copy(src_ref=shard_ref, dst_ref=sib, send_sem=csend.at[0], recv_sem=crecv.at[0],
        device_id=place.at(core=1), device_id_type=MESH)
    sib_copy.start()
    mine = full3_ref.at[pl.ds(pl.multiple_of(c * 2304 + place.chip() * 288, 16), 288), :]
    own3 = pltpu.make_async_copy(down_ref, mine, csem.at[0])
    own3.start()
    theirs = full3_ref.at[pl.ds(pl.multiple_of((1 - c) * 2304 + place.chip() * 288, 16), 288), :]
    def note(t, k, recv=False):
        if recv:
            src = (x if t == 0 else 1 - x) * 16 + (d + 16 - k) % 16
        else:
            src = x * 16 + d
        return pltpu.make_async_remote_copy(src_ref=note_ref.at[(d + k) % 16], dst_ref=inbox_ref.at[src],
            send_sem=msend.at[t, k], recv_sem=mrecv.at[t, k], device_id=peer(t, k), device_id_type=MESH)
    for t in (0, 1):
        for k in range(16):
            if (t, k) != (0, 0):
                note(t, k).start()
    inbox_ref[x * 16 + d] = note_ref[d]
    down_copy = pltpu.make_async_remote_copy(src_ref=down_ref, dst_ref=mine, send_sem=csend.at[1], recv_sem=crecv.at[1],
        device_id=place.at(core=1), device_id_type=MESH)
    down_copy.start()
    sib_copy.wait()
    columns = 512
    def assemble(i, _):
        span = pl.ds(pl.multiple_of(i * columns, columns), columns)
        own, other = shard_ref[0:72, span].astype(jnp.float32), sib[0:72, span].astype(jnp.float32)
        top = jnp.where(c == 0, own, other)
        bottom = jnp.where(c == 0, other, own)
        chip[:, span] = jnp.concatenate([top, bottom], axis=0).astype(jnp.bfloat16)
        return 0
    lax.fori_loop(0, shard_ref.shape[1] // columns, assemble, 0)
    own12 = pltpu.make_async_copy(chip, full12_ref.at[pl.ds(pl.multiple_of(place.chip() * 144, 16), 144), :], csem.at[1])
    own12.start()
    own12.wait()
    own3.wait()
    g = Gather(place, (full12_ref, full3_ref), send, recv)
    g.start(0)
    for t in (0, 1):
        for k in range(16):
            if (t, k) != (0, 0):
                note(t, k, recv=True).wait_recv()
    lhs = inbox_ref[pl.ds(x * 16, 16), 0:8, :].reshape(128, 128).astype(jnp.bfloat16)
    cols = 768
    def project(i, _):
        span = pl.ds(pl.multiple_of(i * cols, cols), cols)
        out = jnp.dot(lhs, mod_ref[:, span], preferred_element_type=jnp.float32)
        for chip_at in range(8):
            for core in range(2):
                dest = (chip_at * 2 + core) * 8
                part[core, chip_at, :, span] = out[dest : dest + 4]
        return 0
    lax.fori_loop(0, mod_ref.shape[1] // cols, project, 0)
    half = pltpu.make_async_remote_copy(src_ref=part.at[1 - c], dst_ref=got0, send_sem=psend.at[0], recv_sem=precv.at[0],
        device_id=place.at(core=1), device_id_type=MESH)
    half.start()
    half.wait()
    for chip_at in range(8):
        part[c, chip_at] += got0[chip_at]
    def share(k):
        dest = (place.chip() + k) % 8
        return pltpu.make_async_remote_copy(src_ref=part.at[c, dest], dst_ref=got1.at[k - 1], send_sem=psend.at[k], recv_sem=precv.at[k],
            device_id=(x, dest * 2 + c), device_id_type=MESH)
    for k in range(1, 8):
        share(k).start()
    for j in (1, 2, 3):
        g.on_z(0, j)
    g.start(1)
    for k in range(1, 8):
        share(k).wait_recv()
    total = part[c, place.chip()]
    for k in range(1, 8):
        total += got1[k - 1]
    modulation_ref[...] = total
    g.on_y(0, 0)
    for j in (1, 2, 3):
        g.on_y(0, j)
    for j in (1, 2, 3):
        g.on_z(1, j)
    for j in (1, 2, 3):
        g.on_x(0, j, 0)
    down_copy.wait()
    g.start(2)
    for j in (1, 2, 3):
        g.on_x(0, j, 1)
    g.on_y(1, 0)
    for j in (1, 2, 3):
        g.on_y(1, j)
    for j in (1, 2, 3):
        g.on_z(2, j)
    for yy in (0, 1):
        for j in (1, 2, 3):
            g.on_x(1, j, yy)
    g.on_y(2, 0)
    for j in (1, 2, 3):
        g.on_y(2, j)
    for yy in (0, 1):
        for j in (1, 2, 3):
            g.on_x(2, j, yy)
    for w in range(3):
        for j in range(4):
            for yy in (0, 1):
                if (j, yy) != (0, 0):
                    g.on_s(w, j, yy)
        g.finish(w)
    for t in (0, 1):
        for k in range(16):
            if (t, k) != (0, 0):
                note(t, k).wait_send()
    for k in range(1, 8):
        share(k).wait_send()

def gather_weights(notes, modulator, shard12, down):
    any_, vm = pl.BlockSpec(memory_space=pl.ANY), pl.BlockSpec(memory_space=pltpu.VMEM)
    width = modulator.shape[1]
    return pl.pallas_call(
        gather_kernel,
        out_shape=(jax.ShapeDtypeStruct((1152, 9216), low), jax.ShapeDtypeStruct((4608, 1152), low),
                   jax.ShapeDtypeStruct((32, 16, 128), full), jax.ShapeDtypeStruct((4, width), full)),
        in_specs=[vm, vm, vm, any_],
        out_specs=(any_, any_, vm, vm),
        scratch_shapes=[
            pltpu.VMEM(shard12.shape, low), pltpu.VMEM((144, shard12.shape[1]), low),
            pltpu.SemaphoreType.DMA((2, 16)), pltpu.SemaphoreType.DMA((2, 16)),
            pltpu.SemaphoreType.DMA((2,)), pltpu.SemaphoreType.DMA((2,)), pltpu.SemaphoreType.DMA((2,)),
            pltpu.SemaphoreType.DMA((3, 20)), pltpu.SemaphoreType.DMA((3, 20)),
            pltpu.VMEM((2, 8, 4, width), full), pltpu.VMEM((8, 4, width), full), pltpu.VMEM((7, 4, width), full),
            pltpu.SemaphoreType.DMA((8,)), pltpu.SemaphoreType.DMA((8,)),
        ],
        compiler_params=pltpu.CompilerParams(collective_id=0, has_side_effects=True, vmem_limit_bytes=40 * 2**20),
    )(notes, modulator, shard12, down)

def feed_order(values, axis, chips):
    shape = values.shape
    part = shape[axis] // (2 * chips)
    split = shape[:axis] + (chips, 2, part) + shape[axis + 1 :]
    return jnp.swapaxes(values.reshape(split), axis, axis + 1).reshape(shape)
def feed_restore(values, axis, chips):
    shape = values.shape
    part = shape[axis] // (2 * chips)
    split = shape[:axis] + (2, chips, part) + shape[axis + 1 :]
    return jnp.swapaxes(values.reshape(split), axis, axis + 1).reshape(shape)


def rs_part(place, w, part):
    x = place.x
    unit = 768 if w < 2 else 96
    off, size = {"all": (0, 3), "ad": (x, 2), "a": (2 * x, 1), "o": (2 - 2 * x, 1), "od": (1 - x, 2)}[part]
    return pl.multiple_of(unit * off, 128 if w < 2 else 16), unit * size

class Scatter:
    def __init__(self, place, acc12, acc3, rx, ry, rz, rf, send, recv):
        self.p, self.acc12, self.acc3, self.rx, self.ry, self.rz, self.rf, self.send, self.recv = place, acc12, acc3, rx, ry, rz, rf, send, recv
    def acc(self, w, chip, part):
        off, size = rs_part(self.p, w, part)
        if w < 2:
            return self.acc12.at[chip, :, pl.ds(2304 * w + off, size)]
        return self.acc3.at[chip, pl.ds(off, size), :]
    def land(self, w, kind, i, size=None):
        b = {"x": self.rx, "y": self.ry, "z": self.rz, "f": self.rf, "Y": self.rf}[kind]
        if kind == "f":
            return self.rf[w].at[0]
        if kind == "Y":
            return self.rf[w].at[1]
        return b[w].at[i]
    def copy(self, w, slot, src, dst, device):
        return pltpu.make_async_remote_copy(src_ref=src, dst_ref=dst, send_sem=self.send.at[w, slot], recv_sem=self.recv.at[w, slot], device_id=device, device_id_type=MESH)
    def x(self, w, j, yy):
        return self.copy(w, 2 * (j - 1) + yy, self.acc(w, self.p.chip(j, yy), "o"), self.land(w, "x", 2 * (j - 1) + yy), self.p.at(x=1))
    def y(self, w, j):
        return self.copy(w, 5 + j, self.acc(w, self.p.chip(j, 1), "ad"), self.land(w, "y", j - 1), self.p.at(y=1))
    def Y(self, w):
        return self.copy(w, 9, self.acc(w, self.p.chip(0, 1), "all"), self.land(w, "Y", 0), self.p.at(y=1))
    def z(self, w, j):
        return self.copy(w, 9 + j, self.acc(w, self.p.chip(j, 0), "ad"), self.land(w, "z", j - 1), self.p.at(j=j))
    def f(self, w):
        return self.copy(w, 13, self.acc(w, self.p.chip(0, 0), "all"), self.land(w, "f", 0), self.p.at(x=1))
    def add(self, w, chip, part, land):
        dst = self.acc(w, chip, part)
        rows = dst.shape[0]
        step = 48
        def body(i, _):
            span = pl.ds(pl.multiple_of(i * step, 16), step)
            dst[span, :] = dst[span, :] + land[span, :]
            return 0
        lax.fori_loop(0, rows // step, body, 0)
    def ready(self, w, j, yy):
        if j > 0:
            self.x(w, j, yy).start()
        elif yy == 1:
            self.Y(w).start()
    def on_x(self, w, j, yy):
        self.x(w, j, yy).wait_recv()
        self.add(w, self.p.chip(j, yy), "a", self.land(w, "x", 2 * (j - 1) + yy))
        if yy == 1:
            self.y(w, j).start()
    def on_y(self, w, j):
        self.y(w, j).wait_recv()
        self.add(w, self.p.chip(j, 0), "ad", self.land(w, "y", j - 1))
        self.z(w, j).start()
    def on_Y(self, w):
        self.Y(w).wait_recv()
        self.add(w, self.p.chip(0, 0), "all", self.land(w, "Y", 0))
    def on_z(self, w, j):
        self.z(w, j).wait_recv()
        self.add(w, self.p.chip(0, 0), "ad", self.land(w, "z", j - 1))
    def last(self, w):
        self.f(w).start()
    def finish(self, w):
        for j in (1, 2, 3):
            for yy in (0, 1):
                self.x(w, j, yy).wait_send()
            self.y(w, j).wait_send()
            self.z(w, j).wait_send()
        self.Y(w).wait_send()

def rs_shapes():
    V, D = pltpu.VMEM, pltpu.SemaphoreType.DMA
    a = [V((8, 144, 4608), low), V((8, 288, 1152), low)]
    rx = [V((6, 144, 768), low), V((6, 144, 768), low), V((6, 96, 1152), low)]
    ry = [V((3, 144, 1536), low), V((3, 144, 1536), low), V((3, 192, 1152), low)]
    rz = [V((3, 144, 1536), low), V((3, 144, 1536), low), V((3, 192, 1152), low)]
    rf = [V((2, 144, 2304), low), V((2, 144, 2304), low), V((2, 288, 1152), low)]
    return a, rx, ry, rz, rf

def scatter_kernel(sizes, mg_ref, vec_ref, inbox_ref, mod_ref, g12_ref, g3_ref,
                   out12_ref, out3_ref, vec_out_ref, gmod_ref, gmodsum_ref, cond_ref, *rest):
    it = iter(rest)
    take = lambda n: [next(it) for _ in range(n)]
    acc12, acc3 = take(2)
    rx, ry, rz, rf = take(3), take(3), take(3), take(3)
    own12, own3, fin, sibfin = take(4)
    vbuf, vsum, mgall, cpart = take(4)
    send, recv, ssend, srecv, lsem, vsend, vrecv, msend, mrecv, csend, crecv, fsend, frecv = take(13)
    place = Place()
    x, d, c, z = place.x, place.d, place.c, place.z
    barrier = pltpu.get_barrier_semaphore()
    for k in range(1, 16):
        pl.semaphore_signal(barrier, inc=1, device_id=(x, (d + k) % 16), device_id_type=MESH)
    pl.semaphore_signal(barrier, inc=1, device_id=place.at(x=1), device_id_type=MESH)
    pl.semaphore_wait(barrier, 16)
    s = Scatter(place, acc12, acc3, rx, ry, rz, rf, send, recv)
    order = [(1, 1), (1, 0), (2, 1), (2, 0), (3, 1), (3, 0), (0, 1), (0, 0)]
    def sib(w, n, recv_side=False):
        j, yy = order[n]
        chip = place.chip(j, yy)
        cc = 1 - c
        if w < 2:
            src = g12_ref.at[pl.ds(pl.multiple_of(chip * 144, 16), 144), pl.ds(pl.multiple_of(4608 * w + 2304 * cc, 128), 2304)]
            dst = acc12.at[chip, :, pl.ds(2304 * w, 2304)]
        else:
            src = g3_ref.at[pl.ds(pl.multiple_of(cc * 2304 + chip * 288, 16), 288), :]
            dst = acc3.at[chip]
        return pltpu.make_async_remote_copy(src_ref=src, dst_ref=dst, send_sem=ssend.at[w, n], recv_sem=srecv.at[w, n], device_id=place.at(core=1), device_id_type=MESH)
    def own(w, n):
        j, yy = order[n]
        chip = place.chip(j, yy)
        if w < 2:
            src = g12_ref.at[pl.ds(pl.multiple_of(chip * 144, 16), 144), pl.ds(pl.multiple_of(4608 * w + 2304 * c, 128), 2304)]
            dst = own12.at[n % 2]
        else:
            src = g3_ref.at[pl.ds(pl.multiple_of(c * 2304 + chip * 288, 16), 288), :]
            dst = own3.at[n % 2]
        return pltpu.make_async_copy(src, dst, lsem.at[w, n])
    def stage0(w):
        for n in range(8):
            sib(w, n).start()
        own(w, 0).start()
        for n in range(8):
            if n < 7:
                own(w, n + 1).start()
            own(w, n).wait()
            sib(w, n).wait_recv()
            j, yy = order[n]
            s.add(w, place.chip(j, yy), "all", (own12 if w < 2 else own3).at[n % 2])
            s.ready(w, j, yy)
    def mids(w):
        for j in (1, 2, 3):
            s.on_x(w, j, 1)
            s.on_x(w, j, 0)
    def ys(w):
        for j in (1, 2, 3):
            s.on_y(w, j)
        s.on_Y(w)
    def zs(w):
        for j in (1, 2, 3):
            s.on_z(w, j)
        s.last(w)
    def vcopy(n):
        if n < 3:
            dev = (place.at(core=1), place.at(x=1), place.at(y=1))[n]
            return pltpu.make_async_remote_copy(src_ref=vsum, dst_ref=vbuf.at[n], send_sem=vsend.at[n], recv_sem=vrecv.at[n], device_id=dev, device_id_type=MESH)
        j = n - 2
        return pltpu.make_async_remote_copy(src_ref=vsum, dst_ref=vbuf.at[3 + z], send_sem=vsend.at[n], recv_sem=vrecv.at[n], device_id=place.at(j=j), device_id_type=MESH)
    def vrecv_wait(j):
        pltpu.make_async_remote_copy(src_ref=vsum, dst_ref=vbuf.at[3 + place.zz(j)], send_sem=vsend.at[2 + j], recv_sem=vrecv.at[2 + j], device_id=place.at(j=j), device_id_type=MESH).wait_recv()
    def mrow(xx, chip, cc):
        return (x if xx == 0 else 1 - x) * 16 + chip * 2 + (c if cc == 0 else 1 - c)
    def mcopy(slot, row, dev):
        return pltpu.make_async_remote_copy(src_ref=mgall.at[row], dst_ref=mgall.at[row], send_sem=msend.at[slot], recv_sem=mrecv.at[slot], device_id=dev, device_id_type=MESH)
    def mz(j, r=False):
        return mcopy(j, mrow(0, place.chip(j if r else 0), 0), place.at(j=j))
    def my(j, r=False):
        return mcopy(4 + j, mrow(0, place.chip(j, 1 if r else 0), 0), place.at(y=1))
    def mx(j, yy, r=False):
        return mcopy(8 + 2 * j + yy, mrow(1 if r else 0, place.chip(j, yy), 0), place.at(x=1))
    def ms(xx, j, yy, r=False):
        return mcopy(16 + xx * 8 + 2 * j + yy, mrow(xx, place.chip(j, yy), 1 if r else 0), place.at(core=1))
    stage0(2)
    vsum[...] = vec_ref[...]
    mgall[x * 16 + d] = mg_ref[...]
    vcopy(0).start()
    for j in (1, 2, 3):
        mz(j).start()
    my(0).start()
    mx(0, 0).start()
    ms(0, 0, 0).start()
    vcopy(0).wait()
    vsum[...] += vbuf[0]
    vcopy(1).start()
    for j in (1, 2, 3):
        mz(j, True).wait_recv()
        my(j).start()
        mx(j, 0).start()
        ms(0, j, 0).start()
    mids(2)
    vcopy(1).wait()
    vsum[...] += vbuf[1]
    vcopy(2).start()
    for j in (0, 1, 2, 3):
        my(j, True).wait_recv()
        mx(j, 1).start()
        ms(0, j, 1).start()
    stage0(1)
    ys(2)
    vcopy(2).wait()
    vsum[...] += vbuf[2]
    for j in (1, 2, 3):
        vcopy(2 + j).start()
    vbuf[3 + z] = vsum[...]
    for yy in (0, 1):
        for j in range(4):
            mx(j, yy, True).wait_recv()
            ms(1, j, yy).start()
    mids(1)
    zs(2)
    stage0(0)
    ys(1)
    mids(0)
    zs(1)
    for j in (1, 2, 3):
        vrecv_wait(j)
    vec_out_ref[...] = vbuf[3] + vbuf[4] + vbuf[5] + vbuf[6]
    for xx in (0, 1):
        for yy in (0, 1):
            for j in range(4):
                ms(xx, j, yy, True).wait_recv()
    def place_rows(p, devices):
        base = 3 * (p - 2) if p >= 2 else 3 * p
        shape = (devices * 16, devices * 8)
        r, q = lax.broadcasted_iota(jnp.int32, shape, 0), lax.broadcasted_iota(jnp.int32, shape, 1)
        return ((r // 16 == q // 8) & (r % 16 - base == q % 8) & (q % 8 < 3)).astype(full).astype(low)
    act = inbox_ref[:, 0:8, :].reshape(256, 128).astype(low)
    cond_total = jnp.zeros((128, 128), full)
    for p in range(6):
        tile = 0 if p >= 2 else 1
        span = slice(1152 * p, 1152 * p + 1152)
        pieces = mgall[:, 16 * tile : 16 * tile + 16, :].reshape(512, 1152)
        where = place_rows(p, 32)
        left = jnp.dot(where, act, preferred_element_type=full).astype(low)
        grad = lax.dot_general(left, pieces, (((0,), (0,)), ((), ())), preferred_element_type=full)
        gmod_ref[:, span] = grad[0:72]
        ones = jnp.broadcast_to((jnp.sum(where.astype(full), axis=1, keepdims=True)).astype(low), (512, 128))
        gmodsum_ref[:, span] = lax.dot_general(ones, pieces, (((0,), (0,)), ((), ())), preferred_element_type=full)[0:8]
        mine = mgall[pl.ds(x * 16, 16), 16 * tile : 16 * tile + 16, :].reshape(256, 1152)
        rows = lax.dot_general(place_rows(p, 16), mine, (((0,), (0,)), ((), ())), preferred_element_type=full).astype(low)
        cond_total += lax.dot_general(rows, mod_ref[:, span], (((1,), (1,)), ((), ())), preferred_element_type=full)
    cpart[...] = cond_total.reshape(16, 8, 128)
    def ccopy(k, r=False):
        dest = (d + k) % 16
        src = (d + 16 - k) % 16
        return pltpu.make_async_remote_copy(src_ref=cpart.at[dest], dst_ref=cond_ref.at[src if r else d], send_sem=csend.at[k], recv_sem=crecv.at[k], device_id=(x, dest), device_id_type=MESH)
    for k in range(1, 16):
        ccopy(k).start()
    cond_ref[d] = cpart[d]
    ys(0)
    zs(0)
    def final(w):
        s.f(w).wait()
        chip = place.chip(0, 0)
        if w == 2:
            out3_ref[...] = acc3[chip].astype(full) + rf[2][0].astype(full)
        else:
            span = slice(2304 * w, 2304 * w + 2304)
            fin[w] = (acc12[chip, :, span].astype(full) + rf[w][0].astype(full)).astype(low)
            fcopy(w).start()
    def fcopy(w):
        return pltpu.make_async_remote_copy(src_ref=fin.at[w], dst_ref=sibfin.at[w], send_sem=fsend.at[w], recv_sem=frecv.at[w], device_id=place.at(core=1), device_id_type=MESH)
    final(2)
    final(1)
    def write(w):
        fcopy(w).wait()
        mine, theirs = fin[w].astype(full), sibfin[w].astype(full)
        mine = jnp.where(c == 0, mine[0:72], mine[72:144])
        theirs = jnp.where(c == 0, theirs[0:72], theirs[72:144])
        out12_ref[:, 4608 * w : 4608 * w + 2304] = jnp.where(c == 0, mine, theirs)
        out12_ref[:, 4608 * w + 2304 : 4608 * w + 4608] = jnp.where(c == 0, theirs, mine)
    write(1)
    final(0)
    write(0)
    for k in range(1, 16):
        ccopy(k, True).wait_recv()
        ccopy(k).wait_send()
    for j in (1, 2, 3):
        vcopy(2 + j).wait_send()
        mz(j).wait_send()
    for j in range(4):
        my(j).wait_send()
        for yy in (0, 1):
            mx(j, yy).wait_send()
            for xx in (0, 1):
                ms(xx, j, yy).wait_send()
    for w in range(3):
        s.finish(w)
        for n in range(8):
            sib(w, n).wait_send()

def scatter_grads(mg, vec, inbox, mod, g12, g3):
    any_, vm = pl.BlockSpec(memory_space=pl.ANY), pl.BlockSpec(memory_space=pltpu.VMEM)
    a, rx, ry, rz, rf = rs_shapes()
    V, D = pltpu.VMEM, pltpu.SemaphoreType.DMA
    S = jax.ShapeDtypeStruct
    return pl.pallas_call(
        functools.partial(scatter_kernel, None),
        out_shape=(S((72, 9216), full), S((288, 1152), full), S(vec.shape, full), S((72, 6912), full), S((8, 6912), full), S((16, 8, 128), full)),
        in_specs=[vm, vm, vm, vm, any_, any_],
        out_specs=(vm,) * 6,
        scratch_shapes=a + rx + ry + rz + rf + [
            V((2, 144, 2304), low), V((2, 288, 1152), low), V((2, 144, 2304), low), V((2, 144, 2304), low),
            V((7,) + vec.shape, full), V(vec.shape, full), V((32, 32, 1152), low), V((16, 8, 128), full),
            D((3, 14)), D((3, 14)), D((3, 8)), D((3, 8)), D((3, 8)), D((6,)), D((6,)), D((32,)), D((32,)), D((16,)), D((16,)), D((2,)), D((2,))],
        compiler_params=pltpu.CompilerParams(collective_id=1, has_side_effects=True, vmem_limit_bytes=63 * 2**20),
    )(mg, vec, inbox, mod, g12, g3)


def shards(
    tokens,
    condition,
    segments,
    positions,
    buckets,
    modulator,
    modulator_bias,
    projector,
    projector_bias,
    position_table,
    output_weight,
    output_bias,
    up_weight,
    up_bias,
    down_weight,
    down_bias,
    cotangent,
):
    heads, bucket_count = position_table.shape
    image_tokens = buckets.shape[0]
    rows, model_width = tokens.shape[1], tokens.shape[2]
    images = condition.shape[1]
    shard = modulator.shape[0]
    feed_width = up_weight.shape[1]
    dp_index = lax.axis_index("dp")
    stream_index = lax.axis_index("stream")
    low = jnp.bfloat16
    full = jnp.float32

    def gather(part):
        return lax.all_gather(part, "dp", axis=0, tiled=True)

    inputs = tokens[0].astype(full)
    slot_ids, places = segments[0], positions[0]
    silu_value, silu_back = jax.vjp(jax.nn.silu, condition[0].astype(full))
    activated = silu_value.astype(low)
    activated_both = lax.all_gather(activated, ("stream", "dp"), axis=0, tiled=True)
    slots = activated_both.shape[0]
    activated_own = lax.dynamic_slice(activated_both, (0, dp_index * shard), (slots, shard))
    stream_slots = slots // 2
    partial = jnp.dot(
        lax.dynamic_slice(activated_own, (stream_index * stream_slots, 0), (stream_slots, shard)),
        modulator,
        preferred_element_type=full,
    )
    bias_parts = (modulator_bias, projector_bias, output_bias, up_bias, down_bias)
    bias_all = lax.all_gather(jnp.concatenate(bias_parts), "dp", axis=0)
    bias_full = []
    start = 0
    for part in bias_parts:
        bias_full.append(bias_all[:, start : start + part.shape[0]].reshape(-1).astype(full))
        start += part.shape[0]
    modulation = (
        lax.psum_scatter(partial, "dp", scatter_dimension=0, tiled=True) + bias_full[0]
    )
    projector_all = gather(projector)
    output_all = gather(output_weight)
    up_all = gather(up_weight)
    down_all = gather(down_weight)
    grid = bias_grid(position_table, buckets)
    local = slot_ids[:, None]
    per_token = jnp.where(
        local == 0, modulation[0:1], jnp.where(local == 1, modulation[1:2], modulation[2:3])
    )
    shift_attn, scale_attn, gate_attn, shift_mlp, scale_mlp, gate_mlp = jnp.split(
        per_token, 6, axis=1
    )
    normed_one, inverse_one = normalize(inputs)
    hidden_one = (normed_one * (1.0 + scale_attn) + shift_attn).astype(low)
    packed_bias = jnp.concatenate(
        [bias_full[1][:model_width], jnp.zeros((model_width,), full), bias_full[1][model_width:]]
    )
    packed = (
        jnp.dot(hidden_one, projector_all, preferred_element_type=full) + packed_bias
    ).astype(low)
    attended, placed, weights = attend_forward(packed, slot_ids, places, grid)
    branch_attn = jnp.dot(attended, output_all, preferred_element_type=full) + bias_full[2]
    middle = inputs + gate_attn * branch_attn
    normed_two, inverse_two = normalize(middle)
    hidden_two = (normed_two * (1.0 + scale_mlp) + shift_mlp).astype(low)
    up_output = jnp.dot(hidden_two, up_all, preferred_element_type=full) + bias_full[3]
    activation, gelu_back = jax.vjp(lambda v: jax.nn.gelu(v, approximate=True), up_output)
    activation_low = activation.astype(low)
    branch_mlp = jnp.dot(activation_low, down_all, preferred_element_type=full) + bias_full[4]
    result = (middle + gate_mlp * branch_mlp).astype(low)

    upstream = cotangent[0].astype(full)
    mlp_grad = (gate_mlp * upstream).astype(low)
    gate_mlp_grad = branch_mlp * upstream

    def scatter(grad):
        part = lax.psum_scatter(grad.astype(low), "dp", scatter_dimension=0, tiled=True)
        return lax.psum(part, "stream").astype(full)

    down_grad = scatter(
        jnp.einsum("tf,td->fd", activation_low, mlp_grad, preferred_element_type=full)
    )
    activation_grad = jnp.einsum("td,fd->tf", mlp_grad, down_all, preferred_element_type=full)
    up_grad_low = gelu_back(activation_grad)[0].astype(low)
    up_grad = scatter(
        jnp.einsum("td,tf->df", hidden_two, up_grad_low, preferred_element_type=full)
    )
    hidden_two_grad = jnp.einsum(
        "tf,df->td", up_grad_low, up_all, preferred_element_type=full
    )
    middle_grad = upstream + normalize_back(
        normed_two, inverse_two, hidden_two_grad * (1.0 + scale_mlp)
    )
    attn_grad = (gate_attn * middle_grad).astype(low)
    gate_attn_grad = branch_attn * middle_grad
    output_grad = scatter(
        jnp.einsum("td,te->de", attended, attn_grad, preferred_element_type=full)
    )
    attended_grad = jnp.einsum(
        "te,de->td", attn_grad, output_all, preferred_element_type=full
    ).astype(low)
    packed_grad, grid_grad = attend_backward(placed, weights, attended_grad, slot_ids, places)
    projector_grad = scatter(
        jnp.einsum("td,te->de", hidden_one, packed_grad, preferred_element_type=full)
    )
    table_grad = table_histogram(grid_grad, buckets, bucket_count)
    packed_sums = jnp.sum(packed_grad.astype(full), axis=0)
    sums = (
        table_grad.reshape(-1),
        packed_sums[:model_width],
        packed_sums[2 * model_width :],
        jnp.sum(attn_grad.astype(full), axis=0),
        jnp.sum(up_grad_low.astype(full), axis=0),
        jnp.sum(mlp_grad.astype(full), axis=0),
    )
    small = lax.psum(jnp.concatenate(sums), ("stream", "dp"))
    table_count = heads * bucket_count
    table_total = small[:table_count].reshape(heads, bucket_count)
    bias_grads = []
    start = table_count
    for part in bias_parts[1:]:
        size = part.shape[0]
        bias_grads.append(lax.dynamic_slice(small, (start + dp_index * size,), (size,)))
        start += size * (model_width // shard)
    hidden_one_grad = jnp.einsum(
        "te,de->td", packed_grad, projector_all, preferred_element_type=full
    )
    inputs_grad = middle_grad + normalize_back(
        normed_one, inverse_one, hidden_one_grad * (1.0 + scale_attn)
    )
    token_mod_grad = jnp.concatenate(
        [
            hidden_one_grad,
            hidden_one_grad * normed_one,
            gate_attn_grad,
            hidden_two_grad,
            hidden_two_grad * normed_two,
            gate_mlp_grad,
        ],
        axis=1,
    )
    modulation_grad = jnp.stack(
        [jnp.sum(jnp.where(local == slot, token_mod_grad, 0.0), axis=0) for slot in range(images)]
    ).astype(low)
    modulation_grad_both = lax.all_gather(modulation_grad, ("stream", "dp"), axis=0, tiled=True)
    modulator_grad = jnp.einsum(
        "id,ie->de", activated_own, modulation_grad_both, preferred_element_type=full
    )
    bias_width = modulator_bias.shape[0]
    modulator_bias_grad = jnp.sum(
        lax.dynamic_slice(
            modulation_grad_both, (0, dp_index * bias_width), (slots, bias_width)
        ).astype(full),
        axis=0,
    )
    activated_part = jnp.einsum(
        "ie,de->id",
        lax.dynamic_slice(
            modulation_grad_both, (stream_index * stream_slots, 0), (stream_slots, 6 * model_width)
        ),
        modulator,
        preferred_element_type=full,
    )
    activated_grad = (
        lax.all_to_all(
            activated_part.reshape(-1, images, shard), "dp", split_axis=0, concat_axis=0, tiled=True
        )
        .transpose(1, 0, 2)
        .reshape(images, model_width)
    )
    condition_grad = silu_back(activated_grad)[0]
    return (
        result[None],
        inputs_grad[None],
        condition_grad[None],
        modulator_grad,
        modulator_bias_grad,
        projector_grad,
        bias_grads[0],
        table_total,
        output_grad,
        bias_grads[1],
        up_grad,
        bias_grads[2],
        down_grad,
        bias_grads[3],
    )


def own_shards(
    tokens,
    condition,
    segments,
    positions,
    buckets,
    modulator,
    modulator_bias,
    projector,
    projector_bias,
    position_table,
    output_weight,
    output_bias,
    up_weight,
    up_bias,
    down_weight,
    down_bias,
    cotangent,
):
    heads, bucket_count = position_table.shape
    image_tokens = buckets.shape[0]
    rows, model_width = tokens.shape[1], tokens.shape[2]
    images = condition.shape[1]
    shard = modulator.shape[0]
    feed_width = up_weight.shape[1]
    dp_index = lax.axis_index("dp")
    stream_index = lax.axis_index("stream")
    low = jnp.bfloat16
    full = jnp.float32

    def gather(part):
        return lax.all_gather(part, "dp", axis=0, tiled=True)

    inputs = tokens[0].astype(full)
    slot_ids, places = segments[0], positions[0]
    silu_value, silu_back = jax.vjp(jax.nn.silu, condition[0].astype(full))
    activated = silu_value.astype(low)
    devices = model_width // shard
    bias_parts = (modulator_bias, projector_bias, output_bias, up_bias, down_bias)
    slices = jnp.pad(
        activated.astype(full).reshape(images, devices, shard).transpose(1, 0, 2),
        ((0, 0), (0, 8 - images), (0, 128 - shard)),
    )
    joined = jnp.concatenate(bias_parts).astype(full)
    joined = jnp.pad(joined, (0, 1024 - joined.shape[0])).reshape(1, 8, 128)
    notes = jnp.concatenate([slices, jnp.broadcast_to(joined, (devices, 8, 128))], axis=1)
    chips = devices // 2
    shard12 = jnp.pad(
        jnp.concatenate([projector, output_weight, feed_order(up_weight, 1, chips)], axis=1),
        ((0, 8), (0, 0)),
    )
    wide_modulator = jnp.pad(modulator, ((0, 128 - shard), (0, 0)))
    full12, down_all, inbox, modulation = gather_weights(
        notes, wide_modulator, shard12, down_weight
    )
    bias_all = lax.dynamic_slice(inbox, (stream_index * devices, 8, 0), (devices, 8, 128)).reshape(
        devices, 1024
    )
    bias_full = []
    start = 0
    for part in bias_parts:
        bias_full.append(bias_all[:, start : start + part.shape[0]].reshape(-1))
        start += part.shape[0]
    bias_full[3] = feed_order(bias_full[3], 0, chips)
    modulation = modulation[:3] + bias_full[0]
    packed_width = 3 * model_width
    projector_all = full12[:, :packed_width]
    output_all = full12[:, packed_width : 4 * model_width]
    up_all = full12[:, 4 * model_width :]
    grid = bias_grid(position_table, buckets)
    local = slot_ids[:, None]
    per_token = jnp.where(
        local == 0, modulation[0:1], jnp.where(local == 1, modulation[1:2], modulation[2:3])
    )
    shift_attn, scale_attn, gate_attn, shift_mlp, scale_mlp, gate_mlp = jnp.split(
        per_token, 6, axis=1
    )
    normed_one, inverse_one = normalize(inputs)
    hidden_one = (normed_one * (1.0 + scale_attn) + shift_attn).astype(low)
    packed_bias = jnp.concatenate(
        [bias_full[1][:model_width], jnp.zeros((model_width,), full), bias_full[1][model_width:]]
    )
    packed = (
        jnp.dot(hidden_one, projector_all, preferred_element_type=full) + packed_bias
    ).astype(low)
    attended, placed, weights = attend_forward(packed, slot_ids, places, grid)
    branch_attn = jnp.dot(attended, output_all, preferred_element_type=full) + bias_full[2]
    middle = inputs + gate_attn * branch_attn
    normed_two, inverse_two = normalize(middle)
    hidden_two = (normed_two * (1.0 + scale_mlp) + shift_mlp).astype(low)
    up_output = jnp.dot(hidden_two, up_all, preferred_element_type=full) + bias_full[3]
    activation, gelu_back = jax.vjp(lambda v: jax.nn.gelu(v, approximate=True), up_output)
    activation_low = activation.astype(low)
    branch_mlp = jnp.dot(activation_low, down_all, preferred_element_type=full) + bias_full[4]
    result = (middle + gate_mlp * branch_mlp).astype(low)

    upstream = cotangent[0].astype(full)
    mlp_grad = (gate_mlp * upstream).astype(low)
    gate_mlp_grad = branch_mlp * upstream

    down_grad = jnp.einsum("tf,td->fd", activation_low, mlp_grad, preferred_element_type=full)
    activation_grad = jnp.einsum("td,fd->tf", mlp_grad, down_all, preferred_element_type=full)
    up_grad_low = gelu_back(activation_grad)[0].astype(low)
    up_grad = jnp.einsum("td,tf->df", hidden_two, up_grad_low, preferred_element_type=full)
    hidden_two_grad = jnp.einsum(
        "tf,df->td", up_grad_low, up_all, preferred_element_type=full
    )
    middle_grad = upstream + normalize_back(
        normed_two, inverse_two, hidden_two_grad * (1.0 + scale_mlp)
    )
    attn_grad = (gate_attn * middle_grad).astype(low)
    gate_attn_grad = branch_attn * middle_grad
    output_grad = jnp.einsum("td,te->de", attended, attn_grad, preferred_element_type=full)
    attended_grad = jnp.einsum(
        "te,de->td", attn_grad, output_all, preferred_element_type=full
    ).astype(low)
    packed_grad, grid_grad = attend_backward(placed, weights, attended_grad, slot_ids, places)
    projector_grad = jnp.einsum("td,te->de", hidden_one, packed_grad, preferred_element_type=full)
    table_grad = table_histogram(grid_grad, buckets, bucket_count)
    packed_sums = jnp.sum(packed_grad.astype(full), axis=0)
    sums = (
        table_grad.reshape(-1),
        packed_sums[:model_width],
        packed_sums[2 * model_width :],
        jnp.sum(attn_grad.astype(full), axis=0),
        jnp.sum(up_grad_low.astype(full), axis=0),
        jnp.sum(mlp_grad.astype(full), axis=0),
    )
    hidden_one_grad = jnp.einsum(
        "te,de->td", packed_grad, projector_all, preferred_element_type=full
    )
    inputs_grad = middle_grad + normalize_back(
        normed_one, inverse_one, hidden_one_grad * (1.0 + scale_attn)
    )
    token_mod_grad = jnp.concatenate(
        [
            hidden_one_grad,
            hidden_one_grad * normed_one,
            gate_attn_grad,
            hidden_two_grad,
            hidden_two_grad * normed_two,
            gate_mlp_grad,
        ],
        axis=1,
    )
    modulation_grad = jnp.stack(
        [jnp.sum(jnp.where(local == slot, token_mod_grad, 0.0), axis=0) for slot in range(images)]
    ).astype(low)
    mg = modulation_grad.reshape(images, 6, model_width).transpose(1, 0, 2)
    mg = mg.reshape(6 * images, model_width)
    late = 2 * images
    mg = jnp.concatenate(
        [
            jnp.pad(mg[late:], ((0, 16 - 4 * images), (0, 0))),
            jnp.pad(mg[:late], ((0, 16 - late), (0, 0))),
        ]
    )
    vector = jnp.concatenate(sums)
    vector = jnp.pad(vector, (0, 25600 - vector.shape[0])).reshape(200, 128)
    grad12 = jnp.concatenate([projector_grad, output_grad, up_grad], axis=1).astype(low)
    out12, down_grad, small, modulator_grad, modulator_sums, cond_parts = scatter_grads(
        mg, vector, inbox, wide_modulator, grad12, down_grad.astype(low)
    )
    small = small.reshape(-1)
    table_count = heads * bucket_count
    table_total = small[:table_count].reshape(heads, bucket_count)
    bias_grads = []
    start = table_count
    for part in bias_parts[1:]:
        size = part.shape[0]
        whole = small[start : start + size * devices]
        if size == 4 * shard:
            whole = feed_restore(whole, 0, chips)
        bias_grads.append(lax.dynamic_slice(whole, (dp_index * size,), (size,)))
        start += size * devices
    bias_width = modulator_bias.shape[0]
    modulator_bias_grad = lax.dynamic_slice(
        modulator_sums[0], (dp_index * bias_width,), (bias_width,)
    )
    activated_grad = (
        cond_parts[:, :images, :shard].transpose(1, 0, 2).reshape(images, model_width)
    )
    projector_grad = out12[:, :packed_width]
    output_grad = out12[:, packed_width : 4 * model_width]
    up_grad = feed_restore(out12[:, 4 * model_width :], 1, chips)
    condition_grad = silu_back(activated_grad)[0]
    return (
        result[None],
        inputs_grad[None],
        condition_grad[None],
        modulator_grad,
        modulator_bias_grad,
        projector_grad,
        bias_grads[0],
        table_total,
        output_grad,
        bias_grads[1],
        up_grad,
        bias_grads[2],
        down_grad,
        bias_grads[3],
    )


def solution(mesh):
    in_specs = (
        P("stream", "dp", None),
        P("stream", "dp", None),
        P("stream", "dp"),
        P("stream", "dp"),
        P(),
        P("dp", None),
        P("dp"),
        P("dp", None),
        P("dp"),
        P(),
        P("dp", None),
        P("dp"),
        P("dp", None),
        P("dp"),
        P("dp", None),
        P("dp"),
        P("stream", "dp", None),
    )
    out_specs = (
        P("stream", "dp", None),
        P("stream", "dp", None),
        P("stream", "dp", None),
        P("dp", None),
        P("dp"),
        P("dp", None),
        P("dp"),
        P(),
        P("dp", None),
        P("dp"),
        P("dp", None),
        P("dp"),
        P("dp", None),
        P("dp"),
    )
    own = dict(mesh.shape) == {'stream': 2, 'dp': 16}
    return jax.shard_map(own_shards if own else shards, mesh=mesh, in_specs=in_specs, out_specs=out_specs, check_vma=False)
```

```python
import functools
import math

import jax
import jax.numpy as jnp
from jax import lax
from jax.experimental import pallas as pl
from jax.experimental.pallas import tpu as pltpu
from jax.sharding import PartitionSpec as P

norm_epsilon = 1e-06
masked_score=-1000000000.0

def grid_kernel(table_ref, buckets_ref, grid_ref):
    chunks = table_ref.shape[1]
    for half in range(buckets_ref.shape[1] // 128):
        span = slice(128 * half, 128 * half + 128)
        index = buckets_ref[:, span]
        low, high = index & 127, index >> 7
        total = jnp.zeros(index.shape, jnp.float32)
        for chunk in range(chunks):
            row = jnp.broadcast_to(table_ref[0, chunk : chunk + 1], index.shape)
            found = jnp.take_along_axis(row, low, axis=1)
            total = jnp.where(high == chunk, found, total)
        grid_ref[0, :, span] = total.astype(jnp.bfloat16)

def bias_grid(table, buckets):
    heads, count = table.shape
    chunks = -(-count // 128)
    wide = jnp.pad(table.astype(jnp.float32), ((0, 0), (0, chunks * 128 - count)))
    return pl.pallas_call(
        grid_kernel,
        grid=(heads,),
        in_specs=[pl.BlockSpec((1, chunks, 128), lambda h: (h, 0, 0)),
                  pl.BlockSpec(buckets.shape, lambda h: (0, 0))],
        out_specs=pl.BlockSpec((1,) + buckets.shape, lambda h: (h, 0, 0)),
        out_shape=jax.ShapeDtypeStruct((heads,) + buckets.shape, jnp.bfloat16),
    )(wide.reshape(heads, chunks, 128), buckets)

def hist_kernel(grad_ref, buckets_ref, out_ref):
    rows, heads, width = grad_ref.shape
    chunks = out_ref.shape[0] // heads
    @pl.when(pl.program_id(0) == 0)
    def _():
        out_ref[...] = jnp.zeros_like(out_ref)
    total = out_ref[...]
    for row in range(rows):
        index = buckets_ref[row : row + 1, :]
        low, high = index & 127, index >> 7
        mask = lax.broadcasted_iota(jnp.int32, (chunks, width), 0) == high
        values = jnp.where(mask[None], grad_ref[row][:, None, :], 0.0)
        left = values.reshape(heads * chunks, width).astype(jnp.bfloat16)
        right = (lax.broadcasted_iota(jnp.int32, (128, width), 0) == low).astype(jnp.float32).astype(jnp.bfloat16)
        total += lax.dot_general(left, right, (((1,), (1,)), ((), ())), preferred_element_type=jnp.float32)
    out_ref[...] = total

def table_histogram(grad, buckets, count):
    places, heads, width = grad.shape
    chunks = -(-count // 128)
    step = 16
    out = pl.pallas_call(
        hist_kernel,
        grid=(places // step,),
        in_specs=[pl.BlockSpec((step, heads, width), lambda a: (a, 0, 0)),
                  pl.BlockSpec((step, width), lambda a: (a, 0))],
        out_specs=pl.BlockSpec((heads * chunks, 128), lambda a: (0, 0)),
        out_shape=jax.ShapeDtypeStruct((heads * chunks, 128), jnp.float32),
    )(grad, buckets)
    return out.reshape(heads, chunks * 128)[:, :count]

def head_windows(heads, head_width):
    found = []
    for head in range(heads):
        start = head * head_width
        base = start // 128 * 128
        stop = -(-(start + head_width) // 128) * 128
        found.append((base, stop - base, start - base))
    return found

def lane_mask(rows, width, offset, head_width):
    lane = lax.broadcasted_iota(jnp.int32, (rows, width), 1)
    return (lane >= offset) & (lane < offset + head_width)

def nt(left, right):
    return lax.dot_general(left, right, (((1,), (1,)), ((), ())), preferred_element_type=jnp.float32)
def tn(left, right):
    return lax.dot_general(left, right, (((0,), (0,)), ((), ())), preferred_element_type=jnp.float32)
def nn(left, right):
    return lax.dot_general(left, right, (((1,), (0,)), ((), ())), preferred_element_type=jnp.float32)

def attend_forward_kernel(heads, packed_ref, frame_row_ref, frame_column_ref, grid_ref, attended_ref, placed_ref, weights_ref, mixed_ref):
    rows, width3 = packed_ref.shape
    frames = placed_ref.shape[0]
    places = grid_ref.shape[1]
    width = width3 // 3
    head_width = width // heads
    scale = head_width ** (-0.5)
    place = (lax.broadcasted_iota(jnp.int32, (frames, rows), 0) == frame_row_ref[...]).astype(jnp.float32).astype(jnp.bfloat16)
    for part in range(3):
        span = slice(part * width, part * width + width)
        placed_ref[:, span] = nn(place, packed_ref[:, span]).astype(jnp.bfloat16)
    filled = nt(jnp.ones((8, rows), jnp.bfloat16), place)[0:1] > 0.5
    filled_f = jnp.where(filled, 0.0, masked_score)
    mixed_ref[...] = jnp.zeros_like(mixed_ref)
    for image in range(frames // places):
        span_rows = slice(image * places, image * places + places)
        offset_row = filled_f[:, span_rows]
        for head, (base, wide, offset) in enumerate(head_windows(heads, head_width)):
            mask = lane_mask(places, wide, offset, head_width)
            query = placed_ref[span_rows, base : base + wide]
            key = placed_ref[span_rows, width + base : width + base + wide]
            value = placed_ref[span_rows, 2 * width + base : 2 * width + base + wide]
            query = jnp.where(mask, query, jnp.zeros_like(query))
            scores = nt(query, key) * scale + grid_ref[head].astype(jnp.float32)
            scores = jnp.where(offset_row < 0.0, masked_score, scores)
            exponent = jnp.exp(scores - jnp.max(scores, axis=-1, keepdims=True))
            weights = (exponent / jnp.sum(exponent, axis=-1, keepdims=True)).astype(jnp.bfloat16)
            weights_ref[image, head] = weights
            mixture = nn(weights, value).astype(jnp.bfloat16)
            before = mixed_ref[span_rows, base : base + wide]
            mixed_ref[span_rows, base : base + wide] = jnp.where(mask, mixture, before)
    back = (lax.broadcasted_iota(jnp.int32, (rows, frames), 1) == frame_column_ref[...]).astype(jnp.float32).astype(jnp.bfloat16)
    attended_ref[...] = nn(back, mixed_ref[...]).astype(jnp.bfloat16)

def attend_forward(packed, slots, places, grid):
    rows = packed.shape[0]
    heads, image, _ = grid.shape
    frame = slots * image + places
    frames = 3 * image
    width = packed.shape[1] // 3
    return pl.pallas_call(
        functools.partial(attend_forward_kernel, heads),
        out_shape=(jax.ShapeDtypeStruct((rows, width), jnp.bfloat16),
                   jax.ShapeDtypeStruct((frames, 3 * width), jnp.bfloat16),
                   jax.ShapeDtypeStruct((3, heads, image, image), jnp.bfloat16)),
        scratch_shapes=[pltpu.VMEM((frames, width), jnp.bfloat16)],
        compiler_params=pltpu.CompilerParams(vmem_limit_bytes=48 * 2**20),
    )(packed, frame[None, :], frame[:, None], grid)

def attend_backward_kernel(heads, placed_ref, weights_ref, upstream_ref, frame_row_ref, frame_column_ref, packed_grad_ref, grid_grad_ref, up_ref, grad_ref, bias_ref):
    frames, width3 = placed_ref.shape
    rows = upstream_ref.shape[0]
    places = weights_ref.shape[2]
    width = width3 // 3
    head_width = width // heads
    scale = head_width ** (-0.5)
    place = (lax.broadcasted_iota(jnp.int32, (frames, rows), 0) == frame_row_ref[...]).astype(jnp.float32).astype(jnp.bfloat16)
    up_ref[...] = nn(place, upstream_ref[...]).astype(jnp.bfloat16)
    grad_ref[...] = jnp.zeros_like(grad_ref)
    for head, (base, wide, offset) in enumerate(head_windows(heads, head_width)):
        mask = lane_mask(places, wide, offset, head_width)
        for image in range(frames // places):
            span_rows = slice(image * places, image * places + places)
            spans = [slice(part * width + base, part * width + base + wide) for part in range(3)]
            query, key = [jnp.where(mask, t, jnp.zeros_like(t)) for t in (placed_ref[span_rows, spans[0]], placed_ref[span_rows, spans[1]])]
            value = placed_ref[span_rows, spans[2]]
            upstream = up_ref[span_rows, spans[0]]
            upstream = jnp.where(mask, upstream, jnp.zeros_like(upstream))
            weights = weights_ref[image, head]
            weights_f = weights.astype(jnp.float32)
            weight_grads = nt(upstream, value)
            inner = jnp.sum(weight_grads * weights_f, axis=-1, keepdims=True)
            score_grads_f = weights_f * (weight_grads - inner)
            score_grads = score_grads_f.astype(jnp.bfloat16)
            if image == 0:
                bias_ref[...] = score_grads_f
            else:
                bias_ref[...] += score_grads_f
            grad_ref[span_rows, spans[0]] += (nn(score_grads, key) * scale).astype(jnp.bfloat16)
            grad_ref[span_rows, spans[1]] += (tn(score_grads, query) * scale).astype(jnp.bfloat16)
            grad_ref[span_rows, spans[2]] += tn(weights, upstream).astype(jnp.bfloat16)
        grid_grad_ref[:, head, :] = bias_ref[...]
    back = (lax.broadcasted_iota(jnp.int32, (rows, frames), 1) == frame_column_ref[...]).astype(jnp.float32).astype(jnp.bfloat16)
    for part in range(3):
        span = slice(part * width, part * width + width)
        packed_grad_ref[:, span] = nn(back, grad_ref[:, span]).astype(jnp.bfloat16)

def attend_backward(placed, weights, upstream, slots, places):
    rows, width = upstream.shape
    _, heads, image, _ = weights.shape
    frame = slots * image + places
    frames = 3 * image
    return pl.pallas_call(
        functools.partial(attend_backward_kernel, heads),
        out_shape=(jax.ShapeDtypeStruct((rows, 3 * width), jnp.bfloat16),
                   jax.ShapeDtypeStruct((image, heads, image), jnp.float32)),
        scratch_shapes=[pltpu.VMEM((frames, width), jnp.bfloat16),
                        pltpu.VMEM((frames, 3 * width), jnp.bfloat16),
                        pltpu.VMEM((image, image), jnp.float32)],
        compiler_params=pltpu.CompilerParams(vmem_limit_bytes=56 * 2**20),
    )(placed, weights, upstream, frame[None, :], frame[:, None])

def normalize(values):
    center = values - jnp.mean(values, axis=-1, keepdims=True)
    inverse = lax.rsqrt(jnp.mean(center * center, axis=-1, keepdims=True) + norm_epsilon)
    return (center * inverse, inverse)


def normalize_back(normed, inverse, upstream):
    return inverse * (
        upstream
        - jnp.mean(upstream, axis=-1, keepdims=True)
        - normed * jnp.mean(upstream * normed, axis=-1, keepdims=True)
    )


def smooth_gelu(values):
    return jax.nn.gelu(values, approximate=True)


MESH = pl.DeviceIdType.MESH
low = jnp.bfloat16
full = jnp.float32


def nt(left, right):
    return lax.dot_general(left, right, (((1,), (1,)), ((), ())), preferred_element_type=full)


def tn(left, right):
    return lax.dot_general(left, right, (((0,), (0,)), ((), ())), preferred_element_type=full)


def nn(left, right):
    return lax.dot_general(left, right, (((1,), (0,)), ((), ())), preferred_element_type=full)


def head_windows(heads, head_width):
    found = []
    for head in range(heads):
        start = head * head_width
        base = start // 128 * 128
        stop = -(-(start + head_width) // 128) * 128
        found.append((base, stop - base, start - base))
    return found


def lane_mask(rows, width, offset, head_width):
    lane = lax.broadcasted_iota(jnp.int32, (rows, width), 1)
    return (lane >= offset) & (lane < offset + head_width)


def one_hot(shape, axis, index):
    return (lax.broadcasted_iota(jnp.int32, shape, axis) == index).astype(full).astype(low)


def normalize_rows(values):
    center = values - jnp.mean(values, axis=-1, keepdims=True)
    inverse = lax.rsqrt(jnp.mean(center * center, axis=-1, keepdims=True) + norm_epsilon)
    return center * inverse, inverse


class Place:
    def __init__(self):
        self.x = lax.axis_index("stream")
        self.d = lax.axis_index("dp")
        self.z = self.d // 4
        self.y = (self.d // 2) % 2
        self.c = self.d % 2

    def zz(self, j):
        return (self.z, self.z + 1 - 2 * (self.z % 2), self.z + 2 - 4 * (self.z // 2), 3 - self.z)[j]

    def source(self, i):
        upper = self.z // 2
        return (self.z, self.z + 1 - 2 * (self.z % 2), 2 - upper, 3 - 3 * upper)[i]

    def chip(self, j=0, yy=0):
        return self.zz(j) * 2 + (self.y if yy == 0 else 1 - self.y)

    def far(self, i, yy=0):
        return self.source(i) * 2 + (self.y if yy == 0 else 1 - self.y)

    def at(self, x=0, y=0, j=0, core=0):
        xx = self.x if x == 0 else 1 - self.x
        cc = self.c if core == 0 else 1 - self.c
        return (xx, self.chip(j, y) * 2 + cc)

    def along(self, z):
        return (self.x, z * 4 + self.y * 2 + self.c)


def gather_region(x, c, full_ref, w, chip, part):
    if w < 2:
        off, size = {"all": (0, 2304), "ad": (1024 * x, 1280), "a": (1280 * x, 1024)}[part]
        col = pl.multiple_of(4608 * w + 2304 * c + off, 128)
        return full_ref[0].at[pl.ds(pl.multiple_of(chip * 144, 16), 144), pl.ds(col, size)]
    off, size = {"all": (0, 288), "ad": (128 * x, 160), "a": (160 * x, 128)}[part]
    row = pl.multiple_of(c * 2304 + chip * 288 + off, 16)
    return full_ref[1].at[pl.ds(row, size), :]


class Gather:
    def __init__(self, place, full_ref, send, recv):
        self.p, self.full, self.send, self.recv = place, full_ref, send, recv

    def copy(self, w, out, into, region, device):
        return pltpu.make_async_remote_copy(
            src_ref=region,
            dst_ref=region,
            send_sem=self.send.at[w, out],
            recv_sem=self.recv.at[w, into],
            device_id=device,
            device_id_type=MESH,
        )

    def region(self, w, chip, part, x=0, core=0):
        p = self.p
        return gather_region(
            p.x if x == 0 else 1 - p.x, p.c if core == 0 else 1 - p.c, self.full, w, chip, part
        )

    def along(self, w, out, source, to):
        p = self.p
        return self.copy(w, out, source, self.region(w, source * 2 + p.y, "ad"), p.along(to))

    def first(self, w, step):
        p = self.p
        to = jnp.clip(p.z + step, 0, 3)
        return self.along(w, 21 if step > 0 else 22, p.z, to)

    def onward(self, w, i):
        p = self.p
        source = p.source(i)
        to = jnp.clip(jnp.where(source < p.z, p.z + 1, p.z - 1), 0, 3)
        return self.along(w, i, source, to)

    def over_y(self, w, i, recv=False):
        p = self.p
        region = self.region(w, p.far(i, 1 if recv else 0), "all" if i == 0 else "ad")
        return self.copy(w, 4 + i, 4 + i, region, p.at(y=1))

    def over_x(self, w, i, yy, recv=False):
        p = self.p
        slot = 8 + 2 * (i - 1) + yy
        region = self.region(w, p.far(i, yy), "a", x=1 if recv else 0)
        return self.copy(w, slot, slot, region, p.at(x=1))

    def over_core(self, w, i, yy, recv=False):
        p = self.p
        slot = 13 + 2 * i + yy
        region = self.region(w, p.far(i, yy), "all", core=1 if recv else 0)
        return self.copy(w, slot, slot, region, p.at(core=1))

    def start(self, w):
        self.start_z(w)
        self.over_y(w, 0).start()

    def start_z(self, w):
        p = self.p

        @pl.when(p.z < 3)
        def _():
            self.first(w, 1).start()

        @pl.when(p.z > 0)
        def _():
            self.first(w, -1).start()

    def start_y(self, w):
        self.over_y(w, 0).start()

    def inner(self):
        return (self.p.z == 1) | (self.p.z == 2)

    def on_z(self, w, i):
        p = self.p
        self.along(w, i, p.source(i), p.z).wait_recv()

        @pl.when(self.inner())
        def _():
            self.onward(w, i).start()

        self.over_y(w, i).start()
        self.over_x(w, i, 0).start()

    def on_y(self, w, i):
        self.over_y(w, i, True).wait_recv()
        if i == 0:
            self.over_core(w, 0, 1).start()
        else:
            self.over_x(w, i, 1).start()

    def on_x(self, w, i, yy):
        self.over_x(w, i, yy, True).wait_recv()
        self.over_core(w, i, yy).start()

    def on_core(self, w):
        for i in range(4):
            for yy in (0, 1):
                if (i, yy) != (0, 0):
                    self.over_core(w, i, yy, True).wait_recv()

    def finish(self, w):
        p = self.p

        @pl.when(p.z < 3)
        def _():
            self.first(w, 1).wait_send()

        @pl.when(p.z > 0)
        def _():
            self.first(w, -1).wait_send()

        @pl.when(self.inner())
        def _():
            for i in (1, 2, 3):
                self.onward(w, i).wait_send()

        for i in range(4):
            self.over_y(w, i).wait_send()
            for yy in (0, 1):
                if i > 0:
                    self.over_x(w, i, yy).wait_send()
                if (i, yy) != (0, 0):
                    self.over_core(w, i, yy).wait_send()


def select_rows(modulation_ref, slots, piece, width):
    span = slice(piece * width, piece * width + width)
    return jnp.where(
        slots == 0,
        modulation_ref[0:1, span],
        jnp.where(slots == 1, modulation_ref[1:2, span], modulation_ref[2:3, span]),
    )


def forward_kernel(
    heads,
    note_ref,
    bias_note_ref,
    mod_in,
    shard_ref,
    tokens_in,
    cotangent_in,
    slots_ref,
    frame_row_ref,
    frame_column_ref,
    table_ref,
    buckets_ref,
    down_ref,
    full12_ref,
    full3_ref,
    hidden_one_out,
    placed_out,
    weights_out,
    attended_out,
    branch_out,
    middle_out,
    hidden_two_out,
    act_out,
    slope_out,
    result_out,
    mlp_grad_out,
    inbox_ref,
    modulation_ref,
    gate_sum_ref,
    mod_ref,
    tokens_ref,
    cotangent_ref,
    sib,
    chip_rows,
    part,
    got0,
    got1,
    bias_box,
    bias_packed,
    bias_out,
    bias_up,
    bias_down,
    grid,
    hidden_one,
    placed,
    weights,
    mixed,
    attended,
    branch,
    middle,
    hidden_two,
    act,
    slope,
    total,
    small_out,
    wide,
    msend,
    mrecv,
    bsend,
    brecv,
    csem,
    csend,
    crecv,
    psend,
    precv,
    send,
    recv,
    wsem,
    osem,
    psem,
    isem,
):
    place = Place()
    x, d, c = place.x, place.d, place.c
    rows, width = tokens_ref.shape
    places = buckets_ref.shape[0]
    frames = placed.shape[0]
    head_width = width // heads
    scale = head_width ** (-0.5)
    feed = act.shape[1]
    inputs = [
        pltpu.make_async_copy(mod_in, mod_ref, isem.at[0]),
        pltpu.make_async_copy(tokens_in, tokens_ref, isem.at[1]),
        pltpu.make_async_copy(cotangent_in, cotangent_ref, isem.at[2]),
    ]
    barrier = pltpu.get_barrier_semaphore()

    def peer(t, k):
        return (x if t == 0 else 1 - x, (d + k) % 16)

    others = [(t, k) for t in (0, 1) for k in range(16) if (t, k) != (0, 0)]
    for t, k in others:
        pl.semaphore_signal(barrier, inc=1, device_id=peer(t, k), device_id_type=MESH)
    mine = full3_ref.at[pl.ds(pl.multiple_of(c * 2304 + place.chip() * 288, 16), 288), :]
    own3 = pltpu.make_async_copy(down_ref, mine, csem.at[0])
    own3.start()
    for cp in inputs:
        cp.start()
    inbox_ref[x * 16 + d] = note_ref[d]
    bias_box[d] = bias_note_ref[...]
    pl.semaphore_wait(barrier, 31)

    def remote(src, dst, s, r, device):
        return pltpu.make_async_remote_copy(
            src_ref=src, dst_ref=dst, send_sem=s, recv_sem=r, device_id=device, device_id_type=MESH
        )

    half_width = 4 * width

    def sib_copy(w):
        span = pl.ds(w * half_width, half_width)
        return remote(
            shard_ref.at[:, span], sib.at[:, span], csend.at[w], crecv.at[w], place.at(core=1)
        )

    sib_copy(0).start()

    def note(t, k, recv_side=False):
        if recv_side:
            src = (x if t == 0 else 1 - x) * 16 + (d + 16 - k) % 16
        else:
            src = x * 16 + d
        return remote(
            note_ref.at[(d + k) % 16], inbox_ref.at[src], msend.at[t, k], mrecv.at[t, k], peer(t, k)
        )

    def bias_note(k, recv_side=False):
        src = (d + 16 - k) % 16 if recv_side else d
        return remote(bias_note_ref, bias_box.at[src], bsend.at[k], brecv.at[k], peer(0, k))

    for t, k in others:
        note(t, k).start()
    sib_copy(1).start()
    down_copy = remote(down_ref, mine, csend.at[2], crecv.at[2], place.at(core=1))
    columns = 512

    def assemble(w):
        def body(i, _):
            span = pl.ds(pl.multiple_of(i * columns, columns), columns)
            own, other = shard_ref[0:72, span].astype(full), sib[0:72, span].astype(full)
            top = jnp.where(c == 0, own, other)
            bottom = jnp.where(c == 0, other, own)
            chip_rows[:, span] = jnp.concatenate([top, bottom], axis=0).astype(low)
            return 0

        sib_copy(w).wait()
        first = w * half_width // columns
        lax.fori_loop(first, first + half_width // columns, body, 0)
        to = pl.ds(pl.multiple_of(place.chip() * 144, 16), 144)
        span = pl.ds(w * half_width, half_width)
        return pltpu.make_async_copy(
            chip_rows.at[:, span], full12_ref.at[to, span], csem.at[1 + w]
        )

    g = Gather(place, (full12_ref, full3_ref), send, recv)
    own1 = assemble(0)
    own1.start()
    own1.wait()

    def bias_grid(first, last):
        def body(h, _):
            for half in range(places // 128):
                span = slice(128 * half, 128 * half + 128)
                index = buckets_ref[:, span]
                lower, upper = index & 127, index >> 7
                found = jnp.zeros(index.shape, full)
                for chunk in range(table_ref.shape[1]):
                    row = jnp.broadcast_to(table_ref[h, chunk : chunk + 1], index.shape)
                    value = jnp.take_along_axis(row, lower, axis=1)
                    found = jnp.where(upper == chunk, value, found)
                grid[h, :, span] = found.astype(low)
            return 0

        lax.fori_loop(first, last, body, 0)

    def project_condition():
        for t, k in others:
            note(t, k, True).wait_recv()
        left = inbox_ref[pl.ds(x * 16, 16)].reshape(128, 128).astype(low)
        cols = 768

        def body(i, _):
            span = pl.ds(pl.multiple_of(i * cols, cols), cols)
            out = nn(left, mod_ref[:, span])
            for chip_at in range(8):
                for core in range(2):
                    dest = (chip_at * 2 + core) * 8
                    part[core, chip_at, :, span] = out[dest : dest + 4]
            return 0

        lax.fori_loop(0, mod_ref.shape[1] // cols, body, 0)
        half().start()

    def half():
        return remote(part.at[1 - c], got0, psend.at[0], precv.at[0], place.at(core=1))

    def share_condition():
        half().wait()
        for chip_at in range(8):
            part[c, chip_at] += got0[chip_at]
        for k in range(1, 8):
            share(k).start()

    def share(k):
        dest = (place.chip() + k) % 8
        return remote(
            part.at[c, dest], got1.at[k - 1], psend.at[k], precv.at[k], (x, dest * 2 + c)
        )

    def finish_condition():
        for k in range(1, 16):
            bias_note(k, True).wait_recv()
        bias_packed[...] = jnp.zeros_like(bias_packed)
        for at in range(16):
            box = bias_box[at]
            q = 144 * at + (width if at >= 8 else 0)
            bias_packed[0:1, q : q + 144] = box[1:2, 0:144]
            bias_out[0:1, 72 * at : 72 * at + 72] = box[2:3, 0:72]
            u = (at % 2) * (feed // 2) + (at // 2) * 288
            bias_up[0:1, u : u + 288] = box[3:4, 0:288]
            bias_down[0:1, 72 * at : 72 * at + 72] = box[4:5, 0:72]
            modulation_ref[0:1, 432 * at : 432 * at + 432] = box[0:1, 0:432]
        for k in range(1, 8):
            share(k).wait_recv()
        summed = part[c, place.chip()]
        for k in range(1, 8):
            summed += got1[k - 1]
        modulation_ref[...] = summed + modulation_ref[0:1, :]

    def copy_out(n, src, dst):
        return pltpu.make_async_copy(src, dst, osem.at[n])

    outs = []

    def put(src, dst):
        cp = copy_out(len(outs), src, dst)
        cp.start()
        outs.append(cp)

    step = 64

    def row_loop(first, last, body):
        def run(i, _):
            body(pl.ds(pl.multiple_of(i * step, step), step))
            return 0

        lax.fori_loop(first // step, last // step, run, 0)

    def norm_one(first, last):
        def body(span):
            normed, _ = normalize_rows(tokens_ref[span, :].astype(full))
            slots = slots_ref[span, :]
            shift = select_rows(modulation_ref, slots, 0, width)
            grow = select_rows(modulation_ref, slots, 1, width)
            hidden_one[span, :] = (normed * (1.0 + grow) + shift).astype(low)
            gate = select_rows(modulation_ref, slots, 5, width)
            small_out[span, :] = (gate * cotangent_ref[span, :].astype(full)).astype(low)

        row_loop(first, last, body)

    loads = []

    def fetch(src):
        n = len(loads)
        cp = pltpu.make_async_copy(src, wide.at[n % 2], wsem.at[n % 2])
        cp.start()
        loads.append(cp)
        return n

    def loaded(n):
        loads[n].wait()
        return wide.at[n % 2]

    tile = 384

    def w12(at):
        return full12_ref.at[:, pl.ds(at, width)]

    def project(n, piece):
        weight = loaded(n)
        where = one_hot((frames, rows), 0, frame_row_ref[...])

        def body(i, _):
            span = pl.ds(pl.multiple_of(i * tile, 128), tile)
            to = pl.ds(pl.multiple_of(piece * width + i * tile, 128), tile)
            out = nn(hidden_one[...], weight[:, span]) + bias_packed[0:1, to]
            placed[:, to] = nn(where, out.astype(low)).astype(low)
            return 0

        lax.fori_loop(0, width // tile, body, 0)

    windows = head_windows(heads, head_width)

    def attend(first, last):
        where = one_hot((frames, rows), 0, frame_row_ref[...])
        filled = nt(jnp.ones((8, rows), low), where)[0:1] > 0.5
        for head in range(first, last):
            base, wide_at, offset = windows[head]
            mask = lane_mask(places, wide_at, offset, head_width)
            slot = head % 2
            if head >= 2:
                weight_copy(head - 2).wait()
            for image in range(frames // places):
                at = slice(image * places, image * places + places)
                spans = [
                    slice(p * width + base, p * width + base + wide_at) for p in range(3)
                ]
                query = placed[at, spans[0]]
                query = jnp.where(mask, query, jnp.zeros_like(query))
                scores = nt(query, placed[at, spans[1]]) * scale + grid[head].astype(full)
                scores = jnp.where(filled[:, at], scores, masked_score)
                exponent = jnp.exp(scores - jnp.max(scores, axis=-1, keepdims=True))
                share_of = (exponent / jnp.sum(exponent, axis=-1, keepdims=True)).astype(low)
                weights[slot, image] = share_of
                mixture = nn(share_of, placed[at, spans[2]]).astype(low)
                mixed[at, spans[0]] = jnp.where(mask, mixture, mixed[at, spans[0]])
            weight_copy(head).start()

    def weight_copy(head):
        return pltpu.make_async_copy(weights.at[head % 2], weights_out.at[head], psem.at[head % 2])

    def gather_back():
        back = one_hot((rows, frames), 1, frame_column_ref[...])
        attended[...] = nn(back, mixed[...]).astype(low)

    def out_project(n):
        weight = loaded(n)

        def body(i, _):
            span = pl.ds(pl.multiple_of(i * tile, 128), tile)
            branch[:, span] = nn(attended[...], weight[:, span]) + bias_out[0:1, span]
            return 0

        lax.fori_loop(0, width // tile, body, 0)

    def norm_two():
        def body(span):
            slots = slots_ref[span, :]
            gate = select_rows(modulation_ref, slots, 2, width)
            mid = tokens_ref[span, :].astype(full) + gate * branch[span, :]
            middle[span, :] = mid
            normed, _ = normalize_rows(mid)
            shift = select_rows(modulation_ref, slots, 3, width)
            grow = select_rows(modulation_ref, slots, 4, width)
            hidden_two[span, :] = (normed * (1.0 + grow) + shift).astype(low)

        row_loop(0, rows, body)

    root = math.sqrt(2.0 / math.pi)

    def up(n, piece):
        weight = loaded(n)

        def body(i, _):
            span = pl.ds(pl.multiple_of(i * tile, 128), tile)
            to = pl.ds(pl.multiple_of(piece * width + i * tile, 128), tile)
            v = nn(hidden_two[...], weight[:, span]) + bias_up[0:1, to]
            square = v * v
            bend = jnp.tanh(root * (v + 0.044715 * (v * square)))
            half = 0.5 * (1.0 + bend)
            act[:, to] = (v * half).astype(low)
            rise = root * (1.0 + (3.0 * 0.044715) * square)
            slope[:, to] = (half + 0.5 * v * (1.0 - bend * bend) * rise).astype(low)
            return 0

        lax.fori_loop(0, width // tile, body, 0)

    def down(n, piece):
        weight = loaded(n)

        def body(i, _):
            span = pl.ds(pl.multiple_of(i * tile, 128), tile)
            out = nn(act[:, piece * width : piece * width + width], weight[:, span])
            if piece == 0:
                total[:, span] = out + bias_down[0:1, span]
            else:
                total[:, span] += out
            return 0

        lax.fori_loop(0, width // tile, body, 0)

    def finish_rows():
        gate_sum_ref[...] = jnp.zeros_like(gate_sum_ref)

        def body(span):
            slots = slots_ref[span, :]
            gate = select_rows(modulation_ref, slots, 5, width)
            out = total[span, :]
            hidden_one[span, :] = (middle[span, :] + gate * out).astype(low)
            product = out * cotangent_ref[span, :].astype(full)
            for slot in range(3):
                gate_sum_ref[slot : slot + 1, :] += jnp.sum(
                    jnp.where(slots == slot, product, 0.0), axis=0, keepdims=True
                )

        row_loop(0, rows, body)

    g.start_z(0)
    g.start_y(0)
    own2 = assemble(1)
    own2.start()
    for k in range(1, 16):
        bias_note(k).start()
    down_copy.start()
    own3.wait()
    own2.wait()
    g.start_z(1)
    g.on_z(0, 1)
    g.on_z(1, 1)
    g.on_z(0, 2)
    g.on_y(0, 1)
    g.on_x(1, 1, 0)
    g.on_z(0, 3)
    g.start_y(1)
    inputs[0].wait()
    project_condition()
    g.start_z(2)
    g.on_x(0, 1, 1)
    g.on_x(0, 1, 0)
    share_condition()
    g.on_y(0, 2)
    bias_grid(0, 6)
    g.on_y(0, 3)
    g.on_x(0, 3, 0)
    bias_grid(6, 9)
    g.on_x(0, 2, 0)
    g.on_x(0, 2, 1)
    g.on_y(1, 1)
    g.on_z(1, 2)
    finish_condition()
    bias_grid(9, 13)
    inputs[1].wait()
    inputs[2].wait()
    norm_one(0, rows // 2)
    g.on_x(0, 3, 1)
    g.on_z(1, 3)
    bias_grid(13, heads)
    g.on_y(0, 0)
    g.on_core(0)
    norm_one(rows // 2, rows)
    put(hidden_one, hidden_one_out)
    put(small_out, mlp_grad_out)
    g.on_z(2, 1)
    g.on_y(1, 2)
    g.on_y(1, 0)
    a = fetch(w12(0))
    b = fetch(w12(width))
    project(a, 0)
    a = fetch(w12(2 * width))
    g.on_z(2, 2)
    project(b, 1)
    b = fetch(w12(3 * width))
    g.on_y(1, 3)
    g.on_x(1, 1, 1)
    g.start_y(2)
    project(a, 2)
    put(placed, placed_out)
    mixed[...] = jnp.zeros_like(mixed)
    attend(0, 3)
    g.on_z(2, 3)
    attend(3, 6)
    attend(6, 10)
    g.on_x(1, 2, 1)
    g.on_x(1, 3, 0)
    g.on_x(1, 2, 0)
    g.on_y(2, 2)
    attend(10, 13)
    g.on_x(2, 2, 0)
    attend(13, heads)
    g.on_x(2, 1, 0)
    g.on_y(2, 1)
    g.on_x(1, 3, 1)
    gather_back()
    put(attended, attended_out)
    out_project(b)
    put(branch, branch_out)
    norm_two()
    put(middle, middle_out)
    put(hidden_two, hidden_two_out)
    g.on_core(1)
    a = fetch(w12(4 * width))
    b = fetch(w12(5 * width))
    g.on_y(2, 3)
    g.on_x(2, 2, 1)
    up(a, 0)
    a = fetch(w12(6 * width))
    up(b, 1)
    b = fetch(w12(7 * width))
    g.on_x(2, 3, 0)
    g.on_y(2, 0)
    up(a, 2)
    g.on_x(2, 1, 1)
    g.on_x(2, 3, 1)
    up(b, 3)
    put(act, act_out)
    put(slope, slope_out)
    g.on_core(2)
    down_copy.wait()
    outs[0].wait()
    pieces = feed // width
    a = fetch(full3_ref.at[pl.ds(0, width), :])
    for piece in range(pieces):
        if piece + 1 < pieces:
            b = fetch(full3_ref.at[pl.ds((piece + 1) * width, width), :])
        down(a, piece)
        a = b
    finish_rows()
    put(hidden_one, result_out)
    for cp in outs[1:]:
        cp.wait()
    weight_copy(heads - 2).wait()
    weight_copy(heads - 1).wait()
    for w in range(3):
        g.finish(w)
    for t, k in others:
        note(t, k).wait_send()
    for k in range(1, 16):
        bias_note(k).wait_send()
    for k in range(1, 8):
        share(k).wait_send()


def forward_pass(heads, notes, bias_note, modulator, shard12, tokens, cotangent, slots, frame, table, buckets, down):
    rows, width = tokens.shape
    feed = 4 * width
    places = buckets.shape[0]
    frames = 3 * places
    any_, vm = pl.BlockSpec(memory_space=pl.ANY), pl.BlockSpec(memory_space=pltpu.VMEM)
    V, D, S = pltpu.VMEM, pltpu.SemaphoreType.DMA, jax.ShapeDtypeStruct
    count = table.shape[1]
    chunks = -(-count // 128)
    table = jnp.pad(table.astype(full), ((0, 0), (0, chunks * 128 - count)))
    table = table.reshape(heads, chunks, 128)
    return pl.pallas_call(
        functools.partial(forward_kernel, heads),
        out_shape=(
            S((width, 2 * feed), low),
            S((feed, width), low),
            S((rows, width), low),
            S((frames, 3 * width), low),
            S((heads, 3, places, places), low),
            S((rows, width), low),
            S((rows, width), full),
            S((rows, width), full),
            S((rows, width), low),
            S((rows, feed), low),
            S((rows, feed), low),
            S((rows, width), low),
            S((rows, width), low),
            S((32, 8, 128), full),
            S((4, 6 * width), full),
            S((8, width), full),
        ),
        in_specs=[vm, vm, any_, vm, any_, any_] + [vm] * 6,
        out_specs=(any_,) * 13 + (vm,) * 3,
        scratch_shapes=[
            V(modulator.shape, low),
            V(tokens.shape, low),
            V(tokens.shape, low),
            V(shard12.shape, low),
            V((144, shard12.shape[1]), low),
            V((2, 8, 4, 6 * width), full),
            V((8, 4, 6 * width), full),
            V((7, 4, 6 * width), full),
            V((16,) + bias_note.shape, full),
            V((1, 3 * width), full),
            V((1, width), full),
            V((1, feed), full),
            V((1, width), full),
            V((heads, places, places), low),
            V((rows, width), low),
            V((frames, 3 * width), low),
            V((2, 3, places, places), low),
            V((frames, width), low),
            V((rows, width), low),
            V((rows, width), full),
            V((rows, width), full),
            V((rows, width), low),
            V((rows, feed), low),
            V((rows, feed), low),
            V((rows, width), full),
            V((rows, width), low),
            V((2, width, width), low),
            D((2, 16)),
            D((2, 16)),
            D((16,)),
            D((16,)),
            D((3,)),
            D((3,)),
            D((3,)),
            D((8,)),
            D((8,)),
            D((3, 23)),
            D((3, 23)),
            D((2,)),
            D((16,)),
            D((2,)),
            D((3,)),
        ],
        compiler_params=pltpu.CompilerParams(
            collective_id=0, has_side_effects=True, vmem_limit_bytes=63 * 2**20
        ),
    )(notes, bias_note, modulator, shard12, tokens, cotangent, slots[:, None], frame[None, :], frame[:, None], table, buckets, down)


def feed_order(values, axis, chips):
    shape = values.shape
    part = shape[axis] // (2 * chips)
    split = shape[:axis] + (chips, 2, part) + shape[axis + 1 :]
    return jnp.swapaxes(values.reshape(split), axis, axis + 1).reshape(shape)
def feed_restore(values, axis, chips):
    shape = values.shape
    part = shape[axis] // (2 * chips)
    split = shape[:axis] + (2, chips, part) + shape[axis + 1 :]
    return jnp.swapaxes(values.reshape(split), axis, axis + 1).reshape(shape)


def rs_part(place, w, part):
    x = place.x
    unit = 768 if w < 2 else 96
    off, size = {"all": (0, 3), "ad": (x, 2), "a": (2 * x, 1), "o": (2 - 2 * x, 1), "od": (1 - x, 2)}[part]
    return pl.multiple_of(unit * off, 128 if w < 2 else 16), unit * size

class Scatter:
    def __init__(self, place, acc12, acc3, rx, ry, rz, rf, send, recv):
        self.p, self.acc12, self.acc3, self.rx, self.ry, self.rz, self.rf, self.send, self.recv = place, acc12, acc3, rx, ry, rz, rf, send, recv
    def acc(self, w, chip, part):
        off, size = rs_part(self.p, w, part)
        if w < 2:
            return self.acc12.at[chip, :, pl.ds(2304 * w + off, size)]
        return self.acc3.at[chip, pl.ds(off, size), :]
    def land(self, w, kind, i, size=None):
        b = {"x": self.rx, "y": self.ry, "z": self.rz, "f": self.rf, "Y": self.rf}[kind]
        if kind == "f":
            return self.rf[w].at[0]
        if kind == "Y":
            return self.rf[w].at[1]
        return b[w].at[i]
    def copy(self, w, slot, src, dst, device):
        return pltpu.make_async_remote_copy(src_ref=src, dst_ref=dst, send_sem=self.send.at[w, slot], recv_sem=self.recv.at[w, slot], device_id=device, device_id_type=MESH)
    def x(self, w, j, yy):
        return self.copy(w, 2 * (j - 1) + yy, self.acc(w, self.p.chip(j, yy), "o"), self.land(w, "x", 2 * (j - 1) + yy), self.p.at(x=1))
    def y(self, w, j):
        return self.copy(w, 5 + j, self.acc(w, self.p.chip(j, 1), "ad"), self.land(w, "y", j - 1), self.p.at(y=1))
    def Y(self, w):
        return self.copy(w, 9, self.acc(w, self.p.chip(0, 1), "all"), self.land(w, "Y", 0), self.p.at(y=1))
    def z(self, w, j):
        return self.copy(w, 9 + j, self.acc(w, self.p.chip(j, 0), "ad"), self.land(w, "z", j - 1), self.p.at(j=j))
    def f(self, w):
        return self.copy(w, 13, self.acc(w, self.p.chip(0, 0), "all"), self.land(w, "f", 0), self.p.at(x=1))
    def add(self, w, chip, part, land):
        dst = self.acc(w, chip, part)
        rows = dst.shape[0]
        step = 48
        def body(i, _):
            span = pl.ds(pl.multiple_of(i * step, 16), step)
            dst[span, :] = dst[span, :] + land[span, :]
            return 0
        lax.fori_loop(0, rows // step, body, 0)
    def ready(self, w, j, yy):
        if j > 0:
            self.x(w, j, yy).start()
        elif yy == 1:
            self.Y(w).start()
    def on_x(self, w, j, yy):
        self.x(w, j, yy).wait_recv()
        self.add(w, self.p.chip(j, yy), "a", self.land(w, "x", 2 * (j - 1) + yy))
        if yy == 1:
            self.y(w, j).start()
    def on_y(self, w, j):
        self.y(w, j).wait_recv()
        self.add(w, self.p.chip(j, 0), "ad", self.land(w, "y", j - 1))
        self.z(w, j).start()
    def on_Y(self, w):
        self.Y(w).wait_recv()
        self.add(w, self.p.chip(0, 0), "all", self.land(w, "Y", 0))
    def on_z(self, w, j):
        self.z(w, j).wait_recv()
        self.add(w, self.p.chip(0, 0), "ad", self.land(w, "z", j - 1))
    def last(self, w):
        self.f(w).start()
    def finish(self, w):
        for j in (1, 2, 3):
            for yy in (0, 1):
                self.x(w, j, yy).wait_send()
            self.y(w, j).wait_send()
            self.z(w, j).wait_send()
        self.Y(w).wait_send()

def rs_shapes():
    V, D = pltpu.VMEM, pltpu.SemaphoreType.DMA
    a = [V((8, 144, 4608), low), V((8, 288, 1152), low)]
    rx = [V((6, 144, 768), low), V((6, 144, 768), low), V((6, 96, 1152), low)]
    ry = [V((3, 144, 1536), low), V((3, 144, 1536), low), V((3, 192, 1152), low)]
    rz = [V((3, 144, 1536), low), V((3, 144, 1536), low), V((3, 192, 1152), low)]
    rf = [V((2, 144, 2304), low), V((2, 144, 2304), low), V((2, 288, 1152), low)]
    return a, rx, ry, rz, rf

def scatter_kernel(sizes, mg_ref, vec_ref, inbox_ref, mod_ref, g12_ref, g3_ref,
                   out12_ref, out3_ref, vec_out_ref, gmod_ref, gmodsum_ref, cond_ref, *rest):
    it = iter(rest)
    take = lambda n: [next(it) for _ in range(n)]
    acc12, acc3 = take(2)
    rx, ry, rz, rf = take(3), take(3), take(3), take(3)
    own12, own3, fin, sibfin = take(4)
    vbuf, vsum, mgall, cpart = take(4)
    send, recv, ssend, srecv, lsem, vsend, vrecv, msend, mrecv, csend, crecv, fsend, frecv = take(13)
    place = Place()
    x, d, c, z = place.x, place.d, place.c, place.z
    barrier = pltpu.get_barrier_semaphore()
    for k in range(1, 16):
        pl.semaphore_signal(barrier, inc=1, device_id=(x, (d + k) % 16), device_id_type=MESH)
    pl.semaphore_signal(barrier, inc=1, device_id=place.at(x=1), device_id_type=MESH)
    pl.semaphore_wait(barrier, 16)
    s = Scatter(place, acc12, acc3, rx, ry, rz, rf, send, recv)
    order = [(1, 1), (1, 0), (2, 1), (2, 0), (3, 1), (3, 0), (0, 1), (0, 0)]
    def sib(w, n, recv_side=False):
        j, yy = order[n]
        chip = place.chip(j, yy)
        cc = 1 - c
        if w < 2:
            src = g12_ref.at[pl.ds(pl.multiple_of(chip * 144, 16), 144), pl.ds(pl.multiple_of(4608 * w + 2304 * cc, 128), 2304)]
            dst = acc12.at[chip, :, pl.ds(2304 * w, 2304)]
        else:
            src = g3_ref.at[pl.ds(pl.multiple_of(cc * 2304 + chip * 288, 16), 288), :]
            dst = acc3.at[chip]
        return pltpu.make_async_remote_copy(src_ref=src, dst_ref=dst, send_sem=ssend.at[w, n], recv_sem=srecv.at[w, n], device_id=place.at(core=1), device_id_type=MESH)
    def own(w, n):
        j, yy = order[n]
        chip = place.chip(j, yy)
        if w < 2:
            src = g12_ref.at[pl.ds(pl.multiple_of(chip * 144, 16), 144), pl.ds(pl.multiple_of(4608 * w + 2304 * c, 128), 2304)]
            dst = own12.at[n % 2]
        else:
            src = g3_ref.at[pl.ds(pl.multiple_of(c * 2304 + chip * 288, 16), 288), :]
            dst = own3.at[n % 2]
        return pltpu.make_async_copy(src, dst, lsem.at[w, n])
    def stage0(w):
        for n in range(8):
            sib(w, n).start()
        own(w, 0).start()
        for n in range(8):
            if n < 7:
                own(w, n + 1).start()
            own(w, n).wait()
            sib(w, n).wait_recv()
            j, yy = order[n]
            s.add(w, place.chip(j, yy), "all", (own12 if w < 2 else own3).at[n % 2])
            s.ready(w, j, yy)
    def mids(w):
        for j in (1, 2, 3):
            s.on_x(w, j, 1)
            s.on_x(w, j, 0)
    def ys(w):
        for j in (1, 2, 3):
            s.on_y(w, j)
        s.on_Y(w)
    def zs(w):
        for j in (1, 2, 3):
            s.on_z(w, j)
        s.last(w)
    def vcopy(n):
        if n < 3:
            dev = (place.at(core=1), place.at(x=1), place.at(y=1))[n]
            return pltpu.make_async_remote_copy(src_ref=vsum, dst_ref=vbuf.at[n], send_sem=vsend.at[n], recv_sem=vrecv.at[n], device_id=dev, device_id_type=MESH)
        j = n - 2
        return pltpu.make_async_remote_copy(src_ref=vsum, dst_ref=vbuf.at[3 + z], send_sem=vsend.at[n], recv_sem=vrecv.at[n], device_id=place.at(j=j), device_id_type=MESH)
    def vrecv_wait(j):
        pltpu.make_async_remote_copy(src_ref=vsum, dst_ref=vbuf.at[3 + place.zz(j)], send_sem=vsend.at[2 + j], recv_sem=vrecv.at[2 + j], device_id=place.at(j=j), device_id_type=MESH).wait_recv()
    def mrow(xx, chip, cc):
        return (x if xx == 0 else 1 - x) * 16 + chip * 2 + (c if cc == 0 else 1 - c)
    def mcopy(slot, row, dev):
        return pltpu.make_async_remote_copy(src_ref=mgall.at[row], dst_ref=mgall.at[row], send_sem=msend.at[slot], recv_sem=mrecv.at[slot], device_id=dev, device_id_type=MESH)
    def mz(j, r=False):
        return mcopy(j, mrow(0, place.chip(j if r else 0), 0), place.at(j=j))
    def my(j, r=False):
        return mcopy(4 + j, mrow(0, place.chip(j, 1 if r else 0), 0), place.at(y=1))
    def mx(j, yy, r=False):
        return mcopy(8 + 2 * j + yy, mrow(1 if r else 0, place.chip(j, yy), 0), place.at(x=1))
    def ms(xx, j, yy, r=False):
        return mcopy(16 + xx * 8 + 2 * j + yy, mrow(xx, place.chip(j, yy), 1 if r else 0), place.at(core=1))
    stage0(2)
    vsum[...] = vec_ref[...]
    mgall[x * 16 + d] = mg_ref[...]
    vcopy(0).start()
    for j in (1, 2, 3):
        mz(j).start()
    my(0).start()
    mx(0, 0).start()
    ms(0, 0, 0).start()
    vcopy(0).wait()
    vsum[...] += vbuf[0]
    vcopy(1).start()
    for j in (1, 2, 3):
        mz(j, True).wait_recv()
        my(j).start()
        mx(j, 0).start()
        ms(0, j, 0).start()
    mids(2)
    vcopy(1).wait()
    vsum[...] += vbuf[1]
    vcopy(2).start()
    for j in (0, 1, 2, 3):
        my(j, True).wait_recv()
        mx(j, 1).start()
        ms(0, j, 1).start()
    stage0(1)
    ys(2)
    vcopy(2).wait()
    vsum[...] += vbuf[2]
    for j in (1, 2, 3):
        vcopy(2 + j).start()
    vbuf[3 + z] = vsum[...]
    for yy in (0, 1):
        for j in range(4):
            mx(j, yy, True).wait_recv()
            ms(1, j, yy).start()
    mids(1)
    zs(2)
    stage0(0)
    ys(1)
    mids(0)
    zs(1)
    for j in (1, 2, 3):
        vrecv_wait(j)
    vec_out_ref[...] = vbuf[3] + vbuf[4] + vbuf[5] + vbuf[6]
    for xx in (0, 1):
        for yy in (0, 1):
            for j in range(4):
                ms(xx, j, yy, True).wait_recv()
    def place_rows(p, devices):
        base = 3 * (p - 2) if p >= 2 else 3 * p
        shape = (devices * 16, devices * 8)
        r, q = lax.broadcasted_iota(jnp.int32, shape, 0), lax.broadcasted_iota(jnp.int32, shape, 1)
        return ((r // 16 == q // 8) & (r % 16 - base == q % 8) & (q % 8 < 3)).astype(full).astype(low)
    act = inbox_ref[...].reshape(256, 128).astype(low)
    cond_total = jnp.zeros((128, 128), full)
    for p in range(6):
        tile = 0 if p >= 2 else 1
        span = slice(1152 * p, 1152 * p + 1152)
        pieces = mgall[:, 16 * tile : 16 * tile + 16, :].reshape(512, 1152)
        where = place_rows(p, 32)
        left = jnp.dot(where, act, preferred_element_type=full).astype(low)
        grad = lax.dot_general(left, pieces, (((0,), (0,)), ((), ())), preferred_element_type=full)
        gmod_ref[:, span] = grad[0:72]
        ones = jnp.broadcast_to((jnp.sum(where.astype(full), axis=1, keepdims=True)).astype(low), (512, 128))
        gmodsum_ref[:, span] = lax.dot_general(ones, pieces, (((0,), (0,)), ((), ())), preferred_element_type=full)[0:8]
        mine = mgall[pl.ds(x * 16, 16), 16 * tile : 16 * tile + 16, :].reshape(256, 1152)
        rows = lax.dot_general(place_rows(p, 16), mine, (((0,), (0,)), ((), ())), preferred_element_type=full).astype(low)
        cond_total += lax.dot_general(rows, mod_ref[:, span], (((1,), (1,)), ((), ())), preferred_element_type=full)
    cpart[...] = cond_total.reshape(16, 8, 128)
    def ccopy(k, r=False):
        dest = (d + k) % 16
        src = (d + 16 - k) % 16
        return pltpu.make_async_remote_copy(src_ref=cpart.at[dest], dst_ref=cond_ref.at[src if r else d], send_sem=csend.at[k], recv_sem=crecv.at[k], device_id=(x, dest), device_id_type=MESH)
    for k in range(1, 16):
        ccopy(k).start()
    cond_ref[d] = cpart[d]
    ys(0)
    zs(0)
    def final(w):
        s.f(w).wait()
        chip = place.chip(0, 0)
        if w == 2:
            out3_ref[...] = acc3[chip].astype(full) + rf[2][0].astype(full)
        else:
            span = slice(2304 * w, 2304 * w + 2304)
            fin[w] = (acc12[chip, :, span].astype(full) + rf[w][0].astype(full)).astype(low)
            fcopy(w).start()
    def fcopy(w):
        return pltpu.make_async_remote_copy(src_ref=fin.at[w], dst_ref=sibfin.at[w], send_sem=fsend.at[w], recv_sem=frecv.at[w], device_id=place.at(core=1), device_id_type=MESH)
    final(2)
    final(1)
    def write(w):
        fcopy(w).wait()
        mine, theirs = fin[w].astype(full), sibfin[w].astype(full)
        mine = jnp.where(c == 0, mine[0:72], mine[72:144])
        theirs = jnp.where(c == 0, theirs[0:72], theirs[72:144])
        out12_ref[:, 4608 * w : 4608 * w + 2304] = jnp.where(c == 0, mine, theirs)
        out12_ref[:, 4608 * w + 2304 : 4608 * w + 4608] = jnp.where(c == 0, theirs, mine)
    write(1)
    final(0)
    write(0)
    for k in range(1, 16):
        ccopy(k, True).wait_recv()
        ccopy(k).wait_send()
    for j in (1, 2, 3):
        vcopy(2 + j).wait_send()
        mz(j).wait_send()
    for j in range(4):
        my(j).wait_send()
        for yy in (0, 1):
            mx(j, yy).wait_send()
            for xx in (0, 1):
                ms(xx, j, yy).wait_send()
    for w in range(3):
        s.finish(w)
        for n in range(8):
            sib(w, n).wait_send()

def scatter_grads(mg, vec, inbox, mod, g12, g3):
    any_, vm = pl.BlockSpec(memory_space=pl.ANY), pl.BlockSpec(memory_space=pltpu.VMEM)
    a, rx, ry, rz, rf = rs_shapes()
    V, D = pltpu.VMEM, pltpu.SemaphoreType.DMA
    S = jax.ShapeDtypeStruct
    return pl.pallas_call(
        functools.partial(scatter_kernel, None),
        out_shape=(S((72, 9216), full), S((288, 1152), full), S(vec.shape, full), S((72, 6912), full), S((8, 6912), full), S((16, 8, 128), full)),
        in_specs=[vm, vm, vm, vm, any_, any_],
        out_specs=(vm,) * 6,
        scratch_shapes=a + rx + ry + rz + rf + [
            V((2, 144, 2304), low), V((2, 288, 1152), low), V((2, 144, 2304), low), V((2, 144, 2304), low),
            V((7,) + vec.shape, full), V(vec.shape, full), V((32, 32, 1152), low), V((16, 8, 128), full),
            D((3, 14)), D((3, 14)), D((3, 8)), D((3, 8)), D((3, 8)), D((6,)), D((6,)), D((32,)), D((32,)), D((16,)), D((16,)), D((2,)), D((2,))],
        compiler_params=pltpu.CompilerParams(collective_id=1, has_side_effects=True, vmem_limit_bytes=63 * 2**20),
    )(mg, vec, inbox, mod, g12, g3)


def shards(
    tokens,
    condition,
    segments,
    positions,
    buckets,
    modulator,
    modulator_bias,
    projector,
    projector_bias,
    position_table,
    output_weight,
    output_bias,
    up_weight,
    up_bias,
    down_weight,
    down_bias,
    cotangent,
):
    heads, bucket_count = position_table.shape
    image_tokens = buckets.shape[0]
    rows, model_width = tokens.shape[1], tokens.shape[2]
    images = condition.shape[1]
    shard = modulator.shape[0]
    feed_width = up_weight.shape[1]
    dp_index = lax.axis_index("dp")
    stream_index = lax.axis_index("stream")
    low = jnp.bfloat16
    full = jnp.float32

    def gather(part):
        return lax.all_gather(part, "dp", axis=0, tiled=True)

    inputs = tokens[0].astype(full)
    slot_ids, places = segments[0], positions[0]
    silu_value, silu_back = jax.vjp(jax.nn.silu, condition[0].astype(full))
    activated = silu_value.astype(low)
    activated_both = lax.all_gather(activated, ("stream", "dp"), axis=0, tiled=True)
    slots = activated_both.shape[0]
    activated_own = lax.dynamic_slice(activated_both, (0, dp_index * shard), (slots, shard))
    stream_slots = slots // 2
    partial = jnp.dot(
        lax.dynamic_slice(activated_own, (stream_index * stream_slots, 0), (stream_slots, shard)),
        modulator,
        preferred_element_type=full,
    )
    bias_parts = (modulator_bias, projector_bias, output_bias, up_bias, down_bias)
    bias_all = lax.all_gather(jnp.concatenate(bias_parts), "dp", axis=0)
    bias_full = []
    start = 0
    for part in bias_parts:
        bias_full.append(bias_all[:, start : start + part.shape[0]].reshape(-1).astype(full))
        start += part.shape[0]
    modulation = (
        lax.psum_scatter(partial, "dp", scatter_dimension=0, tiled=True) + bias_full[0]
    )
    projector_all = gather(projector)
    output_all = gather(output_weight)
    up_all = gather(up_weight)
    down_all = gather(down_weight)
    grid = bias_grid(position_table, buckets)
    local = slot_ids[:, None]
    per_token = jnp.where(
        local == 0, modulation[0:1], jnp.where(local == 1, modulation[1:2], modulation[2:3])
    )
    shift_attn, scale_attn, gate_attn, shift_mlp, scale_mlp, gate_mlp = jnp.split(
        per_token, 6, axis=1
    )
    normed_one, inverse_one = normalize(inputs)
    hidden_one = (normed_one * (1.0 + scale_attn) + shift_attn).astype(low)
    packed_bias = jnp.concatenate(
        [bias_full[1][:model_width], jnp.zeros((model_width,), full), bias_full[1][model_width:]]
    )
    packed = (
        jnp.dot(hidden_one, projector_all, preferred_element_type=full) + packed_bias
    ).astype(low)
    attended, placed, weights = attend_forward(packed, slot_ids, places, grid)
    branch_attn = jnp.dot(attended, output_all, preferred_element_type=full) + bias_full[2]
    middle = inputs + gate_attn * branch_attn
    normed_two, inverse_two = normalize(middle)
    hidden_two = (normed_two * (1.0 + scale_mlp) + shift_mlp).astype(low)
    up_output = jnp.dot(hidden_two, up_all, preferred_element_type=full) + bias_full[3]
    activation, gelu_back = jax.vjp(lambda v: jax.nn.gelu(v, approximate=True), up_output)
    activation_low = activation.astype(low)
    branch_mlp = jnp.dot(activation_low, down_all, preferred_element_type=full) + bias_full[4]
    result = (middle + gate_mlp * branch_mlp).astype(low)

    upstream = cotangent[0].astype(full)
    mlp_grad = (gate_mlp * upstream).astype(low)
    gate_mlp_grad = branch_mlp * upstream

    def scatter(grad):
        part = lax.psum_scatter(grad.astype(low), "dp", scatter_dimension=0, tiled=True)
        return lax.psum(part, "stream").astype(full)

    down_grad = scatter(
        jnp.einsum("tf,td->fd", activation_low, mlp_grad, preferred_element_type=full)
    )
    activation_grad = jnp.einsum("td,fd->tf", mlp_grad, down_all, preferred_element_type=full)
    up_grad_low = gelu_back(activation_grad)[0].astype(low)
    up_grad = scatter(
        jnp.einsum("td,tf->df", hidden_two, up_grad_low, preferred_element_type=full)
    )
    hidden_two_grad = jnp.einsum(
        "tf,df->td", up_grad_low, up_all, preferred_element_type=full
    )
    middle_grad = upstream + normalize_back(
        normed_two, inverse_two, hidden_two_grad * (1.0 + scale_mlp)
    )
    attn_grad = (gate_attn * middle_grad).astype(low)
    gate_attn_grad = branch_attn * middle_grad
    output_grad = scatter(
        jnp.einsum("td,te->de", attended, attn_grad, preferred_element_type=full)
    )
    attended_grad = jnp.einsum(
        "te,de->td", attn_grad, output_all, preferred_element_type=full
    ).astype(low)
    packed_grad, grid_grad = attend_backward(placed, weights, attended_grad, slot_ids, places)
    projector_grad = scatter(
        jnp.einsum("td,te->de", hidden_one, packed_grad, preferred_element_type=full)
    )
    table_grad = table_histogram(grid_grad, buckets, bucket_count)
    packed_sums = jnp.sum(packed_grad.astype(full), axis=0)
    sums = (
        table_grad.reshape(-1),
        packed_sums[:model_width],
        packed_sums[2 * model_width :],
        jnp.sum(attn_grad.astype(full), axis=0),
        jnp.sum(up_grad_low.astype(full), axis=0),
        jnp.sum(mlp_grad.astype(full), axis=0),
    )
    small = lax.psum(jnp.concatenate(sums), ("stream", "dp"))
    table_count = heads * bucket_count
    table_total = small[:table_count].reshape(heads, bucket_count)
    bias_grads = []
    start = table_count
    for part in bias_parts[1:]:
        size = part.shape[0]
        bias_grads.append(lax.dynamic_slice(small, (start + dp_index * size,), (size,)))
        start += size * (model_width // shard)
    hidden_one_grad = jnp.einsum(
        "te,de->td", packed_grad, projector_all, preferred_element_type=full
    )
    inputs_grad = middle_grad + normalize_back(
        normed_one, inverse_one, hidden_one_grad * (1.0 + scale_attn)
    )
    token_mod_grad = jnp.concatenate(
        [
            hidden_one_grad,
            hidden_one_grad * normed_one,
            gate_attn_grad,
            hidden_two_grad,
            hidden_two_grad * normed_two,
            gate_mlp_grad,
        ],
        axis=1,
    )
    modulation_grad = jnp.stack(
        [jnp.sum(jnp.where(local == slot, token_mod_grad, 0.0), axis=0) for slot in range(images)]
    ).astype(low)
    modulation_grad_both = lax.all_gather(modulation_grad, ("stream", "dp"), axis=0, tiled=True)
    modulator_grad = jnp.einsum(
        "id,ie->de", activated_own, modulation_grad_both, preferred_element_type=full
    )
    bias_width = modulator_bias.shape[0]
    modulator_bias_grad = jnp.sum(
        lax.dynamic_slice(
            modulation_grad_both, (0, dp_index * bias_width), (slots, bias_width)
        ).astype(full),
        axis=0,
    )
    activated_part = jnp.einsum(
        "ie,de->id",
        lax.dynamic_slice(
            modulation_grad_both, (stream_index * stream_slots, 0), (stream_slots, 6 * model_width)
        ),
        modulator,
        preferred_element_type=full,
    )
    activated_grad = (
        lax.all_to_all(
            activated_part.reshape(-1, images, shard), "dp", split_axis=0, concat_axis=0, tiled=True
        )
        .transpose(1, 0, 2)
        .reshape(images, model_width)
    )
    condition_grad = silu_back(activated_grad)[0]
    return (
        result[None],
        inputs_grad[None],
        condition_grad[None],
        modulator_grad,
        modulator_bias_grad,
        projector_grad,
        bias_grads[0],
        table_total,
        output_grad,
        bias_grads[1],
        up_grad,
        bias_grads[2],
        down_grad,
        bias_grads[3],
    )


def own_shards(
    tokens,
    condition,
    segments,
    positions,
    buckets,
    modulator,
    modulator_bias,
    projector,
    projector_bias,
    position_table,
    output_weight,
    output_bias,
    up_weight,
    up_bias,
    down_weight,
    down_bias,
    cotangent,
):
    heads, bucket_count = position_table.shape
    image_tokens = buckets.shape[0]
    rows, model_width = tokens.shape[1], tokens.shape[2]
    images = condition.shape[1]
    shard = modulator.shape[0]
    feed_width = up_weight.shape[1]
    dp_index = lax.axis_index("dp")
    stream_index = lax.axis_index("stream")
    low = jnp.bfloat16
    full = jnp.float32

    def gather(part):
        return lax.all_gather(part, "dp", axis=0, tiled=True)

    inputs = tokens[0].astype(full)
    slot_ids, places = segments[0], positions[0]
    silu_value, silu_back = jax.vjp(jax.nn.silu, condition[0].astype(full))
    activated = silu_value.astype(low)
    devices = model_width // shard
    bias_parts = (modulator_bias, projector_bias, output_bias, up_bias, down_bias)
    slices = jnp.pad(
        activated.astype(full).reshape(images, devices, shard).transpose(1, 0, 2),
        ((0, 0), (0, 8 - images), (0, 128 - shard)),
    )
    notes = slices
    bias_note = jnp.stack(
        [jnp.pad(part.astype(full), (0, 512 - part.shape[0])) for part in bias_parts]
    )
    bias_note = jnp.pad(bias_note, ((0, 8 - len(bias_parts)), (0, 0)))
    chips = devices // 2
    shard12 = jnp.pad(
        jnp.concatenate([projector, output_weight, feed_order(up_weight, 1, chips)], axis=1),
        ((0, 8), (0, 0)),
    )
    wide_modulator = jnp.pad(modulator, ((0, 128 - shard), (0, 0)))
    (
        full12,
        down_all,
        hidden_one,
        placed,
        weights,
        attended,
        branch_attn,
        middle,
        hidden_two,
        activation_low,
        slope,
        result,
        mlp_grad,
        inbox,
        modulation,
        gate_sums,
    ) = forward_pass(
        heads,
        notes,
        bias_note,
        wide_modulator,
        shard12,
        tokens[0],
        cotangent[0],
        slot_ids,
        slot_ids * image_tokens + places,
        position_table,
        buckets,
        down_weight,
    )
    packed_width = 3 * model_width
    projector_all = full12[:, :packed_width]
    output_all = full12[:, packed_width : 4 * model_width]
    up_all = full12[:, 4 * model_width :]
    local = slot_ids[:, None]
    per_token = jnp.where(
        local == 0, modulation[0:1], jnp.where(local == 1, modulation[1:2], modulation[2:3])
    )
    shift_attn, scale_attn, gate_attn, shift_mlp, scale_mlp, gate_mlp = jnp.split(
        per_token, 6, axis=1
    )
    normed_one, inverse_one = normalize(inputs)
    normed_two, inverse_two = normalize(middle)
    upstream = cotangent[0].astype(full)

    down_grad = jnp.einsum("tf,td->fd", activation_low, mlp_grad, preferred_element_type=full)
    activation_grad = jnp.einsum("td,fd->tf", mlp_grad, down_all, preferred_element_type=full)
    up_grad_low = (activation_grad * slope.astype(full)).astype(low)
    up_grad = jnp.einsum("td,tf->df", hidden_two, up_grad_low, preferred_element_type=full)
    hidden_two_grad = jnp.einsum(
        "tf,df->td", up_grad_low, up_all, preferred_element_type=full
    )
    middle_grad = upstream + normalize_back(
        normed_two, inverse_two, hidden_two_grad * (1.0 + scale_mlp)
    )
    attn_grad = (gate_attn * middle_grad).astype(low)
    gate_attn_grad = branch_attn * middle_grad
    output_grad = jnp.einsum("td,te->de", attended, attn_grad, preferred_element_type=full)
    attended_grad = jnp.einsum(
        "te,de->td", attn_grad, output_all, preferred_element_type=full
    ).astype(low)
    packed_grad, grid_grad = attend_backward(placed, jnp.swapaxes(weights, 0, 1), attended_grad, slot_ids, places)
    projector_grad = jnp.einsum("td,te->de", hidden_one, packed_grad, preferred_element_type=full)
    table_grad = table_histogram(grid_grad, buckets, bucket_count)
    packed_sums = jnp.sum(packed_grad.astype(full), axis=0)
    sums = (
        table_grad.reshape(-1),
        packed_sums[:model_width],
        packed_sums[2 * model_width :],
        jnp.sum(attn_grad.astype(full), axis=0),
        jnp.sum(up_grad_low.astype(full), axis=0),
        jnp.sum(mlp_grad.astype(full), axis=0),
    )
    hidden_one_grad = jnp.einsum(
        "te,de->td", packed_grad, projector_all, preferred_element_type=full
    )
    inputs_grad = middle_grad + normalize_back(
        normed_one, inverse_one, hidden_one_grad * (1.0 + scale_attn)
    )
    token_mod_grad = jnp.concatenate(
        [
            hidden_one_grad,
            hidden_one_grad * normed_one,
            gate_attn_grad,
            hidden_two_grad,
            hidden_two_grad * normed_two,
        ],
        axis=1,
    )
    modulation_grad = jnp.stack(
        [jnp.sum(jnp.where(local == slot, token_mod_grad, 0.0), axis=0) for slot in range(images)]
    )
    modulation_grad = jnp.concatenate([modulation_grad, gate_sums[:images]], axis=1).astype(low)
    mg = modulation_grad.reshape(images, 6, model_width).transpose(1, 0, 2)
    mg = mg.reshape(6 * images, model_width)
    late = 2 * images
    mg = jnp.concatenate(
        [
            jnp.pad(mg[late:], ((0, 16 - 4 * images), (0, 0))),
            jnp.pad(mg[:late], ((0, 16 - late), (0, 0))),
        ]
    )
    vector = jnp.concatenate(sums)
    vector = jnp.pad(vector, (0, 25600 - vector.shape[0])).reshape(200, 128)
    grad12 = jnp.concatenate([projector_grad, output_grad, up_grad], axis=1).astype(low)
    out12, down_grad, small, modulator_grad, modulator_sums, cond_parts = scatter_grads(
        mg, vector, inbox, wide_modulator, grad12, down_grad.astype(low)
    )
    small = small.reshape(-1)
    table_count = heads * bucket_count
    table_total = small[:table_count].reshape(heads, bucket_count)
    bias_grads = []
    start = table_count
    for part in bias_parts[1:]:
        size = part.shape[0]
        whole = small[start : start + size * devices]
        if size == 4 * shard:
            whole = feed_restore(whole, 0, chips)
        bias_grads.append(lax.dynamic_slice(whole, (dp_index * size,), (size,)))
        start += size * devices
    bias_width = modulator_bias.shape[0]
    modulator_bias_grad = lax.dynamic_slice(
        modulator_sums[0], (dp_index * bias_width,), (bias_width,)
    )
    activated_grad = (
        cond_parts[:, :images, :shard].transpose(1, 0, 2).reshape(images, model_width)
    )
    projector_grad = out12[:, :packed_width]
    output_grad = out12[:, packed_width : 4 * model_width]
    up_grad = feed_restore(out12[:, 4 * model_width :], 1, chips)
    condition_grad = silu_back(activated_grad)[0]
    return (
        result[None],
        inputs_grad[None],
        condition_grad[None],
        modulator_grad,
        modulator_bias_grad,
        projector_grad,
        bias_grads[0],
        table_total,
        output_grad,
        bias_grads[1],
        up_grad,
        bias_grads[2],
        down_grad,
        bias_grads[3],
    )


def solution(mesh):
    in_specs = (
        P("stream", "dp", None),
        P("stream", "dp", None),
        P("stream", "dp"),
        P("stream", "dp"),
        P(),
        P("dp", None),
        P("dp"),
        P("dp", None),
        P("dp"),
        P(),
        P("dp", None),
        P("dp"),
        P("dp", None),
        P("dp"),
        P("dp", None),
        P("dp"),
        P("stream", "dp", None),
    )
    out_specs = (
        P("stream", "dp", None),
        P("stream", "dp", None),
        P("stream", "dp", None),
        P("dp", None),
        P("dp"),
        P("dp", None),
        P("dp"),
        P(),
        P("dp", None),
        P("dp"),
        P("dp", None),
        P("dp"),
        P("dp", None),
        P("dp"),
    )
    own = dict(mesh.shape) == {'stream': 2, 'dp': 16}
    return jax.shard_map(own_shards if own else shards, mesh=mesh, in_specs=in_specs, out_specs=out_specs, check_vma=False)
```

```python
import functools
import math

import jax
import jax.numpy as jnp
from jax import lax
from jax.experimental import pallas as pl
from jax.experimental.pallas import tpu as pltpu
from jax.sharding import PartitionSpec as P

norm_epsilon = 1e-06
masked_score=-1000000000.0

def grid_kernel(table_ref, buckets_ref, grid_ref):
    chunks = table_ref.shape[1]
    for half in range(buckets_ref.shape[1] // 128):
        span = slice(128 * half, 128 * half + 128)
        index = buckets_ref[:, span]
        low, high = index & 127, index >> 7
        total = jnp.zeros(index.shape, jnp.float32)
        for chunk in range(chunks):
            row = jnp.broadcast_to(table_ref[0, chunk : chunk + 1], index.shape)
            found = jnp.take_along_axis(row, low, axis=1)
            total = jnp.where(high == chunk, found, total)
        grid_ref[0, :, span] = total.astype(jnp.bfloat16)

def bias_grid(table, buckets):
    heads, count = table.shape
    chunks = -(-count // 128)
    wide = jnp.pad(table.astype(jnp.float32), ((0, 0), (0, chunks * 128 - count)))
    return pl.pallas_call(
        grid_kernel,
        grid=(heads,),
        in_specs=[pl.BlockSpec((1, chunks, 128), lambda h: (h, 0, 0)),
                  pl.BlockSpec(buckets.shape, lambda h: (0, 0))],
        out_specs=pl.BlockSpec((1,) + buckets.shape, lambda h: (h, 0, 0)),
        out_shape=jax.ShapeDtypeStruct((heads,) + buckets.shape, jnp.bfloat16),
    )(wide.reshape(heads, chunks, 128), buckets)

def hist_kernel(grad_ref, buckets_ref, out_ref):
    rows, heads, width = grad_ref.shape
    chunks = out_ref.shape[0] // heads
    @pl.when(pl.program_id(0) == 0)
    def _():
        out_ref[...] = jnp.zeros_like(out_ref)
    total = out_ref[...]
    for row in range(rows):
        index = buckets_ref[row : row + 1, :]
        low, high = index & 127, index >> 7
        mask = lax.broadcasted_iota(jnp.int32, (chunks, width), 0) == high
        values = jnp.where(mask[None], grad_ref[row][:, None, :], 0.0)
        left = values.reshape(heads * chunks, width).astype(jnp.bfloat16)
        right = (lax.broadcasted_iota(jnp.int32, (128, width), 0) == low).astype(jnp.float32).astype(jnp.bfloat16)
        total += lax.dot_general(left, right, (((1,), (1,)), ((), ())), preferred_element_type=jnp.float32)
    out_ref[...] = total

def table_histogram(grad, buckets, count):
    places, heads, width = grad.shape
    chunks = -(-count // 128)
    step = 16
    out = pl.pallas_call(
        hist_kernel,
        grid=(places // step,),
        in_specs=[pl.BlockSpec((step, heads, width), lambda a: (a, 0, 0)),
                  pl.BlockSpec((step, width), lambda a: (a, 0))],
        out_specs=pl.BlockSpec((heads * chunks, 128), lambda a: (0, 0)),
        out_shape=jax.ShapeDtypeStruct((heads * chunks, 128), jnp.float32),
    )(grad, buckets)
    return out.reshape(heads, chunks * 128)[:, :count]

def head_windows(heads, head_width):
    found = []
    for head in range(heads):
        start = head * head_width
        base = start // 128 * 128
        stop = -(-(start + head_width) // 128) * 128
        found.append((base, stop - base, start - base))
    return found

def lane_mask(rows, width, offset, head_width):
    lane = lax.broadcasted_iota(jnp.int32, (rows, width), 1)
    return (lane >= offset) & (lane < offset + head_width)

def nt(left, right):
    return lax.dot_general(left, right, (((1,), (1,)), ((), ())), preferred_element_type=jnp.float32)
def tn(left, right):
    return lax.dot_general(left, right, (((0,), (0,)), ((), ())), preferred_element_type=jnp.float32)
def nn(left, right):
    return lax.dot_general(left, right, (((1,), (0,)), ((), ())), preferred_element_type=jnp.float32)

def attend_forward_kernel(heads, packed_ref, frame_row_ref, frame_column_ref, grid_ref, attended_ref, placed_ref, weights_ref, mixed_ref):
    rows, width3 = packed_ref.shape
    frames = placed_ref.shape[0]
    places = grid_ref.shape[1]
    width = width3 // 3
    head_width = width // heads
    scale = head_width ** (-0.5)
    place = (lax.broadcasted_iota(jnp.int32, (frames, rows), 0) == frame_row_ref[...]).astype(jnp.float32).astype(jnp.bfloat16)
    for part in range(3):
        span = slice(part * width, part * width + width)
        placed_ref[:, span] = nn(place, packed_ref[:, span]).astype(jnp.bfloat16)
    filled = nt(jnp.ones((8, rows), jnp.bfloat16), place)[0:1] > 0.5
    filled_f = jnp.where(filled, 0.0, masked_score)
    mixed_ref[...] = jnp.zeros_like(mixed_ref)
    for image in range(frames // places):
        span_rows = slice(image * places, image * places + places)
        offset_row = filled_f[:, span_rows]
        for head, (base, wide, offset) in enumerate(head_windows(heads, head_width)):
            mask = lane_mask(places, wide, offset, head_width)
            query = placed_ref[span_rows, base : base + wide]
            key = placed_ref[span_rows, width + base : width + base + wide]
            value = placed_ref[span_rows, 2 * width + base : 2 * width + base + wide]
            query = jnp.where(mask, query, jnp.zeros_like(query))
            scores = nt(query, key) * scale + grid_ref[head].astype(jnp.float32)
            scores = jnp.where(offset_row < 0.0, masked_score, scores)
            exponent = jnp.exp(scores - jnp.max(scores, axis=-1, keepdims=True))
            weights = (exponent / jnp.sum(exponent, axis=-1, keepdims=True)).astype(jnp.bfloat16)
            weights_ref[image, head] = weights
            mixture = nn(weights, value).astype(jnp.bfloat16)
            before = mixed_ref[span_rows, base : base + wide]
            mixed_ref[span_rows, base : base + wide] = jnp.where(mask, mixture, before)
    back = (lax.broadcasted_iota(jnp.int32, (rows, frames), 1) == frame_column_ref[...]).astype(jnp.float32).astype(jnp.bfloat16)
    attended_ref[...] = nn(back, mixed_ref[...]).astype(jnp.bfloat16)

def attend_forward(packed, slots, places, grid):
    rows = packed.shape[0]
    heads, image, _ = grid.shape
    frame = slots * image + places
    frames = 3 * image
    width = packed.shape[1] // 3
    return pl.pallas_call(
        functools.partial(attend_forward_kernel, heads),
        out_shape=(jax.ShapeDtypeStruct((rows, width), jnp.bfloat16),
                   jax.ShapeDtypeStruct((frames, 3 * width), jnp.bfloat16),
                   jax.ShapeDtypeStruct((3, heads, image, image), jnp.bfloat16)),
        scratch_shapes=[pltpu.VMEM((frames, width), jnp.bfloat16)],
        compiler_params=pltpu.CompilerParams(vmem_limit_bytes=48 * 2**20),
    )(packed, frame[None, :], frame[:, None], grid)

def attend_backward_kernel(heads, placed_ref, weights_ref, upstream_ref, frame_row_ref, frame_column_ref, packed_grad_ref, grid_grad_ref, up_ref, grad_ref, bias_ref):
    frames, width3 = placed_ref.shape
    rows = upstream_ref.shape[0]
    places = weights_ref.shape[2]
    width = width3 // 3
    head_width = width // heads
    scale = head_width ** (-0.5)
    place = (lax.broadcasted_iota(jnp.int32, (frames, rows), 0) == frame_row_ref[...]).astype(jnp.float32).astype(jnp.bfloat16)
    up_ref[...] = nn(place, upstream_ref[...]).astype(jnp.bfloat16)
    grad_ref[...] = jnp.zeros_like(grad_ref)
    for head, (base, wide, offset) in enumerate(head_windows(heads, head_width)):
        mask = lane_mask(places, wide, offset, head_width)
        for image in range(frames // places):
            span_rows = slice(image * places, image * places + places)
            spans = [slice(part * width + base, part * width + base + wide) for part in range(3)]
            query, key = [jnp.where(mask, t, jnp.zeros_like(t)) for t in (placed_ref[span_rows, spans[0]], placed_ref[span_rows, spans[1]])]
            value = placed_ref[span_rows, spans[2]]
            upstream = up_ref[span_rows, spans[0]]
            upstream = jnp.where(mask, upstream, jnp.zeros_like(upstream))
            weights = weights_ref[image, head]
            weights_f = weights.astype(jnp.float32)
            weight_grads = nt(upstream, value)
            inner = jnp.sum(weight_grads * weights_f, axis=-1, keepdims=True)
            score_grads_f = weights_f * (weight_grads - inner)
            score_grads = score_grads_f.astype(jnp.bfloat16)
            if image == 0:
                bias_ref[...] = score_grads_f
            else:
                bias_ref[...] += score_grads_f
            grad_ref[span_rows, spans[0]] += (nn(score_grads, key) * scale).astype(jnp.bfloat16)
            grad_ref[span_rows, spans[1]] += (tn(score_grads, query) * scale).astype(jnp.bfloat16)
            grad_ref[span_rows, spans[2]] += tn(weights, upstream).astype(jnp.bfloat16)
        grid_grad_ref[:, head, :] = bias_ref[...]
    back = (lax.broadcasted_iota(jnp.int32, (rows, frames), 1) == frame_column_ref[...]).astype(jnp.float32).astype(jnp.bfloat16)
    for part in range(3):
        span = slice(part * width, part * width + width)
        packed_grad_ref[:, span] = nn(back, grad_ref[:, span]).astype(jnp.bfloat16)

def attend_backward(placed, weights, upstream, slots, places):
    rows, width = upstream.shape
    _, heads, image, _ = weights.shape
    frame = slots * image + places
    frames = 3 * image
    return pl.pallas_call(
        functools.partial(attend_backward_kernel, heads),
        out_shape=(jax.ShapeDtypeStruct((rows, 3 * width), jnp.bfloat16),
                   jax.ShapeDtypeStruct((image, heads, image), jnp.float32)),
        scratch_shapes=[pltpu.VMEM((frames, width), jnp.bfloat16),
                        pltpu.VMEM((frames, 3 * width), jnp.bfloat16),
                        pltpu.VMEM((image, image), jnp.float32)],
        compiler_params=pltpu.CompilerParams(vmem_limit_bytes=56 * 2**20),
    )(placed, weights, upstream, frame[None, :], frame[:, None])

def normalize(values):
    center = values - jnp.mean(values, axis=-1, keepdims=True)
    inverse = lax.rsqrt(jnp.mean(center * center, axis=-1, keepdims=True) + norm_epsilon)
    return (center * inverse, inverse)


def normalize_back(normed, inverse, upstream):
    return inverse * (
        upstream
        - jnp.mean(upstream, axis=-1, keepdims=True)
        - normed * jnp.mean(upstream * normed, axis=-1, keepdims=True)
    )


def smooth_gelu(values):
    return jax.nn.gelu(values, approximate=True)


MESH = pl.DeviceIdType.MESH
low = jnp.bfloat16
full = jnp.float32


def nt(left, right):
    return lax.dot_general(left, right, (((1,), (1,)), ((), ())), preferred_element_type=full)


def tn(left, right):
    return lax.dot_general(left, right, (((0,), (0,)), ((), ())), preferred_element_type=full)


def nn(left, right):
    return lax.dot_general(left, right, (((1,), (0,)), ((), ())), preferred_element_type=full)


def head_windows(heads, head_width):
    found = []
    for head in range(heads):
        start = head * head_width
        base = start // 128 * 128
        stop = -(-(start + head_width) // 128) * 128
        found.append((base, stop - base, start - base))
    return found


def lane_mask(rows, width, offset, head_width):
    lane = lax.broadcasted_iota(jnp.int32, (rows, width), 1)
    return (lane >= offset) & (lane < offset + head_width)


def one_hot(shape, axis, index):
    return (lax.broadcasted_iota(jnp.int32, shape, axis) == index).astype(full).astype(low)


def normalize_rows(values):
    center = values - jnp.mean(values, axis=-1, keepdims=True)
    inverse = lax.rsqrt(jnp.mean(center * center, axis=-1, keepdims=True) + norm_epsilon)
    return center * inverse, inverse


class Place:
    def __init__(self):
        self.x = lax.axis_index("stream")
        self.d = lax.axis_index("dp")
        self.z = self.d // 4
        self.y = (self.d // 2) % 2
        self.c = self.d % 2

    def zz(self, j):
        return (self.z, self.z + 1 - 2 * (self.z % 2), self.z + 2 - 4 * (self.z // 2), 3 - self.z)[j]

    def source(self, i):
        upper = self.z // 2
        return (self.z, self.z + 1 - 2 * (self.z % 2), 2 - upper, 3 - 3 * upper)[i]

    def chip(self, j=0, yy=0):
        return self.zz(j) * 2 + (self.y if yy == 0 else 1 - self.y)

    def far(self, i, yy=0):
        return self.source(i) * 2 + (self.y if yy == 0 else 1 - self.y)

    def at(self, x=0, y=0, j=0, core=0):
        xx = self.x if x == 0 else 1 - self.x
        cc = self.c if core == 0 else 1 - self.c
        return (xx, self.chip(j, y) * 2 + cc)

    def along(self, z):
        return (self.x, z * 4 + self.y * 2 + self.c)


def gather_region(x, c, full_ref, w, chip, part):
    if w < 2:
        off, size = {"all": (0, 2304), "ad": (1024 * x, 1280), "a": (1280 * x, 1024)}[part]
        col = pl.multiple_of(4608 * w + 2304 * c + off, 128)
        return full_ref[0].at[pl.ds(pl.multiple_of(chip * 144, 16), 144), pl.ds(col, size)]
    off, size = {"all": (0, 288), "ad": (128 * x, 160), "a": (160 * x, 128)}[part]
    row = pl.multiple_of(c * 2304 + chip * 288 + off, 16)
    return full_ref[1].at[pl.ds(row, size), :]


class Gather:
    def __init__(self, place, full_ref, send, recv):
        self.p, self.full, self.send, self.recv = place, full_ref, send, recv

    def copy(self, w, out, into, region, device):
        return pltpu.make_async_remote_copy(
            src_ref=region,
            dst_ref=region,
            send_sem=self.send.at[w, out],
            recv_sem=self.recv.at[w, into],
            device_id=device,
            device_id_type=MESH,
        )

    def region(self, w, chip, part, x=0, core=0):
        p = self.p
        return gather_region(
            p.x if x == 0 else 1 - p.x, p.c if core == 0 else 1 - p.c, self.full, w, chip, part
        )

    def along(self, w, out, source, to):
        p = self.p
        return self.copy(w, out, source, self.region(w, source * 2 + p.y, "ad"), p.along(to))

    def first(self, w, step):
        p = self.p
        to = jnp.clip(p.z + step, 0, 3)
        return self.along(w, 21 if step > 0 else 22, p.z, to)

    def onward(self, w, i):
        p = self.p
        source = p.source(i)
        to = jnp.clip(jnp.where(source < p.z, p.z + 1, p.z - 1), 0, 3)
        return self.along(w, i, source, to)

    def over_y(self, w, i, recv=False):
        p = self.p
        region = self.region(w, p.far(i, 1 if recv else 0), "all" if i == 0 else "ad")
        return self.copy(w, 4 + i, 4 + i, region, p.at(y=1))

    def over_x(self, w, i, yy, recv=False):
        p = self.p
        slot = 8 + 2 * (i - 1) + yy
        region = self.region(w, p.far(i, yy), "a", x=1 if recv else 0)
        return self.copy(w, slot, slot, region, p.at(x=1))

    def over_core(self, w, i, yy, recv=False):
        p = self.p
        slot = 13 + 2 * i + yy
        region = self.region(w, p.far(i, yy), "all", core=1 if recv else 0)
        return self.copy(w, slot, slot, region, p.at(core=1))

    def start(self, w):
        self.start_z(w)
        self.over_y(w, 0).start()

    def start_z(self, w):
        p = self.p

        @pl.when(p.z < 3)
        def _():
            self.first(w, 1).start()

        @pl.when(p.z > 0)
        def _():
            self.first(w, -1).start()

    def start_y(self, w):
        self.over_y(w, 0).start()

    def inner(self):
        return (self.p.z == 1) | (self.p.z == 2)

    def on_z(self, w, i):
        p = self.p
        self.along(w, i, p.source(i), p.z).wait_recv()

        @pl.when(self.inner())
        def _():
            self.onward(w, i).start()

        self.over_y(w, i).start()
        self.over_x(w, i, 0).start()

    def on_y(self, w, i):
        self.over_y(w, i, True).wait_recv()
        if i == 0:
            self.over_core(w, 0, 1).start()
        else:
            self.over_x(w, i, 1).start()

    def on_x(self, w, i, yy):
        self.over_x(w, i, yy, True).wait_recv()
        self.over_core(w, i, yy).start()

    def on_core(self, w):
        for i in range(4):
            for yy in (0, 1):
                if (i, yy) != (0, 0):
                    self.over_core(w, i, yy, True).wait_recv()

    def finish(self, w):
        p = self.p

        @pl.when(p.z < 3)
        def _():
            self.first(w, 1).wait_send()

        @pl.when(p.z > 0)
        def _():
            self.first(w, -1).wait_send()

        @pl.when(self.inner())
        def _():
            for i in (1, 2, 3):
                self.onward(w, i).wait_send()

        for i in range(4):
            self.over_y(w, i).wait_send()
            for yy in (0, 1):
                if i > 0:
                    self.over_x(w, i, yy).wait_send()
                if (i, yy) != (0, 0):
                    self.over_core(w, i, yy).wait_send()


def select_rows(modulation_ref, slots, piece, width):
    span = slice(piece * width, piece * width + width)
    return jnp.where(
        slots == 0,
        modulation_ref[0:1, span],
        jnp.where(slots == 1, modulation_ref[1:2, span], modulation_ref[2:3, span]),
    )


def forward_kernel(
    heads,
    note_ref,
    bias_note_ref,
    mod_in,
    shard_ref,
    tokens_in,
    cotangent_in,
    slots_ref,
    frame_row_ref,
    frame_column_ref,
    table_ref,
    buckets_ref,
    down_ref,
    full12_ref,
    full3_ref,
    hidden_one_out,
    placed_out,
    weights_out,
    attended_out,
    branch_out,
    middle_out,
    hidden_two_out,
    act_out,
    slope_out,
    result_out,
    mlp_grad_out,
    inbox_ref,
    modulation_ref,
    gate_sum_ref,
    mod_ref,
    tokens_ref,
    cotangent_ref,
    sib,
    chip_rows,
    part,
    got0,
    got1,
    bias_box,
    bias_packed,
    bias_out,
    bias_up,
    bias_down,
    grid,
    hidden_one,
    placed,
    weights,
    mixed,
    attended,
    branch,
    middle,
    hidden_two,
    act,
    slope,
    total,
    small_out,
    wide,
    msend,
    mrecv,
    bsend,
    brecv,
    csem,
    csend,
    crecv,
    psend,
    precv,
    send,
    recv,
    wsem,
    osem,
    psem,
    isem,
):
    place = Place()
    x, d, c = place.x, place.d, place.c
    rows, width = tokens_ref.shape
    places = buckets_ref.shape[0]
    frames = placed.shape[0]
    head_width = width // heads
    scale = head_width ** (-0.5)
    feed = act.shape[1]
    inputs = [
        pltpu.make_async_copy(mod_in, mod_ref, isem.at[0]),
        pltpu.make_async_copy(tokens_in, tokens_ref, isem.at[1]),
        pltpu.make_async_copy(cotangent_in, cotangent_ref, isem.at[2]),
    ]
    barrier = pltpu.get_barrier_semaphore()

    def peer(t, k):
        return (x if t == 0 else 1 - x, (d + k) % 16)

    others = [(t, k) for t in (0, 1) for k in range(16) if (t, k) != (0, 0)]
    for t, k in others:
        pl.semaphore_signal(barrier, inc=1, device_id=peer(t, k), device_id_type=MESH)
    mine = full3_ref.at[pl.ds(pl.multiple_of(c * 2304 + place.chip() * 288, 16), 288), :]
    own3 = pltpu.make_async_copy(down_ref, mine, csem.at[0])
    own3.start()
    for cp in inputs:
        cp.start()
    inbox_ref[x * 16 + d] = note_ref[d]
    bias_box[d] = bias_note_ref[...]
    pl.semaphore_wait(barrier, 31)

    def remote(src, dst, s, r, device):
        return pltpu.make_async_remote_copy(
            src_ref=src, dst_ref=dst, send_sem=s, recv_sem=r, device_id=device, device_id_type=MESH
        )

    half_width = 4 * width

    def sib_copy(w):
        span = pl.ds(w * half_width, half_width)
        return remote(
            shard_ref.at[:, span], sib.at[:, span], csend.at[w], crecv.at[w], place.at(core=1)
        )

    sib_copy(0).start()

    def note(t, k, recv_side=False):
        if recv_side:
            src = (x if t == 0 else 1 - x) * 16 + (d + 16 - k) % 16
        else:
            src = x * 16 + d
        return remote(
            note_ref.at[(d + k) % 16], inbox_ref.at[src], msend.at[t, k], mrecv.at[t, k], peer(t, k)
        )

    def bias_note(k, recv_side=False):
        src = (d + 16 - k) % 16 if recv_side else d
        return remote(bias_note_ref, bias_box.at[src], bsend.at[k], brecv.at[k], peer(0, k))

    for t, k in others:
        note(t, k).start()
    sib_copy(1).start()
    down_copy = remote(down_ref, mine, csend.at[2], crecv.at[2], place.at(core=1))
    columns = 512

    def assemble(w):
        def body(i, _):
            span = pl.ds(pl.multiple_of(i * columns, columns), columns)
            own, other = shard_ref[0:72, span].astype(full), sib[0:72, span].astype(full)
            top = jnp.where(c == 0, own, other)
            bottom = jnp.where(c == 0, other, own)
            chip_rows[:, span] = jnp.concatenate([top, bottom], axis=0).astype(low)
            return 0

        sib_copy(w).wait()
        first = w * half_width // columns
        lax.fori_loop(first, first + half_width // columns, body, 0)
        to = pl.ds(pl.multiple_of(place.chip() * 144, 16), 144)
        span = pl.ds(w * half_width, half_width)
        return pltpu.make_async_copy(
            chip_rows.at[:, span], full12_ref.at[to, span], csem.at[1 + w]
        )

    g = Gather(place, (full12_ref, full3_ref), send, recv)
    own1 = assemble(0)
    own1.start()
    own1.wait()

    def bias_grid(first, last):
        def body(h, _):
            for half in range(places // 128):
                span = slice(128 * half, 128 * half + 128)
                index = buckets_ref[:, span]
                lower, upper = index & 127, index >> 7
                found = jnp.zeros(index.shape, full)
                for chunk in range(table_ref.shape[1]):
                    row = jnp.broadcast_to(table_ref[h, chunk : chunk + 1], index.shape)
                    value = jnp.take_along_axis(row, lower, axis=1)
                    found = jnp.where(upper == chunk, value, found)
                grid[h, :, span] = found.astype(low)
            return 0

        lax.fori_loop(first, last, body, 0)

    def project_condition():
        for t, k in others:
            note(t, k, True).wait_recv()
        left = inbox_ref[pl.ds(x * 16, 16)].reshape(128, 128).astype(low)
        cols = 768

        def body(i, _):
            span = pl.ds(pl.multiple_of(i * cols, cols), cols)
            out = nn(left, mod_ref[:, span])
            for chip_at in range(8):
                for core in range(2):
                    dest = (chip_at * 2 + core) * 8
                    part[core, chip_at, :, span] = out[dest : dest + 4]
            return 0

        lax.fori_loop(0, mod_ref.shape[1] // cols, body, 0)
        half().start()

    def half():
        return remote(part.at[1 - c], got0, psend.at[0], precv.at[0], place.at(core=1))

    def share_condition():
        half().wait()
        for chip_at in range(8):
            part[c, chip_at] += got0[chip_at]
        for k in range(1, 8):
            share(k).start()

    def share(k):
        dest = (place.chip() + k) % 8
        return remote(
            part.at[c, dest], got1.at[k - 1], psend.at[k], precv.at[k], (x, dest * 2 + c)
        )

    def finish_condition():
        for k in range(1, 16):
            bias_note(k, True).wait_recv()
        bias_packed[...] = jnp.zeros_like(bias_packed)
        for at in range(16):
            box = bias_box[at]
            q = 144 * at + (width if at >= 8 else 0)
            bias_packed[0:1, q : q + 144] = box[1:2, 0:144]
            bias_out[0:1, 72 * at : 72 * at + 72] = box[2:3, 0:72]
            u = (at % 2) * (feed // 2) + (at // 2) * 288
            bias_up[0:1, u : u + 288] = box[3:4, 0:288]
            bias_down[0:1, 72 * at : 72 * at + 72] = box[4:5, 0:72]
            modulation_ref[0:1, 432 * at : 432 * at + 432] = box[0:1, 0:432]
        for k in range(1, 8):
            share(k).wait_recv()
        summed = part[c, place.chip()]
        for k in range(1, 8):
            summed += got1[k - 1]
        modulation_ref[...] = summed + modulation_ref[0:1, :]

    def copy_out(n, src, dst):
        return pltpu.make_async_copy(src, dst, osem.at[n])

    outs = []

    def put(src, dst):
        cp = copy_out(len(outs), src, dst)
        cp.start()
        outs.append(cp)

    step = 64

    def row_loop(first, last, body):
        def run(i, _):
            body(pl.ds(pl.multiple_of(i * step, step), step))
            return 0

        lax.fori_loop(first // step, last // step, run, 0)

    def norm_one(first, last):
        def body(span):
            normed, _ = normalize_rows(tokens_ref[span, :].astype(full))
            slots = slots_ref[span, :]
            shift = select_rows(modulation_ref, slots, 0, width)
            grow = select_rows(modulation_ref, slots, 1, width)
            hidden_one[span, :] = (normed * (1.0 + grow) + shift).astype(low)
            gate = select_rows(modulation_ref, slots, 5, width)
            small_out[span, :] = (gate * cotangent_ref[span, :].astype(full)).astype(low)

        row_loop(first, last, body)

    loads = []

    def fetch(src):
        n = len(loads)
        cp = pltpu.make_async_copy(src, wide.at[n % 2], wsem.at[n % 2])
        cp.start()
        loads.append(cp)
        return n

    def loaded(n):
        loads[n].wait()
        return wide.at[n % 2]

    tile = 384

    def w12(at):
        return full12_ref.at[:, pl.ds(at, width)]

    def project(n, piece):
        weight = loaded(n)
        where = one_hot((frames, rows), 0, frame_row_ref[...])

        def body(i, _):
            span = pl.ds(pl.multiple_of(i * tile, 128), tile)
            to = pl.ds(pl.multiple_of(piece * width + i * tile, 128), tile)
            out = nn(hidden_one[...], weight[:, span]) + bias_packed[0:1, to]
            placed[:, to] = nn(where, out.astype(low)).astype(low)
            return 0

        lax.fori_loop(0, width // tile, body, 0)

    windows = head_windows(heads, head_width)

    def attend(first, last):
        where = one_hot((frames, rows), 0, frame_row_ref[...])
        filled = nt(jnp.ones((8, rows), low), where)[0:1] > 0.5
        for head in range(first, last):
            base, wide_at, offset = windows[head]
            mask = lane_mask(places, wide_at, offset, head_width)
            slot = head % 2
            if head >= 2:
                weight_copy(head - 2).wait()
            for image in range(frames // places):
                at = slice(image * places, image * places + places)
                spans = [
                    slice(p * width + base, p * width + base + wide_at) for p in range(3)
                ]
                query = placed[at, spans[0]]
                query = jnp.where(mask, query, jnp.zeros_like(query))
                scores = nt(query, placed[at, spans[1]]) * scale + grid[head].astype(full)
                scores = jnp.where(filled[:, at], scores, masked_score)
                exponent = jnp.exp(scores - jnp.max(scores, axis=-1, keepdims=True))
                share_of = (exponent / jnp.sum(exponent, axis=-1, keepdims=True)).astype(low)
                weights[slot, image] = share_of
                mixture = nn(share_of, placed[at, spans[2]]).astype(low)
                mixed[at, spans[0]] = jnp.where(mask, mixture, mixed[at, spans[0]])
            weight_copy(head).start()

    def weight_copy(head):
        return pltpu.make_async_copy(weights.at[head % 2], weights_out.at[head], psem.at[head % 2])

    def gather_back():
        back = one_hot((rows, frames), 1, frame_column_ref[...])
        attended[...] = nn(back, mixed[...]).astype(low)

    def out_project(n):
        weight = loaded(n)

        def body(i, _):
            span = pl.ds(pl.multiple_of(i * tile, 128), tile)
            branch[:, span] = nn(attended[...], weight[:, span]) + bias_out[0:1, span]
            return 0

        lax.fori_loop(0, width // tile, body, 0)

    def norm_two():
        def body(span):
            slots = slots_ref[span, :]
            gate = select_rows(modulation_ref, slots, 2, width)
            mid = tokens_ref[span, :].astype(full) + gate * branch[span, :]
            middle[span, :] = mid
            normed, _ = normalize_rows(mid)
            shift = select_rows(modulation_ref, slots, 3, width)
            grow = select_rows(modulation_ref, slots, 4, width)
            hidden_two[span, :] = (normed * (1.0 + grow) + shift).astype(low)

        row_loop(0, rows, body)

    root = math.sqrt(2.0 / math.pi)

    def up(n, piece):
        weight = loaded(n)

        def body(i, _):
            span = pl.ds(pl.multiple_of(i * tile, 128), tile)
            to = pl.ds(pl.multiple_of(piece * width + i * tile, 128), tile)
            v = nn(hidden_two[...], weight[:, span]) + bias_up[0:1, to]
            square = v * v
            bend = jnp.tanh(root * (v + 0.044715 * (v * square)))
            half = 0.5 * (1.0 + bend)
            act[:, to] = (v * half).astype(low)
            rise = root * (1.0 + (3.0 * 0.044715) * square)
            slope[:, to] = (half + 0.5 * v * (1.0 - bend * bend) * rise).astype(low)
            return 0

        lax.fori_loop(0, width // tile, body, 0)

    def down(n, piece):
        weight = loaded(n)

        def body(i, _):
            span = pl.ds(pl.multiple_of(i * tile, 128), tile)
            out = nn(act[:, piece * width : piece * width + width], weight[:, span])
            if piece == 0:
                total[:, span] = out + bias_down[0:1, span]
            else:
                total[:, span] += out
            return 0

        lax.fori_loop(0, width // tile, body, 0)

    def finish_rows():
        gate_sum_ref[...] = jnp.zeros_like(gate_sum_ref)

        def body(span):
            slots = slots_ref[span, :]
            gate = select_rows(modulation_ref, slots, 5, width)
            out = total[span, :]
            hidden_one[span, :] = (middle[span, :] + gate * out).astype(low)
            product = out * cotangent_ref[span, :].astype(full)
            for slot in range(3):
                gate_sum_ref[slot : slot + 1, :] += jnp.sum(
                    jnp.where(slots == slot, product, 0.0), axis=0, keepdims=True
                )

        row_loop(0, rows, body)

    g.start_z(0)
    g.start_y(0)
    own2 = assemble(1)
    own2.start()
    for k in range(1, 16):
        bias_note(k).start()
    down_copy.start()
    own3.wait()
    own2.wait()
    g.start_z(1)
    g.on_z(0, 1)
    g.on_z(1, 1)
    g.on_z(0, 2)
    g.on_y(0, 1)
    g.on_x(1, 1, 0)
    g.on_z(0, 3)
    g.start_y(1)
    inputs[0].wait()
    project_condition()
    g.start_z(2)
    g.on_x(0, 1, 1)
    g.on_x(0, 1, 0)
    share_condition()
    g.on_y(0, 2)
    bias_grid(0, 6)
    g.on_y(0, 3)
    g.on_x(0, 3, 0)
    bias_grid(6, 9)
    g.on_x(0, 2, 0)
    g.on_x(0, 2, 1)
    g.on_y(1, 1)
    g.on_z(1, 2)
    finish_condition()
    bias_grid(9, 13)
    inputs[1].wait()
    inputs[2].wait()
    norm_one(0, rows // 2)
    g.on_x(0, 3, 1)
    g.on_z(1, 3)
    bias_grid(13, heads)
    g.on_y(0, 0)
    g.on_core(0)
    norm_one(rows // 2, rows)
    put(hidden_one, hidden_one_out)
    put(small_out, mlp_grad_out)
    g.on_z(2, 1)
    g.on_y(1, 2)
    g.on_y(1, 0)
    a = fetch(w12(0))
    b = fetch(w12(width))
    project(a, 0)
    a = fetch(w12(2 * width))
    g.on_z(2, 2)
    project(b, 1)
    b = fetch(w12(3 * width))
    g.on_y(1, 3)
    g.on_x(1, 1, 1)
    g.start_y(2)
    project(a, 2)
    put(placed, placed_out)
    mixed[...] = jnp.zeros_like(mixed)
    attend(0, 3)
    g.on_z(2, 3)
    attend(3, 6)
    attend(6, 10)
    g.on_x(1, 2, 1)
    g.on_x(1, 3, 0)
    g.on_x(1, 2, 0)
    g.on_y(2, 2)
    attend(10, 13)
    g.on_x(2, 2, 0)
    attend(13, heads)
    g.on_x(2, 1, 0)
    g.on_y(2, 1)
    g.on_x(1, 3, 1)
    gather_back()
    put(attended, attended_out)
    out_project(b)
    put(branch, branch_out)
    norm_two()
    put(middle, middle_out)
    put(hidden_two, hidden_two_out)
    g.on_core(1)
    a = fetch(w12(4 * width))
    b = fetch(w12(5 * width))
    g.on_y(2, 3)
    g.on_x(2, 2, 1)
    up(a, 0)
    a = fetch(w12(6 * width))
    up(b, 1)
    b = fetch(w12(7 * width))
    g.on_x(2, 3, 0)
    g.on_y(2, 0)
    up(a, 2)
    g.on_x(2, 1, 1)
    g.on_x(2, 3, 1)
    up(b, 3)
    put(act, act_out)
    put(slope, slope_out)
    g.on_core(2)
    down_copy.wait()
    outs[0].wait()
    pieces = feed // width
    a = fetch(full3_ref.at[pl.ds(0, width), :])
    for piece in range(pieces):
        if piece + 1 < pieces:
            b = fetch(full3_ref.at[pl.ds((piece + 1) * width, width), :])
        down(a, piece)
        a = b
    finish_rows()
    put(hidden_one, result_out)
    for cp in outs[1:]:
        cp.wait()
    weight_copy(heads - 2).wait()
    weight_copy(heads - 1).wait()
    for w in range(3):
        g.finish(w)
    for t, k in others:
        note(t, k).wait_send()
    for k in range(1, 16):
        bias_note(k).wait_send()
    for k in range(1, 8):
        share(k).wait_send()


def forward_pass(heads, notes, bias_note, modulator, shard12, tokens, cotangent, slots, frame, table, buckets, down):
    rows, width = tokens.shape
    feed = 4 * width
    places = buckets.shape[0]
    frames = 3 * places
    any_, vm = pl.BlockSpec(memory_space=pl.ANY), pl.BlockSpec(memory_space=pltpu.VMEM)
    V, D, S = pltpu.VMEM, pltpu.SemaphoreType.DMA, jax.ShapeDtypeStruct
    count = table.shape[1]
    chunks = -(-count // 128)
    table = jnp.pad(table.astype(full), ((0, 0), (0, chunks * 128 - count)))
    table = table.reshape(heads, chunks, 128)
    return pl.pallas_call(
        functools.partial(forward_kernel, heads),
        out_shape=(
            S((width, 2 * feed), low),
            S((feed, width), low),
            S((rows, width), low),
            S((frames, 3 * width), low),
            S((heads, 3, places, places), low),
            S((rows, width), low),
            S((rows, width), full),
            S((rows, width), full),
            S((rows, width), low),
            S((rows, feed), low),
            S((rows, feed), low),
            S((rows, width), low),
            S((rows, width), low),
            S((32, 8, 128), full),
            S((4, 6 * width), full),
            S((8, width), full),
        ),
        in_specs=[vm, vm, any_, vm, any_, any_] + [vm] * 6,
        out_specs=(any_,) * 13 + (vm,) * 3,
        scratch_shapes=[
            V(modulator.shape, low),
            V(tokens.shape, low),
            V(tokens.shape, low),
            V(shard12.shape, low),
            V((144, shard12.shape[1]), low),
            V((2, 8, 4, 6 * width), full),
            V((8, 4, 6 * width), full),
            V((7, 4, 6 * width), full),
            V((16,) + bias_note.shape, full),
            V((1, 3 * width), full),
            V((1, width), full),
            V((1, feed), full),
            V((1, width), full),
            V((heads, places, places), low),
            V((rows, width), low),
            V((frames, 3 * width), low),
            V((2, 3, places, places), low),
            V((frames, width), low),
            V((rows, width), low),
            V((rows, width), full),
            V((rows, width), full),
            V((rows, width), low),
            V((rows, feed), low),
            V((rows, feed), low),
            V((rows, width), full),
            V((rows, width), low),
            V((2, width, width), low),
            D((2, 16)),
            D((2, 16)),
            D((16,)),
            D((16,)),
            D((3,)),
            D((3,)),
            D((3,)),
            D((8,)),
            D((8,)),
            D((3, 23)),
            D((3, 23)),
            D((2,)),
            D((16,)),
            D((2,)),
            D((3,)),
        ],
        compiler_params=pltpu.CompilerParams(
            collective_id=0, has_side_effects=True, vmem_limit_bytes=63 * 2**20
        ),
    )(notes, bias_note, modulator, shard12, tokens, cotangent, slots[:, None], frame[None, :], frame[:, None], table, buckets, down)


def aligned(value, size):
    return value if isinstance(value, int) else pl.multiple_of(value, size)


def scatter_part(x, w, part):
    unit = 768 if w < 2 else 96
    off, size = {
        "all": (0, 3),
        "ad": (x, 2),
        "a": (2 * x, 1),
        "other": (2 - 2 * x, 1),
    }[part]
    return unit * off, unit * size


class Scatter:
    def __init__(self, place, acc, over_x, over_y, over_z, ends, send, recv):
        self.p, self.sums = place, acc
        self.over_x, self.over_y, self.over_z, self.ends = over_x, over_y, over_z, ends
        self.send, self.recv = send, recv

    def acc(self, w, chip, part):
        off, size = scatter_part(self.p.x, w, part)
        if w < 2:
            rows = pl.ds(aligned(chip * 144, 16), 144)
            return self.sums[w].at[rows, pl.ds(aligned(off, 128), size)]
        return self.sums[2].at[pl.ds(aligned(chip * 288 + off, 16), size), :]

    def copy(self, w, slot, src, dst, device):
        return pltpu.make_async_remote_copy(
            src_ref=src,
            dst_ref=dst,
            send_sem=self.send.at[w, slot],
            recv_sem=self.recv.at[w, slot],
            device_id=device,
            device_id_type=MESH,
        )

    def x(self, w, j, yy):
        slot = 2 * (j - 1) + yy
        src = self.acc(w, self.p.chip(j, yy), "other")
        return self.copy(w, slot, src, self.over_x[w].at[slot], self.p.at(x=1))

    def y(self, w, j):
        if j == 0:
            return self.copy(
                w, 9, self.acc(w, self.p.chip(0, 1), "all"), self.ends[w].at[0], self.p.at(y=1)
            )
        src = self.acc(w, self.p.chip(j, 1), "ad")
        return self.copy(w, 5 + j, src, self.over_y[w].at[j - 1], self.p.at(y=1))

    def z(self, w, j):
        src = self.acc(w, self.p.chip(j, 0), "ad")
        return self.copy(w, 9 + j, src, self.over_z[w].at[j - 1], self.p.at(j=j))

    def f(self, w):
        src = self.acc(w, self.p.chip(0, 0), "all")
        return self.copy(w, 13, src, self.ends[w].at[1], self.p.at(x=1))

    def add(self, w, chip, part, land):
        dst = self.acc(w, chip, part)
        step = 48

        def body(i, _):
            span = pl.ds(aligned(i * step, 16), step)
            dst[span, :] = dst[span, :] + land[span, :]
            return 0

        lax.fori_loop(0, dst.shape[0] // step, body, 0)

    def start_x(self, w, j):
        for yy in (1, 0):
            self.x(w, j, yy).start()

    def start_y(self, w):
        self.y(w, 0).start()

    def on_x(self, w, j, yy):
        self.x(w, j, yy).wait_recv()
        self.add(w, self.p.chip(j, yy), "a", self.over_x[w].at[2 * (j - 1) + yy])
        if yy == 1:
            self.y(w, j).start()

    def on_y(self, w, j):
        self.y(w, j).wait_recv()
        if j == 0:
            self.add(w, self.p.chip(0, 0), "all", self.ends[w].at[0])
        else:
            self.add(w, self.p.chip(j, 0), "ad", self.over_y[w].at[j - 1])
            self.z(w, j).start()

    def on_z(self, w, j):
        self.z(w, j).wait_recv()
        self.add(w, self.p.chip(0, 0), "ad", self.over_z[w].at[j - 1])

    def start_f(self, w):
        self.f(w).start()

    def finish(self, w):
        for j in (1, 2, 3):
            for yy in (0, 1):
                self.x(w, j, yy).wait_send()
            self.y(w, j).wait_send()
            self.z(w, j).wait_send()
        self.y(w, 0).wait_send()


def backward_kernel(
    heads,
    full12_ref,
    full3_ref,
    hidden_one_in,
    placed_in,
    weights_in,
    attended_in,
    branch_in,
    middle_in,
    hidden_two_in,
    act_in,
    slope_in,
    mlp_grad_in,
    cotangent_in,
    tokens_in,
    mod_in,
    inbox_ref,
    modulation_ref,
    gate_sum_ref,
    slots_ref,
    frame_row_ref,
    frame_column_ref,
    buckets_ref,
    out12_ref,
    gmod_ref,
    tokens_grad_ref,
    spread_ref,
    grid_ref,
    out3_ref,
    vec_out_ref,
    gmod_sum_ref,
    cond_ref,
    acc0,
    acc1,
    acc3,
    x0,
    x1,
    x2,
    y0,
    y1,
    y2,
    z0,
    z1,
    z2,
    e0,
    e1,
    e2,
    slots3,
    turned,
    feed_ref,
    wide,
    total,
    middle,
    sib_end,
    vsum,
    vbuf,
    msum,
    mine_ref,
    cpart,
    hist,
    send,
    recv,
    ssend,
    srecv,
    lsem,
    wsem,
    vsend,
    vrecv,
    msend,
    mrecv,
    csend,
    crecv,
    fsend,
    frecv,
    psem,
    gsem,
    osem,
):
    place = Place()
    x, d, c, z = place.x, place.d, place.c, place.z
    rows, feed = feed_ref.shape
    width = total.shape[1]
    places = buckets_ref.shape[0]
    head_width = width // heads
    frames = 3 * places
    scale = head_width ** (-0.5)
    tile = 384
    barrier = pltpu.get_barrier_semaphore()
    for k in range(1, 16):
        pl.semaphore_signal(barrier, inc=1, device_id=(x, (d + k) % 16), device_id_type=MESH)
    pl.semaphore_signal(barrier, inc=1, device_id=place.at(x=1), device_id_type=MESH)

    used = []

    def local(src, dst):
        cp = pltpu.make_async_copy(src, dst, lsem.at[len(used)])
        used.append(cp)
        cp.start()
        return cp

    def remote(src, dst, s, r, device):
        return pltpu.make_async_remote_copy(
            src_ref=src, dst_ref=dst, send_sem=s, recv_sem=r, device_id=device, device_id_type=MESH
        )

    get_act = local(act_in, feed_ref)
    s = Scatter(
        place, (acc0, acc1, acc3), (x0, x1, x2), (y0, y1, y2), (z0, z1, z2), (e0, e1, e2), send, recv
    )

    sent = []

    def to_sibling(w, k, value, dst):
        n = len(sent)
        if n >= 2:
            slot_free(n % 2)
        slots3[n % 2] = value.astype(low)
        remote(slots3.at[n % 2], dst, ssend.at[n % 2], srecv.at[w, k], place.at(core=1)).start()
        sent.append(n)

    def slot_free(n):
        remote(
            slots3.at[n], slots3.at[n], ssend.at[n], ssend.at[n], place.at(core=1)
        ).wait_send()

    def from_sibling(w, k, value, dst):
        remote(slots3.at[0], dst, ssend.at[0], srecv.at[w, k], place.at(core=1)).wait_recv()
        half = dst.shape[0] // 2
        for part in (0, 1):
            span = pl.ds(part * half, half)
            dst[span, :] = (value[part * half : part * half + half] + dst[span, :].astype(full)).astype(low)

    def turn(to, src, base):
        def body(i, _):
            cols = pl.ds(aligned(base + i * 128, 128), 128)
            turned[to, pl.ds(aligned(i * 128, 128), 128), :] = src[:, cols].T
            return 0

        lax.fori_loop(0, width // 128, body, 0)

    def down_group(side, group, mlp_ref):
        core = 1 - c if side == 0 else c
        half = 1 - z // 2 if group == 0 else z // 2
        turn(group, feed_ref, core * (feed // 2) + half * width)
        for k in range(3):
            value = nn(turned[group], mlp_ref[:, k * tile : k * tile + tile])
            dst = acc3.at[pl.ds(aligned(half * width, 16), width), k * tile : k * tile + tile]
            (from_sibling if side else to_sibling)(2, 3 * group + k, value, dst)

    def column_tile(side, w, k, which):
        core = 1 - c if side == 0 else c
        off = (1536 * (1 - x), 768, 1536 * x)[k // 2] + tile * (k % 2)
        cols = pl.ds(aligned(core * (feed // 2) + off, 128), tile)
        if not which:
            left = 0
        elif isinstance(off, int):
            left = core if off >= width else 0
        else:
            left = jnp.where(off >= width, core, 0)
        value = nn(turned[left], feed_ref[:, cols])
        dst = s.sums[w].at[:, pl.ds(aligned(off, 128), tile)]
        (from_sibling if side else to_sibling)(w, k, value, dst)

    loads = []

    def load_of(n):
        which, piece = loads[n]
        span = pl.ds(piece * width, width)
        src = full3_ref.at[span, :] if which else full12_ref.at[:, span]
        return pltpu.make_async_copy(src, wide.at[n % 2], wsem.at[n % 2])

    def fetch(src):
        loads.append(src)
        load_of(len(loads) - 1).start()
        return len(loads) - 1

    def loaded(n):
        load_of(n).wait()
        return wide.at[n % 2]

    def w12(piece):
        return (0, piece)

    def w3(piece):
        return (1, piece)

    def tiles(body):
        def run(i, _):
            body(i * tile)
            return 0

        lax.fori_loop(0, width // tile, run, 0)

    def span_of(at, size=tile):
        return pl.ds(aligned(at, 128), size)

    def into_vec(row, value):
        for i in range(value.shape[1] // 128):
            vsum[row + i : row + i + 1, :] = value[:, 128 * i : 128 * i + 128]

    step = 64

    def row_loop(first, last, body):
        def run(i, _):
            body(pl.ds(aligned(i * step, step), step))
            return 0

        lax.fori_loop(first // step, last // step, run, 0)

    def piece_sums(row, slots, value):
        for slot in range(3):
            msum[row + slot : row + slot + 1, :] += jnp.sum(
                jnp.where(slots == slot, value, 0.0), axis=0, keepdims=True
            )

    def back_rows(normed, inverse, upstream):
        return inverse * (
            upstream
            - jnp.mean(upstream, axis=-1, keepdims=True)
            - normed * jnp.mean(upstream * normed, axis=-1, keepdims=True)
        )

    def feed_forward(slope_buf, branch_buf, mlp_ref, cotangent_ref, hidden_ref):
        get_mlp = local(mlp_grad_in, mlp_ref)
        a = fetch(w3(0))
        b = fetch(w3(1))
        get_slope = [local(slope_in.at[:, pl.ds(k * width, width)], slope_buf.at[k]) for k in (0, 1)]
        get_hidden = local(hidden_two_in, hidden_ref)
        get_branch = local(branch_in, branch_buf)
        get_middle = local(middle_in, middle)
        get_cotangent = local(cotangent_in, cotangent_ref)
        msum[...] = jnp.zeros_like(msum)
        msum[9:12, :] = gate_sum_ref[0:3, :]
        pl.semaphore_wait(barrier, 16)
        get_act.wait()
        get_mlp.wait()
        down_group(0, 0, mlp_ref)
        down_group(0, 1, mlp_ref)
        down_group(1, 0, mlp_ref)
        s.start_x(2, 2)
        s.start_x(2, 3)
        down_group(1, 1, mlp_ref)
        s.start_x(2, 1)
        s.start_y(2)

        def up_grad(n, piece):
            weight = loaded(n)
            get_slope[piece].wait()
            slope = slope_buf.at[piece % 2]

            def body(at):
                value = nt(mlp_ref[...], weight[span_of(at), :]) * slope[:, span_of(at)].astype(full)
                feed_ref[:, span_of(piece * width + at)] = value.astype(low)

            tiles(body)
            if piece < 2:
                get_slope.append(
                    local(slope_in.at[:, pl.ds((piece + 2) * width, width)], slope_buf.at[piece])
                )

        up_grad(a, 0)
        a = fetch(w3(2))
        s.on_x(2, 2, 1)
        up_grad(b, 1)
        b = fetch(w3(3))
        s.on_x(2, 3, 1)
        s.on_x(2, 2, 0)
        up_grad(a, 2)
        a = fetch(w12(4))
        s.on_x(2, 3, 0)
        s.on_x(2, 1, 1)
        up_grad(b, 3)
        b = fetch(w12(5))
        s.on_x(2, 1, 0)
        s.on_y(2, 0)
        s.on_y(2, 2)
        get_hidden.wait()
        turn(0, hidden_ref, 0)
        for k in range(6):
            column_tile(0, 1, k, False)
        s.on_y(2, 3)
        for k in range(6):
            column_tile(1, 1, k, False)
            if k == 1:
                for j in (2, 3, 1):
                    s.start_x(1, j)
        s.start_y(1)
        s.on_y(2, 1)

        def hidden_grad(n, piece):
            weight = loaded(n)

            def body(at):
                value = nt(feed_ref[:, piece * width : piece * width + width], weight[span_of(at), :])
                if piece == 0:
                    total[:, span_of(at)] = value
                else:
                    total[:, span_of(at)] += value

            tiles(body)

        hidden_grad(a, 0)
        a = fetch(w12(6))
        s.on_z(2, 2)
        hidden_grad(b, 1)
        b = fetch(w12(7))
        s.on_z(2, 3)
        s.on_z(2, 1)
        s.start_f(2)
        hidden_grad(a, 2)
        a = fetch(w12(3))
        s.on_x(1, 2, 1)
        hidden_grad(b, 3)
        s.on_x(1, 3, 1)
        for piece in range(feed // width):
            span = slice(piece * width, piece * width + width)
            into_vec(
                128 + 27 + 9 * piece, jnp.sum(feed_ref[:, span].astype(full), axis=0, keepdims=True)
            )
        into_vec(128 + 63, jnp.sum(mlp_ref[...].astype(full), axis=0, keepdims=True))
        get_branch.wait()
        get_middle.wait()
        get_cotangent.wait()

        def norm_two(span):
            slots = slots_ref[span, :]
            normed, inverse = normalize_rows(middle[span, :])
            grad = total[span, :]
            grow = select_rows(modulation_ref, slots, 4, width)
            mid = cotangent_ref[span, :].astype(full) + back_rows(
                normed, inverse, grad * (1.0 + grow)
            )
            middle[span, :] = mid
            gate = select_rows(modulation_ref, slots, 2, width)
            feed_ref[span, 3 * width : 4 * width] = (gate * mid).astype(low)
            piece_sums(0, slots, branch_buf[span, :] * mid)
            piece_sums(3, slots, grad)
            piece_sums(6, slots, grad * normed)

        row_loop(0, rows, norm_two)
        into_vec(
            128 + 18, jnp.sum(feed_ref[:, 3 * width :].astype(full), axis=0, keepdims=True)
        )
        return a

    windows = head_windows(heads, head_width)

    def attention(n, placed, up, weights, grid_part):
        get_placed = local(placed_in, placed)
        head_loads = {}

        def get_weights(head):
            cp = pltpu.make_async_copy(weights_in.at[head], weights.at[head % 2], psem.at[head % 2])
            cp.start()
            head_loads[head] = cp

        get_weights(0)
        get_weights(1)
        weight = loaded(n)

        def body(at):
            value = nt(feed_ref[:, 3 * width :], weight[span_of(at), :])
            where = one_hot((frames, rows), 0, frame_row_ref[...])
            up[:, span_of(at)] = nn(where, value.astype(low)).astype(low)

        tiles(body)
        s.on_x(1, 2, 0)
        s.on_x(1, 3, 0)
        get_placed.wait()

        def grid_copy(head):
            return pltpu.make_async_copy(grid_part.at[head % 2], grid_ref.at[head], gsem.at[head % 2])

        def attend(first, last):
            for head in range(first, last):
                base, wide_at, offset = windows[head]
                mask = lane_mask(places, wide_at, offset, head_width)
                slot = head % 2
                head_loads[head].wait()
                if head >= 2:
                    grid_copy(head - 2).wait()
                for image in range(frames // places):
                    at = slice(image * places, image * places + places)
                    spans = [slice(p * width + base, p * width + base + wide_at) for p in range(3)]
                    olds = [placed[at, span] for span in spans]
                    query, key = [jnp.where(mask, t, jnp.zeros_like(t)) for t in olds[:2]]
                    upstream = up[at, spans[0]]
                    upstream = jnp.where(mask, upstream, jnp.zeros_like(upstream))
                    shares = weights[slot, image]
                    shares_f = shares.astype(full)
                    share_grads = nt(upstream, olds[2])
                    inner = jnp.sum(share_grads * shares_f, axis=-1, keepdims=True)
                    score_f = shares_f * (share_grads - inner)
                    score = score_f.astype(low)
                    if image == 0:
                        grid_part[slot] = score_f
                    else:
                        grid_part[slot] += score_f
                    grads = (
                        (nn(score, key) * scale).astype(low),
                        (tn(score, query) * scale).astype(low),
                        tn(shares, upstream).astype(low),
                    )
                    for span, old, grad in zip(spans, olds, grads):
                        placed[at, span] = jnp.where(mask, grad, old)
                grid_copy(head).start()
                if head + 2 < heads:
                    get_weights(head + 2)

        attend(0, 3)
        s.on_x(1, 1, 1)
        s.on_y(1, 2)
        attend(3, 6)
        s.on_x(1, 1, 0)
        s.on_y(1, 3)
        attend(6, 9)
        s.on_y(1, 0)
        s.on_y(1, 1)
        attend(9, 12)
        s.on_z(1, 2)
        s.on_z(1, 3)
        attend(12, heads)
        s.on_z(1, 1)
        s.start_f(1)
        grid_copy(heads - 2).wait()
        grid_copy(heads - 1).wait()
        for piece in range(3):

            def body(at):
                back = one_hot((rows, frames), 1, frame_column_ref[...])
                span = span_of(piece * width + at)
                feed_ref[:, span] = nn(back, placed[:, span]).astype(low)

            tiles(body)

    def projection(tokens_ref, hidden_ref, attended_ref):
        get_hidden = local(hidden_one_in, hidden_ref)
        get_attended = local(attended_in, attended_ref)
        get_tokens = local(tokens_in, tokens_ref)
        a = fetch(w12(0))
        b = fetch(w12(1))
        get_hidden.wait()
        turn(0, hidden_ref, 0)
        get_attended.wait()
        turn(1, attended_ref, 0)
        for k in range(6):
            column_tile(0, 0, k, True)
        for k in range(6):
            column_tile(1, 0, k, True)
            if k == 1:
                for j in (2, 3, 1):
                    s.start_x(0, j)
        s.start_y(0)

        def hidden_grad(n, piece):
            weight = loaded(n)

            def body(at):
                value = nt(feed_ref[:, piece * width : piece * width + width], weight[span_of(at), :])
                if piece == 0:
                    total[:, span_of(at)] = value
                else:
                    total[:, span_of(at)] += value

            tiles(body)

        hidden_grad(a, 0)
        a = fetch(w12(2))
        s.on_x(0, 2, 1)
        hidden_grad(b, 1)
        s.on_x(0, 3, 1)
        hidden_grad(a, 2)
        s.on_x(0, 1, 1)
        for i, piece in ((0, 0), (1, 2)):
            span = slice(piece * width, piece * width + width)
            into_vec(128 + 9 * i, jnp.sum(feed_ref[:, span].astype(full), axis=0, keepdims=True))
        get_tokens.wait()

        def norm_one(span):
            slots = slots_ref[span, :]
            normed, inverse = normalize_rows(tokens_ref[span, :].astype(full))
            grad = total[span, :]
            grow = select_rows(modulation_ref, slots, 1, width)
            middle[span, :] += back_rows(normed, inverse, grad * (1.0 + grow))
            piece_sums(16, slots, grad)
            piece_sums(19, slots, grad * normed)

        row_loop(0, rows, norm_one)

    def row_of(xx, chip, cc):
        return (x if xx == 0 else 1 - x) * 16 + chip * 2 + (c if cc == 0 else 1 - c)

    def spread(slot, row, device, src=None):
        return remote(
            spread_ref.at[row] if src is None else src,
            spread_ref.at[row],
            msend.at[slot],
            mrecv.at[slot],
            device,
        )

    def first(slot, device):
        return spread(slot, row_of(0, place.chip(), 0), device, mine_ref)

    def mz(j, r=False):
        if not r:
            return first(j, place.at(j=j))
        return spread(j, row_of(0, place.chip(j), 0), place.at(j=j))

    def my(j, r=False):
        if j == 0 and not r:
            return first(4, place.at(y=1))
        return spread(4 + j, row_of(0, place.chip(j, 1 if r else 0), 0), place.at(y=1))

    def mx(j, yy, r=False):
        if j == 0 and yy == 0 and not r:
            return first(8, place.at(x=1))
        row = row_of(1 if r else 0, place.chip(j, yy), 0)
        return spread(8 + 2 * j + yy, row, place.at(x=1))

    def ms(xx, j, yy, r=False):
        slot = 16 + xx * 8 + 2 * j + yy
        if xx == 0 and j == 0 and yy == 0 and not r:
            return first(slot, place.at(core=1))
        return spread(slot, row_of(xx, place.chip(j, yy), 1 if r else 0), place.at(core=1))

    def vcopy(n):
        if n < 3:
            device = (place.at(core=1), place.at(x=1), place.at(y=1))[n]
            return remote(vsum, vbuf.at[n], vsend.at[n], vrecv.at[n], device)
        return remote(vsum, vbuf.at[3 + z], vsend.at[n], vrecv.at[n], place.at(j=n - 2))

    def varrive(j):
        remote(
            vsum, vbuf.at[3 + place.zz(j)], vsend.at[2 + j], vrecv.at[2 + j], place.at(j=j)
        ).wait_recv()

    def histogram(box):
        span = box.shape[2]
        parts = places // span

        def get(n):
            return pltpu.make_async_copy(
                grid_ref.at[:, pl.ds(n * span, span), :], box.at[n % 2], gsem.at[n % 2]
            )

        get(0).start()
        hist[...] = jnp.zeros_like(hist)
        for n in range(parts):
            if n + 1 < parts:
                get(n + 1).start()
            get(n).wait()

            def body(a8, _):
                base = aligned(a8 * 8, 8)
                index8 = buckets_ref[pl.ds(aligned(n * span + base, 8), 8), :]
                values8 = box[n % 2, :, pl.ds(base, 8), :]
                out = hist[...]
                for a in range(8):
                    index = index8[a : a + 1, :]
                    lower, upper = index & 127, index >> 7
                    mask = lax.broadcasted_iota(jnp.int32, (8, places), 0) == upper
                    values = jnp.where(mask[None], values8[:, a : a + 1, :], 0.0)
                    left = values.reshape(heads * 8, places).astype(low)
                    right = one_hot((128, places), 0, lower)
                    out += nt(left, right)
                hist[...] = out
                return 0

            lax.fori_loop(0, span // 8, body, 0)

    def modulator_grads(pieces_ref, mod_ref):
        get_pieces = local(spread_ref, pieces_ref)
        get_mod = local(mod_in, mod_ref)

        def place_rows(p, devices):
            base = 3 * (p - 2) if p >= 2 else 3 * p
            shape = (devices * 16, devices * 8)
            r = lax.broadcasted_iota(jnp.int32, shape, 0)
            q = lax.broadcasted_iota(jnp.int32, shape, 1)
            same = (r // 16 == q // 8) & (r % 16 - base == q % 8) & (q % 8 < 3)
            return same.astype(full).astype(low)

        activated = inbox_ref[...].reshape(256, 128).astype(low)
        get_pieces.wait()
        get_mod.wait()
        cond_total = jnp.zeros((128, 128), full)
        puts = []
        for p in range(6):
            half = 0 if p >= 2 else 16
            span = slice(width * p, width * p + width)
            pieces = pieces_ref[:, half : half + 16, :].reshape(512, width)
            where = place_rows(p, 32)
            left = nn(where, activated).astype(low)
            total[72 * p : 72 * p + 72, :] = tn(left, pieces)[0:72]
            puts.append(
                local(total.at[pl.ds(72 * p, 72), :], gmod_ref.at[:, pl.ds(width * p, width)])
            )
            ones = jnp.sum(where.astype(full), axis=1, keepdims=True).astype(low)
            gmod_sum_ref[:, span] = tn(jnp.broadcast_to(ones, (512, 128)), pieces)[0:8]
            mine = pieces_ref[pl.ds(x * 16, 16), half : half + 16, :].reshape(256, width)
            cond_rows = tn(place_rows(p, 16), mine).astype(low)
            cond_total += nt(cond_rows, mod_ref[:, span])
        cpart[...] = cond_total.reshape(16, 8, 128)
        for cp in puts:
            cp.wait()

    def ccopy(k, r=False):
        dest = (d + k) % 16
        src = (d + 16 - k) % 16
        return remote(
            cpart.at[dest], cond_ref.at[src if r else d], csend.at[k], crecv.at[k], (x, dest)
        )

    ends = []
    three = []

    def end_copy(w):
        chip = place.chip(0, 0)
        return remote(
            s.acc(w, chip, "all"), sib_end.at[w], fsend.at[w], frecv.at[w], place.at(core=1)
        )

    def final(w):
        s.f(w).wait()
        chip = place.chip(0, 0)
        if w == 2:
            rows3 = pl.ds(aligned(chip * 288, 16), 288)
            total[0:288, :] = acc3[rows3, :].astype(full) + e2[1].astype(full)
            three.append(local(total.at[pl.ds(0, 288), :], out3_ref))
        else:
            s.add(w, chip, "all", s.ends[w].at[1])
            end_copy(w).start()

    def write(w):
        end_copy(w).wait()
        own_rows = pl.ds(aligned(place.chip(0, 0) * 144, 16), 144)
        for piece in range(4):
            half, k = piece // 2, piece % 2
            span = slice(width * k, width * k + width)
            mine = s.sums[w][own_rows, span].astype(full)
            theirs = sib_end[w, :, span].astype(full)
            value = jnp.where(c == half, mine, theirs)
            value = jnp.where(c == 0, value[0:72], value[72:144])
            at = 4 * w + piece
            stage, row = (middle, 72 * at) if at < 7 else (total, 432)
            stage[row : row + 72, :] = value
            ends.append(
                local(stage.at[pl.ds(row, 72), :], out12_ref.at[:, pl.ds(width * at, width)])
            )

    V = pltpu.VMEM
    picked = []
    pl.run_scoped(
        lambda *r: picked.append(feed_forward(*r)),
        V((2, rows, width), low),
        V((rows, width), full),
        V((rows, width), low),
        V((rows, width), low),
        V((rows, width), low),
    )
    pl.run_scoped(
        functools.partial(attention, picked[0]),
        V((frames, 3 * width), low),
        V((frames, width), low),
        V((2, 3, places, places), low),
        V((2, places, places), full),
    )
    pl.run_scoped(
        projection, V((rows, width), low), V((rows, width), low), V((rows, width), low)
    )
    mine_ref[...] = msum[...].astype(low)
    put_mine = local(mine_ref, spread_ref.at[row_of(0, place.chip(), 0)])
    for j in (1, 2, 3):
        mz(j).start()
    my(0).start()
    mx(0, 0).start()
    ms(0, 0, 0).start()
    put_tokens = local(middle, tokens_grad_ref)
    s.on_x(0, 2, 0)
    s.on_x(0, 3, 0)
    s.on_y(0, 2)
    s.on_x(0, 1, 0)
    for j in (1, 2, 3):
        mz(j, True).wait_recv()
        my(j).start()
        mx(j, 0).start()
        ms(0, j, 0).start()
    s.on_y(0, 3)
    final(2)
    pl.run_scoped(histogram, V((2, heads, 32, places), full))
    vsum[0:128, :] = hist[...]
    vcopy(0).start()
    for j in range(4):
        my(j, True).wait_recv()
        mx(j, 1).start()
        ms(0, j, 1).start()
    s.on_y(0, 1)
    s.on_y(0, 0)
    vcopy(0).wait()
    vsum[...] += vbuf[0]
    vcopy(1).start()
    s.on_z(0, 2)
    s.on_z(0, 3)
    s.on_z(0, 1)
    s.start_f(0)
    final(1)
    for yy in (0, 1):
        for j in range(4):
            mx(j, yy, True).wait_recv()
            ms(1, j, yy).start()
    vcopy(1).wait()
    vsum[...] += vbuf[1]
    vcopy(2).start()
    put_mine.wait()
    put_tokens.wait()
    for xx in (0, 1):
        for yy in (0, 1):
            for j in range(4):
                ms(xx, j, yy, True).wait_recv()
    vcopy(2).wait()
    vsum[...] += vbuf[2]
    for j in (1, 2, 3):
        vcopy(2 + j).start()
    vbuf[3 + z] = vsum[...]
    three[0].wait()
    pl.run_scoped(modulator_grads, V((32, 32, width), low), V(mod_in.shape, low))
    for k in range(1, 16):
        ccopy(k).start()
    cond_ref[d] = cpart[d]
    write(1)
    for j in (1, 2, 3):
        varrive(j)
    vec_out_ref[...] = vbuf[3] + vbuf[4] + vbuf[5] + vbuf[6]
    final(0)
    write(0)
    for k in range(1, 16):
        ccopy(k, True).wait_recv()
        ccopy(k).wait_send()
    for cp in ends:
        cp.wait()
    for n in range(2):
        slot_free(n)
    for j in (1, 2, 3):
        vcopy(2 + j).wait_send()
        mz(j).wait_send()
    for j in range(4):
        my(j).wait_send()
        for yy in (0, 1):
            mx(j, yy).wait_send()
            for xx in (0, 1):
                ms(xx, j, yy).wait_send()
    for w in range(3):
        s.finish(w)


def backward_pass(heads, big, small):
    any_, vm = pl.BlockSpec(memory_space=pl.ANY), pl.BlockSpec(memory_space=pltpu.VMEM)
    V, D, S = pltpu.VMEM, pltpu.SemaphoreType.DMA, jax.ShapeDtypeStruct
    rows, width = big[2].shape
    feed = 4 * width
    places = small[-1].shape[0]
    flat = V((3, 144, 1536), low)
    tall = V((3, 192, width), low)
    return pl.pallas_call(
        functools.partial(backward_kernel, heads),
        out_shape=(
            S((72, 8 * width), full),
            S((72, 6 * width), full),
            S((rows, width), full),
            S((32, 32, width), low),
            S((heads, places, places), full),
            S((288, width), full),
            S((200, 128), full),
            S((8, 6 * width), full),
            S((16, 8, 128), full),
        ),
        in_specs=[any_] * len(big) + [vm] * len(small),
        out_specs=(any_,) * 6 + (vm,) * 3,
        scratch_shapes=[
            V((width, 2 * width), low),
            V((width, 2 * width), low),
            V((2 * width, width), low),
            V((6, 144, 768), low),
            V((6, 144, 768), low),
            V((6, 96, width), low),
            flat,
            flat,
            tall,
            flat,
            flat,
            tall,
            V((2, 144, 2 * width), low),
            V((2, 144, 2 * width), low),
            V((2, 288, width), low),
            V((2, width, 384), low),
            V((2, width, rows), low),
            V((rows, feed), low),
            V((2, width, width), low),
            V((rows, width), full),
            V((rows, width), full),
            V((2, 144, 2 * width), low),
            V((200, 128), full),
            V((7, 200, 128), full),
            V((32, width), full),
            V((32, width), low),
            V((16, 8, 128), full),
            V((128, 128), full),
            D((3, 14)),
            D((3, 14)),
            D((2,)),
            D((3, 6)),
            D((40,)),
            D((2,)),
            D((6,)),
            D((6,)),
            D((32,)),
            D((32,)),
            D((16,)),
            D((16,)),
            D((2,)),
            D((2,)),
            D((2,)),
            D((2,)),
            D((2,)),
        ],
        compiler_params=pltpu.CompilerParams(
            collective_id=1, has_side_effects=True, vmem_limit_bytes=64 * 2**20
        ),
    )(*big, *small)


def feed_order(values, axis, chips):
    shape = values.shape
    part = shape[axis] // (2 * chips)
    split = shape[:axis] + (chips, 2, part) + shape[axis + 1 :]
    return jnp.swapaxes(values.reshape(split), axis, axis + 1).reshape(shape)
def feed_restore(values, axis, chips):
    shape = values.shape
    part = shape[axis] // (2 * chips)
    split = shape[:axis] + (2, chips, part) + shape[axis + 1 :]
    return jnp.swapaxes(values.reshape(split), axis, axis + 1).reshape(shape)


def shards(
    tokens,
    condition,
    segments,
    positions,
    buckets,
    modulator,
    modulator_bias,
    projector,
    projector_bias,
    position_table,
    output_weight,
    output_bias,
    up_weight,
    up_bias,
    down_weight,
    down_bias,
    cotangent,
):
    heads, bucket_count = position_table.shape
    image_tokens = buckets.shape[0]
    rows, model_width = tokens.shape[1], tokens.shape[2]
    images = condition.shape[1]
    shard = modulator.shape[0]
    feed_width = up_weight.shape[1]
    dp_index = lax.axis_index("dp")
    stream_index = lax.axis_index("stream")
    low = jnp.bfloat16
    full = jnp.float32

    def gather(part):
        return lax.all_gather(part, "dp", axis=0, tiled=True)

    inputs = tokens[0].astype(full)
    slot_ids, places = segments[0], positions[0]
    silu_value, silu_back = jax.vjp(jax.nn.silu, condition[0].astype(full))
    activated = silu_value.astype(low)
    activated_both = lax.all_gather(activated, ("stream", "dp"), axis=0, tiled=True)
    slots = activated_both.shape[0]
    activated_own = lax.dynamic_slice(activated_both, (0, dp_index * shard), (slots, shard))
    stream_slots = slots // 2
    partial = jnp.dot(
        lax.dynamic_slice(activated_own, (stream_index * stream_slots, 0), (stream_slots, shard)),
        modulator,
        preferred_element_type=full,
    )
    bias_parts = (modulator_bias, projector_bias, output_bias, up_bias, down_bias)
    bias_all = lax.all_gather(jnp.concatenate(bias_parts), "dp", axis=0)
    bias_full = []
    start = 0
    for part in bias_parts:
        bias_full.append(bias_all[:, start : start + part.shape[0]].reshape(-1).astype(full))
        start += part.shape[0]
    modulation = (
        lax.psum_scatter(partial, "dp", scatter_dimension=0, tiled=True) + bias_full[0]
    )
    projector_all = gather(projector)
    output_all = gather(output_weight)
    up_all = gather(up_weight)
    down_all = gather(down_weight)
    grid = bias_grid(position_table, buckets)
    local = slot_ids[:, None]
    per_token = jnp.where(
        local == 0, modulation[0:1], jnp.where(local == 1, modulation[1:2], modulation[2:3])
    )
    shift_attn, scale_attn, gate_attn, shift_mlp, scale_mlp, gate_mlp = jnp.split(
        per_token, 6, axis=1
    )
    normed_one, inverse_one = normalize(inputs)
    hidden_one = (normed_one * (1.0 + scale_attn) + shift_attn).astype(low)
    packed_bias = jnp.concatenate(
        [bias_full[1][:model_width], jnp.zeros((model_width,), full), bias_full[1][model_width:]]
    )
    packed = (
        jnp.dot(hidden_one, projector_all, preferred_element_type=full) + packed_bias
    ).astype(low)
    attended, placed, weights = attend_forward(packed, slot_ids, places, grid)
    branch_attn = jnp.dot(attended, output_all, preferred_element_type=full) + bias_full[2]
    middle = inputs + gate_attn * branch_attn
    normed_two, inverse_two = normalize(middle)
    hidden_two = (normed_two * (1.0 + scale_mlp) + shift_mlp).astype(low)
    up_output = jnp.dot(hidden_two, up_all, preferred_element_type=full) + bias_full[3]
    activation, gelu_back = jax.vjp(lambda v: jax.nn.gelu(v, approximate=True), up_output)
    activation_low = activation.astype(low)
    branch_mlp = jnp.dot(activation_low, down_all, preferred_element_type=full) + bias_full[4]
    result = (middle + gate_mlp * branch_mlp).astype(low)

    upstream = cotangent[0].astype(full)
    mlp_grad = (gate_mlp * upstream).astype(low)
    gate_mlp_grad = branch_mlp * upstream

    def scatter(grad):
        part = lax.psum_scatter(grad.astype(low), "dp", scatter_dimension=0, tiled=True)
        return lax.psum(part, "stream").astype(full)

    down_grad = scatter(
        jnp.einsum("tf,td->fd", activation_low, mlp_grad, preferred_element_type=full)
    )
    activation_grad = jnp.einsum("td,fd->tf", mlp_grad, down_all, preferred_element_type=full)
    up_grad_low = gelu_back(activation_grad)[0].astype(low)
    up_grad = scatter(
        jnp.einsum("td,tf->df", hidden_two, up_grad_low, preferred_element_type=full)
    )
    hidden_two_grad = jnp.einsum(
        "tf,df->td", up_grad_low, up_all, preferred_element_type=full
    )
    middle_grad = upstream + normalize_back(
        normed_two, inverse_two, hidden_two_grad * (1.0 + scale_mlp)
    )
    attn_grad = (gate_attn * middle_grad).astype(low)
    gate_attn_grad = branch_attn * middle_grad
    output_grad = scatter(
        jnp.einsum("td,te->de", attended, attn_grad, preferred_element_type=full)
    )
    attended_grad = jnp.einsum(
        "te,de->td", attn_grad, output_all, preferred_element_type=full
    ).astype(low)
    packed_grad, grid_grad = attend_backward(placed, weights, attended_grad, slot_ids, places)
    projector_grad = scatter(
        jnp.einsum("td,te->de", hidden_one, packed_grad, preferred_element_type=full)
    )
    table_grad = table_histogram(grid_grad, buckets, bucket_count)
    packed_sums = jnp.sum(packed_grad.astype(full), axis=0)
    sums = (
        table_grad.reshape(-1),
        packed_sums[:model_width],
        packed_sums[2 * model_width :],
        jnp.sum(attn_grad.astype(full), axis=0),
        jnp.sum(up_grad_low.astype(full), axis=0),
        jnp.sum(mlp_grad.astype(full), axis=0),
    )
    small = lax.psum(jnp.concatenate(sums), ("stream", "dp"))
    table_count = heads * bucket_count
    table_total = small[:table_count].reshape(heads, bucket_count)
    bias_grads = []
    start = table_count
    for part in bias_parts[1:]:
        size = part.shape[0]
        bias_grads.append(lax.dynamic_slice(small, (start + dp_index * size,), (size,)))
        start += size * (model_width // shard)
    hidden_one_grad = jnp.einsum(
        "te,de->td", packed_grad, projector_all, preferred_element_type=full
    )
    inputs_grad = middle_grad + normalize_back(
        normed_one, inverse_one, hidden_one_grad * (1.0 + scale_attn)
    )
    token_mod_grad = jnp.concatenate(
        [
            hidden_one_grad,
            hidden_one_grad * normed_one,
            gate_attn_grad,
            hidden_two_grad,
            hidden_two_grad * normed_two,
            gate_mlp_grad,
        ],
        axis=1,
    )
    modulation_grad = jnp.stack(
        [jnp.sum(jnp.where(local == slot, token_mod_grad, 0.0), axis=0) for slot in range(images)]
    ).astype(low)
    modulation_grad_both = lax.all_gather(modulation_grad, ("stream", "dp"), axis=0, tiled=True)
    modulator_grad = jnp.einsum(
        "id,ie->de", activated_own, modulation_grad_both, preferred_element_type=full
    )
    bias_width = modulator_bias.shape[0]
    modulator_bias_grad = jnp.sum(
        lax.dynamic_slice(
            modulation_grad_both, (0, dp_index * bias_width), (slots, bias_width)
        ).astype(full),
        axis=0,
    )
    activated_part = jnp.einsum(
        "ie,de->id",
        lax.dynamic_slice(
            modulation_grad_both, (stream_index * stream_slots, 0), (stream_slots, 6 * model_width)
        ),
        modulator,
        preferred_element_type=full,
    )
    activated_grad = (
        lax.all_to_all(
            activated_part.reshape(-1, images, shard), "dp", split_axis=0, concat_axis=0, tiled=True
        )
        .transpose(1, 0, 2)
        .reshape(images, model_width)
    )
    condition_grad = silu_back(activated_grad)[0]
    return (
        result[None],
        inputs_grad[None],
        condition_grad[None],
        modulator_grad,
        modulator_bias_grad,
        projector_grad,
        bias_grads[0],
        table_total,
        output_grad,
        bias_grads[1],
        up_grad,
        bias_grads[2],
        down_grad,
        bias_grads[3],
    )


def own_shards(
    tokens,
    condition,
    segments,
    positions,
    buckets,
    modulator,
    modulator_bias,
    projector,
    projector_bias,
    position_table,
    output_weight,
    output_bias,
    up_weight,
    up_bias,
    down_weight,
    down_bias,
    cotangent,
):
    heads, bucket_count = position_table.shape
    image_tokens = buckets.shape[0]
    rows, model_width = tokens.shape[1], tokens.shape[2]
    images = condition.shape[1]
    shard = modulator.shape[0]
    feed_width = up_weight.shape[1]
    dp_index = lax.axis_index("dp")
    stream_index = lax.axis_index("stream")
    low = jnp.bfloat16
    full = jnp.float32

    def gather(part):
        return lax.all_gather(part, "dp", axis=0, tiled=True)

    inputs = tokens[0].astype(full)
    slot_ids, places = segments[0], positions[0]
    silu_value, silu_back = jax.vjp(jax.nn.silu, condition[0].astype(full))
    activated = silu_value.astype(low)
    devices = model_width // shard
    bias_parts = (modulator_bias, projector_bias, output_bias, up_bias, down_bias)
    slices = jnp.pad(
        activated.astype(full).reshape(images, devices, shard).transpose(1, 0, 2),
        ((0, 0), (0, 8 - images), (0, 128 - shard)),
    )
    notes = slices
    bias_note = jnp.stack(
        [jnp.pad(part.astype(full), (0, 512 - part.shape[0])) for part in bias_parts]
    )
    bias_note = jnp.pad(bias_note, ((0, 8 - len(bias_parts)), (0, 0)))
    chips = devices // 2
    frame = slot_ids * image_tokens + places
    shard12 = jnp.pad(
        jnp.concatenate([projector, output_weight, feed_order(up_weight, 1, chips)], axis=1),
        ((0, 8), (0, 0)),
    )
    wide_modulator = jnp.pad(modulator, ((0, 128 - shard), (0, 0)))
    (
        full12,
        down_all,
        hidden_one,
        placed,
        weights,
        attended,
        branch_attn,
        middle,
        hidden_two,
        activation_low,
        slope,
        result,
        mlp_grad,
        inbox,
        modulation,
        gate_sums,
    ) = forward_pass(
        heads,
        notes,
        bias_note,
        wide_modulator,
        shard12,
        tokens[0],
        cotangent[0],
        slot_ids,
        frame,
        position_table,
        buckets,
        down_weight,
    )
    packed_width = 3 * model_width
    (
        out12,
        modulator_grad,
        inputs_grad,
        _,
        _,
        down_grad,
        small,
        modulator_sums,
        cond_parts,
    ) = backward_pass(
        heads,
        (
            full12,
            down_all,
            hidden_one,
            placed,
            weights,
            attended,
            branch_attn,
            middle,
            hidden_two,
            activation_low,
            slope,
            mlp_grad,
            cotangent[0],
            tokens[0],
            wide_modulator,
        ),
        (
            inbox,
            modulation,
            gate_sums,
            slot_ids[:, None],
            frame[None, :],
            frame[:, None],
            buckets,
        ),
    )
    small = small.reshape(-1)
    table_count = 128 * 128
    table_total = small[:table_count].reshape(heads, -1)[:, :bucket_count]
    bias_grads = []
    start = table_count
    for part in bias_parts[1:]:
        size = part.shape[0]
        whole = small[start : start + size * devices]
        if size == 4 * shard:
            whole = feed_restore(whole, 0, chips)
        bias_grads.append(lax.dynamic_slice(whole, (dp_index * size,), (size,)))
        start += size * devices
    bias_width = modulator_bias.shape[0]
    modulator_bias_grad = lax.dynamic_slice(
        modulator_sums[0], (dp_index * bias_width,), (bias_width,)
    )
    activated_grad = (
        cond_parts[:, :images, :shard].transpose(1, 0, 2).reshape(images, model_width)
    )
    projector_grad = out12[:, :packed_width]
    output_grad = out12[:, packed_width : 4 * model_width]
    up_grad = feed_restore(out12[:, 4 * model_width :], 1, chips)
    condition_grad = silu_back(activated_grad)[0]
    return (
        result[None],
        inputs_grad[None],
        condition_grad[None],
        modulator_grad,
        modulator_bias_grad,
        projector_grad,
        bias_grads[0],
        table_total,
        output_grad,
        bias_grads[1],
        up_grad,
        bias_grads[2],
        down_grad,
        bias_grads[3],
    )


def solution(mesh):
    in_specs = (
        P("stream", "dp", None),
        P("stream", "dp", None),
        P("stream", "dp"),
        P("stream", "dp"),
        P(),
        P("dp", None),
        P("dp"),
        P("dp", None),
        P("dp"),
        P(),
        P("dp", None),
        P("dp"),
        P("dp", None),
        P("dp"),
        P("dp", None),
        P("dp"),
        P("stream", "dp", None),
    )
    out_specs = (
        P("stream", "dp", None),
        P("stream", "dp", None),
        P("stream", "dp", None),
        P("dp", None),
        P("dp"),
        P("dp", None),
        P("dp"),
        P(),
        P("dp", None),
        P("dp"),
        P("dp", None),
        P("dp"),
        P("dp", None),
        P("dp"),
    )
    own = dict(mesh.shape) == {'stream': 2, 'dp': 16}
    return jax.shard_map(own_shards if own else shards, mesh=mesh, in_specs=in_specs, out_specs=out_specs, check_vma=False)
```

```python
import functools
import math

import jax
import jax.numpy as jnp
from jax import lax
from jax.experimental import pallas as pl
from jax.experimental.pallas import tpu as pltpu
from jax.sharding import PartitionSpec as P

norm_epsilon = 1e-06
masked_score=-1000000000.0

def grid_kernel(table_ref, buckets_ref, grid_ref):
    chunks = table_ref.shape[1]
    for half in range(buckets_ref.shape[1] // 128):
        span = slice(128 * half, 128 * half + 128)
        index = buckets_ref[:, span]
        low, high = index & 127, index >> 7
        total = jnp.zeros(index.shape, jnp.float32)
        for chunk in range(chunks):
            row = jnp.broadcast_to(table_ref[0, chunk : chunk + 1], index.shape)
            found = jnp.take_along_axis(row, low, axis=1)
            total = jnp.where(high == chunk, found, total)
        grid_ref[0, :, span] = total.astype(jnp.bfloat16)

def bias_grid(table, buckets):
    heads, count = table.shape
    chunks = -(-count // 128)
    wide = jnp.pad(table.astype(jnp.float32), ((0, 0), (0, chunks * 128 - count)))
    return pl.pallas_call(
        grid_kernel,
        grid=(heads,),
        in_specs=[pl.BlockSpec((1, chunks, 128), lambda h: (h, 0, 0)),
                  pl.BlockSpec(buckets.shape, lambda h: (0, 0))],
        out_specs=pl.BlockSpec((1,) + buckets.shape, lambda h: (h, 0, 0)),
        out_shape=jax.ShapeDtypeStruct((heads,) + buckets.shape, jnp.bfloat16),
    )(wide.reshape(heads, chunks, 128), buckets)

def hist_kernel(grad_ref, buckets_ref, out_ref):
    rows, heads, width = grad_ref.shape
    chunks = out_ref.shape[0] // heads
    @pl.when(pl.program_id(0) == 0)
    def _():
        out_ref[...] = jnp.zeros_like(out_ref)
    total = out_ref[...]
    for row in range(rows):
        index = buckets_ref[row : row + 1, :]
        low, high = index & 127, index >> 7
        mask = lax.broadcasted_iota(jnp.int32, (chunks, width), 0) == high
        values = jnp.where(mask[None], grad_ref[row][:, None, :], 0.0)
        left = values.reshape(heads * chunks, width).astype(jnp.bfloat16)
        right = (lax.broadcasted_iota(jnp.int32, (128, width), 0) == low).astype(jnp.float32).astype(jnp.bfloat16)
        total += lax.dot_general(left, right, (((1,), (1,)), ((), ())), preferred_element_type=jnp.float32)
    out_ref[...] = total

def table_histogram(grad, buckets, count):
    places, heads, width = grad.shape
    chunks = -(-count // 128)
    step = 16
    out = pl.pallas_call(
        hist_kernel,
        grid=(places // step,),
        in_specs=[pl.BlockSpec((step, heads, width), lambda a: (a, 0, 0)),
                  pl.BlockSpec((step, width), lambda a: (a, 0))],
        out_specs=pl.BlockSpec((heads * chunks, 128), lambda a: (0, 0)),
        out_shape=jax.ShapeDtypeStruct((heads * chunks, 128), jnp.float32),
    )(grad, buckets)
    return out.reshape(heads, chunks * 128)[:, :count]

def head_windows(heads, head_width):
    found = []
    for head in range(heads):
        start = head * head_width
        base = start // 128 * 128
        stop = -(-(start + head_width) // 128) * 128
        found.append((base, stop - base, start - base))
    return found

def lane_mask(rows, width, offset, head_width):
    lane = lax.broadcasted_iota(jnp.int32, (rows, width), 1)
    return (lane >= offset) & (lane < offset + head_width)

def nt(left, right):
    return lax.dot_general(left, right, (((1,), (1,)), ((), ())), preferred_element_type=jnp.float32)
def tn(left, right):
    return lax.dot_general(left, right, (((0,), (0,)), ((), ())), preferred_element_type=jnp.float32)
def nn(left, right):
    return lax.dot_general(left, right, (((1,), (0,)), ((), ())), preferred_element_type=jnp.float32)

def attend_forward_kernel(heads, packed_ref, frame_row_ref, frame_column_ref, grid_ref, attended_ref, placed_ref, weights_ref, mixed_ref):
    rows, width3 = packed_ref.shape
    frames = placed_ref.shape[0]
    places = grid_ref.shape[1]
    width = width3 // 3
    head_width = width // heads
    scale = head_width ** (-0.5)
    place = (lax.broadcasted_iota(jnp.int32, (frames, rows), 0) == frame_row_ref[...]).astype(jnp.float32).astype(jnp.bfloat16)
    for part in range(3):
        span = slice(part * width, part * width + width)
        placed_ref[:, span] = nn(place, packed_ref[:, span]).astype(jnp.bfloat16)
    filled = nt(jnp.ones((8, rows), jnp.bfloat16), place)[0:1] > 0.5
    filled_f = jnp.where(filled, 0.0, masked_score)
    mixed_ref[...] = jnp.zeros_like(mixed_ref)
    for image in range(frames // places):
        span_rows = slice(image * places, image * places + places)
        offset_row = filled_f[:, span_rows]
        for head, (base, wide, offset) in enumerate(head_windows(heads, head_width)):
            mask = lane_mask(places, wide, offset, head_width)
            query = placed_ref[span_rows, base : base + wide]
            key = placed_ref[span_rows, width + base : width + base + wide]
            value = placed_ref[span_rows, 2 * width + base : 2 * width + base + wide]
            query = jnp.where(mask, query, jnp.zeros_like(query))
            scores = nt(query, key) * scale + grid_ref[head].astype(jnp.float32)
            scores = jnp.where(offset_row < 0.0, masked_score, scores)
            exponent = jnp.exp(scores - jnp.max(scores, axis=-1, keepdims=True))
            weights = (exponent / jnp.sum(exponent, axis=-1, keepdims=True)).astype(jnp.bfloat16)
            weights_ref[image, head] = weights
            mixture = nn(weights, value).astype(jnp.bfloat16)
            before = mixed_ref[span_rows, base : base + wide]
            mixed_ref[span_rows, base : base + wide] = jnp.where(mask, mixture, before)
    back = (lax.broadcasted_iota(jnp.int32, (rows, frames), 1) == frame_column_ref[...]).astype(jnp.float32).astype(jnp.bfloat16)
    attended_ref[...] = nn(back, mixed_ref[...]).astype(jnp.bfloat16)

def attend_forward(packed, slots, places, grid):
    rows = packed.shape[0]
    heads, image, _ = grid.shape
    frame = slots * image + places
    frames = 3 * image
    width = packed.shape[1] // 3
    return pl.pallas_call(
        functools.partial(attend_forward_kernel, heads),
        out_shape=(jax.ShapeDtypeStruct((rows, width), jnp.bfloat16),
                   jax.ShapeDtypeStruct((frames, 3 * width), jnp.bfloat16),
                   jax.ShapeDtypeStruct((3, heads, image, image), jnp.bfloat16)),
        scratch_shapes=[pltpu.VMEM((frames, width), jnp.bfloat16)],
        compiler_params=pltpu.CompilerParams(vmem_limit_bytes=48 * 2**20),
    )(packed, frame[None, :], frame[:, None], grid)

def attend_backward_kernel(heads, placed_ref, weights_ref, upstream_ref, frame_row_ref, frame_column_ref, packed_grad_ref, grid_grad_ref, up_ref, grad_ref, bias_ref):
    frames, width3 = placed_ref.shape
    rows = upstream_ref.shape[0]
    places = weights_ref.shape[2]
    width = width3 // 3
    head_width = width // heads
    scale = head_width ** (-0.5)
    place = (lax.broadcasted_iota(jnp.int32, (frames, rows), 0) == frame_row_ref[...]).astype(jnp.float32).astype(jnp.bfloat16)
    up_ref[...] = nn(place, upstream_ref[...]).astype(jnp.bfloat16)
    grad_ref[...] = jnp.zeros_like(grad_ref)
    for head, (base, wide, offset) in enumerate(head_windows(heads, head_width)):
        mask = lane_mask(places, wide, offset, head_width)
        for image in range(frames // places):
            span_rows = slice(image * places, image * places + places)
            spans = [slice(part * width + base, part * width + base + wide) for part in range(3)]
            query, key = [jnp.where(mask, t, jnp.zeros_like(t)) for t in (placed_ref[span_rows, spans[0]], placed_ref[span_rows, spans[1]])]
            value = placed_ref[span_rows, spans[2]]
            upstream = up_ref[span_rows, spans[0]]
            upstream = jnp.where(mask, upstream, jnp.zeros_like(upstream))
            weights = weights_ref[image, head]
            weights_f = weights.astype(jnp.float32)
            weight_grads = nt(upstream, value)
            inner = jnp.sum(weight_grads * weights_f, axis=-1, keepdims=True)
            score_grads_f = weights_f * (weight_grads - inner)
            score_grads = score_grads_f.astype(jnp.bfloat16)
            if image == 0:
                bias_ref[...] = score_grads_f
            else:
                bias_ref[...] += score_grads_f
            grad_ref[span_rows, spans[0]] += (nn(score_grads, key) * scale).astype(jnp.bfloat16)
            grad_ref[span_rows, spans[1]] += (tn(score_grads, query) * scale).astype(jnp.bfloat16)
            grad_ref[span_rows, spans[2]] += tn(weights, upstream).astype(jnp.bfloat16)
        grid_grad_ref[:, head, :] = bias_ref[...]
    back = (lax.broadcasted_iota(jnp.int32, (rows, frames), 1) == frame_column_ref[...]).astype(jnp.float32).astype(jnp.bfloat16)
    for part in range(3):
        span = slice(part * width, part * width + width)
        packed_grad_ref[:, span] = nn(back, grad_ref[:, span]).astype(jnp.bfloat16)

def attend_backward(placed, weights, upstream, slots, places):
    rows, width = upstream.shape
    _, heads, image, _ = weights.shape
    frame = slots * image + places
    frames = 3 * image
    return pl.pallas_call(
        functools.partial(attend_backward_kernel, heads),
        out_shape=(jax.ShapeDtypeStruct((rows, 3 * width), jnp.bfloat16),
                   jax.ShapeDtypeStruct((image, heads, image), jnp.float32)),
        scratch_shapes=[pltpu.VMEM((frames, width), jnp.bfloat16),
                        pltpu.VMEM((frames, 3 * width), jnp.bfloat16),
                        pltpu.VMEM((image, image), jnp.float32)],
        compiler_params=pltpu.CompilerParams(vmem_limit_bytes=56 * 2**20),
    )(placed, weights, upstream, frame[None, :], frame[:, None])

def normalize(values):
    center = values - jnp.mean(values, axis=-1, keepdims=True)
    inverse = lax.rsqrt(jnp.mean(center * center, axis=-1, keepdims=True) + norm_epsilon)
    return (center * inverse, inverse)


def normalize_back(normed, inverse, upstream):
    return inverse * (
        upstream
        - jnp.mean(upstream, axis=-1, keepdims=True)
        - normed * jnp.mean(upstream * normed, axis=-1, keepdims=True)
    )


def smooth_gelu(values):
    return jax.nn.gelu(values, approximate=True)


MESH = pl.DeviceIdType.MESH
low = jnp.bfloat16
full = jnp.float32


def nt(left, right):
    return lax.dot_general(left, right, (((1,), (1,)), ((), ())), preferred_element_type=full)


def tn(left, right):
    return lax.dot_general(left, right, (((0,), (0,)), ((), ())), preferred_element_type=full)


def nn(left, right):
    return lax.dot_general(left, right, (((1,), (0,)), ((), ())), preferred_element_type=full)


def head_windows(heads, head_width):
    found = []
    for head in range(heads):
        start = head * head_width
        base = start // 128 * 128
        stop = -(-(start + head_width) // 128) * 128
        found.append((base, stop - base, start - base))
    return found


def lane_mask(rows, width, offset, head_width):
    lane = lax.broadcasted_iota(jnp.int32, (rows, width), 1)
    return (lane >= offset) & (lane < offset + head_width)


def one_hot(shape, axis, index):
    return (lax.broadcasted_iota(jnp.int32, shape, axis) == index).astype(full).astype(low)


def normalize_rows(values):
    center = values - jnp.mean(values, axis=-1, keepdims=True)
    inverse = lax.rsqrt(jnp.mean(center * center, axis=-1, keepdims=True) + norm_epsilon)
    return center * inverse, inverse


class Place:
    def __init__(self):
        self.x = lax.axis_index("stream")
        self.d = lax.axis_index("dp")
        self.z = self.d // 4
        self.y = (self.d // 2) % 2
        self.c = self.d % 2

    def zz(self, j):
        return (self.z, self.z + 1 - 2 * (self.z % 2), self.z + 2 - 4 * (self.z // 2), 3 - self.z)[j]

    def source(self, i):
        upper = self.z // 2
        return (self.z, self.z + 1 - 2 * (self.z % 2), 2 - upper, 3 - 3 * upper)[i]

    def chip(self, j=0, yy=0):
        return self.zz(j) * 2 + (self.y if yy == 0 else 1 - self.y)

    def far(self, i, yy=0):
        return self.source(i) * 2 + (self.y if yy == 0 else 1 - self.y)

    def at(self, x=0, y=0, j=0, core=0):
        xx = self.x if x == 0 else 1 - self.x
        cc = self.c if core == 0 else 1 - self.c
        return (xx, self.chip(j, y) * 2 + cc)

    def along(self, z):
        return (self.x, z * 4 + self.y * 2 + self.c)


def gather_region(x, c, full_ref, w, chip, part):
    if w < 2:
        off, size = {"all": (0, 2304), "ad": (1024 * x, 1280), "a": (1280 * x, 1024)}[part]
        col = pl.multiple_of(4608 * w + 2304 * c + off, 128)
        return full_ref[0].at[pl.ds(pl.multiple_of(chip * 144, 16), 144), pl.ds(col, size)]
    off, size = {"all": (0, 288), "ad": (128 * x, 160), "a": (160 * x, 128)}[part]
    row = pl.multiple_of(c * 2304 + chip * 288 + off, 16)
    return full_ref[1].at[pl.ds(row, size), :]


class Gather:
    def __init__(self, place, full_ref, send, recv):
        self.p, self.full, self.send, self.recv = place, full_ref, send, recv

    def copy(self, w, out, into, region, device):
        return pltpu.make_async_remote_copy(
            src_ref=region,
            dst_ref=region,
            send_sem=self.send.at[w, out],
            recv_sem=self.recv.at[w, into],
            device_id=device,
            device_id_type=MESH,
        )

    def region(self, w, chip, part, x=0, core=0):
        p = self.p
        return gather_region(
            p.x if x == 0 else 1 - p.x, p.c if core == 0 else 1 - p.c, self.full, w, chip, part
        )

    def along(self, w, out, source, to):
        p = self.p
        return self.copy(w, out, source, self.region(w, source * 2 + p.y, "ad"), p.along(to))

    def first(self, w, step):
        p = self.p
        to = jnp.clip(p.z + step, 0, 3)
        return self.along(w, 21 if step > 0 else 22, p.z, to)

    def onward(self, w, i):
        p = self.p
        source = p.source(i)
        to = jnp.clip(jnp.where(source < p.z, p.z + 1, p.z - 1), 0, 3)
        return self.along(w, i, source, to)

    def over_y(self, w, i, recv=False):
        p = self.p
        region = self.region(w, p.far(i, 1 if recv else 0), "all" if i == 0 else "ad")
        return self.copy(w, 4 + i, 4 + i, region, p.at(y=1))

    def over_x(self, w, i, yy, recv=False):
        p = self.p
        slot = 8 + 2 * (i - 1) + yy
        region = self.region(w, p.far(i, yy), "a", x=1 if recv else 0)
        return self.copy(w, slot, slot, region, p.at(x=1))

    def over_core(self, w, i, yy, recv=False):
        p = self.p
        slot = 13 + 2 * i + yy
        region = self.region(w, p.far(i, yy), "all", core=1 if recv else 0)
        return self.copy(w, slot, slot, region, p.at(core=1))

    def start(self, w):
        self.start_z(w)
        self.over_y(w, 0).start()

    def start_z(self, w):
        p = self.p

        @pl.when(p.z < 3)
        def _():
            self.first(w, 1).start()

        @pl.when(p.z > 0)
        def _():
            self.first(w, -1).start()

    def start_y(self, w):
        self.over_y(w, 0).start()

    def inner(self):
        return (self.p.z == 1) | (self.p.z == 2)

    def on_z(self, w, i):
        p = self.p
        self.along(w, i, p.source(i), p.z).wait_recv()

        @pl.when(self.inner())
        def _():
            self.onward(w, i).start()

        self.over_y(w, i).start()
        self.over_x(w, i, 0).start()

    def on_y(self, w, i):
        self.over_y(w, i, True).wait_recv()
        if i == 0:
            self.over_core(w, 0, 1).start()
        else:
            self.over_x(w, i, 1).start()

    def on_x(self, w, i, yy):
        self.over_x(w, i, yy, True).wait_recv()
        self.over_core(w, i, yy).start()

    def on_core(self, w):
        for i in range(4):
            for yy in (0, 1):
                if (i, yy) != (0, 0):
                    self.over_core(w, i, yy, True).wait_recv()

    def finish(self, w):
        p = self.p

        @pl.when(p.z < 3)
        def _():
            self.first(w, 1).wait_send()

        @pl.when(p.z > 0)
        def _():
            self.first(w, -1).wait_send()

        @pl.when(self.inner())
        def _():
            for i in (1, 2, 3):
                self.onward(w, i).wait_send()

        for i in range(4):
            self.over_y(w, i).wait_send()
            for yy in (0, 1):
                if i > 0:
                    self.over_x(w, i, yy).wait_send()
                if (i, yy) != (0, 0):
                    self.over_core(w, i, yy).wait_send()


def select_rows(modulation_ref, slots, piece, width):
    span = slice(piece * width, piece * width + width)
    return jnp.where(
        slots == 0,
        modulation_ref[0:1, span],
        jnp.where(slots == 1, modulation_ref[1:2, span], modulation_ref[2:3, span]),
    )


def forward_kernel(
    heads,
    condition_ref,
    mod_in,
    biases_ref,
    projector_ref,
    output_ref,
    up_ref,
    down_ref,
    tokens_in,
    cotangent_in,
    segments_ref,
    positions_ref,
    table_in,
    buckets_ref,
    full12_ref,
    full3_ref,
    placed_out,
    weights_out,
    branch_out,
    middle_out,
    slope_out,
    result_out,
    mlp_grad_out,
    turned_one_out,
    turned_mix_out,
    turned_two_out,
    down_near_out,
    down_far_out,
    inbox_ref,
    modulation_ref,
    gate_sum_ref,
    mod_ref,
    tokens_ref,
    cotangent_ref,
    note_ref,
    bias_note_ref,
    shard_ref,
    slots_col,
    frame_row_ref,
    frame_col,
    table_ref,
    sib,
    chip_rows,
    part,
    part_low,
    got0,
    got1,
    bias_box,
    bias_packed,
    bias_out,
    bias_up,
    bias_down,
    grid,
    hidden_one,
    placed,
    weights,
    mixed,
    attended,
    branch,
    middle,
    hidden_two,
    act,
    slope,
    total,
    small_out,
    wide,
    turned,
    tiles3,
    buckets_t,
    penalty,
    msend,
    mrecv,
    bsend,
    brecv,
    csem,
    csend,
    crecv,
    psend,
    precv,
    send,
    recv,
    wsem,
    osem,
    psem,
    isem,
    dsend,
    drecv,
    dsem,
    tsem,
):
    place = Place()
    x, d, c = place.x, place.d, place.c
    rows, width = tokens_ref.shape
    places = buckets_ref.shape[0]
    frames = placed.shape[0]
    head_width = width // heads
    scale = head_width ** (-0.5)
    feed = act.shape[1]
    inputs = [
        pltpu.make_async_copy(mod_in, mod_ref, isem.at[0]),
        pltpu.make_async_copy(tokens_in, tokens_ref, isem.at[1]),
        pltpu.make_async_copy(cotangent_in, cotangent_ref, isem.at[2]),
    ]
    barrier = pltpu.get_barrier_semaphore()

    def peer(t, k):
        return (x if t == 0 else 1 - x, (d + k) % 16)

    others = [(t, k) for t in (0, 1) for k in range(16) if (t, k) != (0, 0)]
    for t, k in others:
        pl.semaphore_signal(barrier, inc=1, device_id=peer(t, k), device_id_type=MESH)
    mine = full3_ref.at[pl.ds(pl.multiple_of(c * 2304 + place.chip() * 288, 16), 288), :]
    own3 = pltpu.make_async_copy(down_ref, mine, csem.at[0])
    own3.start()
    for cp in inputs:
        cp.start()
    shard = projector_ref.shape[0]
    images = condition_ref.shape[0]
    shard_ref[shard:, :] = jnp.zeros((shard_ref.shape[0] - shard, shard_ref.shape[1]), low)
    shard_ref[0:shard, 0 : 3 * width] = projector_ref[...]
    shard_ref[0:shard, 3 * width : 4 * width] = output_ref[...]
    part_width = feed // 16
    for at in range(16):
        to = 4 * width + (at % 2) * (feed // 2) + (at // 2) * part_width
        shard_ref[0:shard, to : to + part_width] = up_ref[:, at * part_width : (at + 1) * part_width]
    raw = condition_ref[...].astype(full)
    activated = (raw / (1.0 + jnp.exp(-raw))).astype(low).astype(full)
    note_ref[...] = jnp.zeros_like(note_ref)
    for at in range(16):
        note_ref[at, 0:images, 0:shard] = activated[:, at * shard : (at + 1) * shard]
    bias_note_ref[...] = jnp.zeros_like(bias_note_ref)
    biases = biases_ref[...].astype(full)
    start = 0
    for row, size in enumerate((6 * shard, 2 * shard, shard, feed // 16, shard)):
        bias_note_ref[row : row + 1, 0:size] = biases[:, start : start + size]
        start += size
    slots_row = segments_ref[...]
    frame_row_ref[...] = slots_row * places + positions_ref[...]
    inbox_ref[x * 16 + d] = note_ref[d]
    bias_box[d] = bias_note_ref[...]
    pl.semaphore_wait(barrier, 31)

    def remote(src, dst, s, r, device):
        return pltpu.make_async_remote_copy(
            src_ref=src, dst_ref=dst, send_sem=s, recv_sem=r, device_id=device, device_id_type=MESH
        )

    half_width = 4 * width

    def sib_copy(w):
        span = pl.ds(w * half_width, half_width)
        return remote(
            shard_ref.at[:, span], sib.at[:, span], csend.at[w], crecv.at[w], place.at(core=1)
        )

    sib_copy(0).start()

    def note(t, k, recv_side=False):
        if recv_side:
            src = (x if t == 0 else 1 - x) * 16 + (d + 16 - k) % 16
        else:
            src = x * 16 + d
        return remote(
            note_ref.at[(d + k) % 16], inbox_ref.at[src], msend.at[t, k], mrecv.at[t, k], peer(t, k)
        )

    def bias_note(k, recv_side=False):
        src = (d + 16 - k) % 16 if recv_side else d
        return remote(bias_note_ref, bias_box.at[src], bsend.at[k], brecv.at[k], peer(0, k))

    for t, k in others:
        note(t, k).start()
    sib_copy(1).start()
    down_copy = remote(down_ref, mine, csend.at[2], crecv.at[2], place.at(core=1))
    columns = 512

    def assemble(w):
        def body(i, _):
            span = pl.ds(pl.multiple_of(i * columns, columns), columns)
            own, other = shard_ref[0:72, span].astype(full), sib[0:72, span].astype(full)
            top = jnp.where(c == 0, own, other)
            bottom = jnp.where(c == 0, other, own)
            chip_rows[:, span] = jnp.concatenate([top, bottom], axis=0).astype(low)
            return 0

        sib_copy(w).wait()
        first = w * half_width // columns
        lax.fori_loop(first, first + half_width // columns, body, 0)
        to = pl.ds(pl.multiple_of(place.chip() * 144, 16), 144)
        span = pl.ds(w * half_width, half_width)
        return pltpu.make_async_copy(
            chip_rows.at[:, span], full12_ref.at[to, span], csem.at[1 + w]
        )

    g = Gather(place, (full12_ref, full3_ref), send, recv)
    own1 = assemble(0)
    own1.start()
    own1.wait()

    def bias_grid(first, last):
        if first == 0:
            buckets_t[...] = buckets_ref[...].T
            table_ref[...] = jnp.zeros_like(table_ref)
            entries = table_in[...].astype(full)
            for chunk in range(table_ref.shape[1]):
                stop = min(128, entries.shape[1] - 128 * chunk)
                table_ref[:, chunk, 0:stop] = entries[:, 128 * chunk : 128 * chunk + stop]
            slots_col[...] = jnp.broadcast_to(slots_row, (128, rows)).T
            frame_col[...] = jnp.broadcast_to(frame_row_ref[...], (128, rows)).T

        def body(h, _):
            for half in range(places // 128):
                span = slice(128 * half, 128 * half + 128)
                index = buckets_t[:, span]
                lower, upper = index & 127, index >> 7
                found = jnp.zeros(index.shape, full)
                for chunk in range(table_ref.shape[1]):
                    row = jnp.broadcast_to(table_ref[h, chunk : chunk + 1], index.shape)
                    value = jnp.take_along_axis(row, lower, axis=1)
                    found = jnp.where(upper == chunk, value, found)
                grid[h, :, span] = found.astype(low)
            return 0

        lax.fori_loop(first, last, body, 0)

    def project_condition():
        for t, k in others:
            note(t, k, True).wait_recv()
        left = inbox_ref[pl.ds(x * 16, 16)].reshape(128, 128)[:, 0:shard].astype(low)
        for piece in range(6):
            out = nn(left, mod_ref[:, piece * width : piece * width + width])
            for at in range(16):
                part[at % 2, at // 2, 3 * piece : 3 * piece + 3, :] = out[8 * at : 8 * at + 3]
        half().start()

    def half():
        return remote(part.at[1 - c], got0, psend.at[0], precv.at[0], place.at(core=1))

    def share_condition():
        half().wait()
        for chip_at in range(8):
            both = part[c, chip_at] + got0[chip_at]
            part[c, chip_at] = both
            part_low[chip_at, 0:24, :] = both.astype(low)
        for k in range(1, 8):
            share(k).start()

    def share(k):
        dest = (place.chip() + k) % 8
        return remote(
            part_low.at[dest], got1.at[k - 1], psend.at[k], precv.at[k], (x, dest * 2 + c)
        )

    def finish_condition():
        for k in range(1, 16):
            bias_note(k, True).wait_recv()
        bias_packed[...] = jnp.zeros_like(bias_packed)
        for at in range(16):
            box = bias_box[at]
            q = 144 * at + (width if at >= 8 else 0)
            bias_packed[0:1, q : q + 144] = box[1:2, 0:144]
            bias_out[0:1, 72 * at : 72 * at + 72] = box[2:3, 0:72]
            u = (at % 2) * (feed // 2) + (at // 2) * 288
            bias_up[0:1, u : u + 288] = box[3:4, 0:288]
            bias_down[0:1, 72 * at : 72 * at + 72] = box[4:5, 0:72]
            modulation_ref[3:4, 432 * at : 432 * at + 432] = box[0:1, 0:432]
        for k in range(1, 8):
            share(k).wait_recv()
        summed = part[c, place.chip()]
        for k in range(1, 8):
            summed += got1[k - 1, 0:24, :].astype(full)
        for piece in range(6):
            span = slice(piece * width, piece * width + width)
            modulation_ref[0:3, span] = (
                summed[3 * piece : 3 * piece + 3] + modulation_ref[3:4, span]
            )

    def copy_out(n, src, dst):
        return pltpu.make_async_copy(src, dst, osem.at[n])

    outs = []

    def put(src, dst):
        cp = copy_out(len(outs), src, dst)
        cp.start()
        outs.append(cp)

    step = 64

    def row_loop(first, last, body):
        def run(i, _):
            body(pl.ds(pl.multiple_of(i * step, step), step))
            return 0

        lax.fori_loop(first // step, last // step, run, 0)

    def norm_one(first, last):
        def body(span):
            normed, _ = normalize_rows(tokens_ref[span, :].astype(full))
            slots = slots_col[span, 0:1]
            shift = select_rows(modulation_ref, slots, 0, width)
            grow = select_rows(modulation_ref, slots, 1, width)
            hidden_one[span, :] = (normed * (1.0 + grow) + shift).astype(low)
            gate = select_rows(modulation_ref, slots, 5, width)
            small_out[span, :] = (gate * cotangent_ref[span, :].astype(full)).astype(low)

        row_loop(first, last, body)

    loads = []

    def fetch(src):
        n = len(loads)
        cp = pltpu.make_async_copy(src, wide.at[n % 2], wsem.at[n % 2])
        cp.start()
        loads.append(cp)
        return n

    def loaded(n):
        loads[n].wait()
        return wide.at[n % 2]

    tile = 384

    def w12(at):
        return full12_ref.at[:, pl.ds(at, width)]

    def project(n, piece):
        weight = loaded(n)
        where = one_hot((frames, rows), 0, frame_row_ref[...])

        def body(i, _):
            span = pl.ds(pl.multiple_of(i * tile, 128), tile)
            to = pl.ds(pl.multiple_of(piece * width + i * tile, 128), tile)
            out = nn(hidden_one[...], weight[:, span]) + bias_packed[0:1, to]
            placed[:, to] = nn(where, out.astype(low)).astype(low)
            return 0

        lax.fori_loop(0, width // tile, body, 0)

    windows = head_windows(heads, head_width)

    def attend(first, last):
        if first == 0:
            where = one_hot((frames, rows), 0, frame_row_ref[...])
            filled = jnp.sum(where.astype(full), axis=1, keepdims=True)
            penalty[...] = jnp.broadcast_to((1.0 - filled) * masked_score, penalty.shape)
        for head in range(first, last):
            base, wide_at, offset = windows[head]
            mask = lane_mask(places, wide_at, offset, head_width)
            slot = head % 2
            if head >= 2:
                weight_copy(head - 2).wait()
            for image in range(frames // places):
                at = slice(image * places, image * places + places)
                spans = [
                    slice(p * width + base, p * width + base + wide_at) for p in range(3)
                ]
                query = placed[at, spans[0]]
                query = jnp.where(mask, query, jnp.zeros_like(query))
                scores = nt(placed[at, spans[1]], query) * scale + grid[head].astype(full)
                scores = scores + penalty[at, :]
                exponent = jnp.exp(scores - jnp.max(scores, axis=0, keepdims=True))
                inverse = 1.0 / jnp.sum(exponent, axis=0, keepdims=True)
                share_of = (exponent * inverse).astype(low)
                weights[slot, image] = share_of
                mixture = tn(share_of, placed[at, spans[2]]).astype(low)
                mixed[at, spans[0]] = jnp.where(mask, mixture, mixed[at, spans[0]])
            weight_copy(head).start()

    def weight_copy(head):
        return pltpu.make_async_copy(weights.at[head % 2], weights_out.at[head], psem.at[head % 2])

    def gather_back():
        back = one_hot((rows, frames), 1, frame_col[:, 0:1])
        attended[...] = nn(back, mixed[...]).astype(low)

    def turn(src, dst, n):
        def body(i, _):
            span = pl.ds(pl.multiple_of(i * 128, 128), 128)
            turned[span, :] = src[:, span].T
            return 0

        if n > 0:
            turns[n - 1].wait()
        lax.fori_loop(0, width // 128, body, 0)
        cp = pltpu.make_async_copy(turned, dst, tsem.at[n])
        cp.start()
        turns.append(cp)

    turns = []

    def down_grad_tile(n):
        side, k = n // 6, n % 6
        core = 1 - c if side == 0 else c
        cols = pl.ds(pl.multiple_of(core * (feed // 2) + k * tile, 128), tile)
        if n >= 2:
            down_grad_copy(n - 2, True)
        tiles3[n % 2] = tn(act[:, cols], small_out[...]).astype(low)
        down_grad_copy(n, False)

    def down_grad_copy(n, done):
        side, k = n // 6, n % 6
        span = pl.ds(k * tile, tile)
        if side == 0:
            cp = remote(
                tiles3.at[n % 2], down_far_out.at[span, :], dsend.at[n % 2], drecv.at[k], place.at(core=1)
            )
            (cp.wait_send if done else cp.start)()
        else:
            cp = pltpu.make_async_copy(tiles3.at[n % 2], down_near_out.at[span, :], dsem.at[n % 2])
            (cp.wait if done else cp.start)()

    def finish_down_grad():
        down_grad_copy(10, True)
        down_grad_copy(11, True)
        for k in range(6):
            remote(
                tiles3.at[0], down_far_out.at[pl.ds(k * tile, tile), :], dsend.at[0], drecv.at[k], place.at(core=1)
            ).wait_recv()

    def out_project(n):
        weight = loaded(n)

        def body(i, _):
            span = pl.ds(pl.multiple_of(i * tile, 128), tile)
            branch[:, span] = nn(attended[...], weight[:, span]) + bias_out[0:1, span]
            return 0

        lax.fori_loop(0, width // tile, body, 0)

    def norm_two():
        def body(span):
            slots = slots_col[span, 0:1]
            gate = select_rows(modulation_ref, slots, 2, width)
            mid = tokens_ref[span, :].astype(full) + gate * branch[span, :]
            middle[span, :] = mid
            normed, _ = normalize_rows(mid)
            shift = select_rows(modulation_ref, slots, 3, width)
            grow = select_rows(modulation_ref, slots, 4, width)
            hidden_two[span, :] = (normed * (1.0 + grow) + shift).astype(low)

        row_loop(0, rows, body)

    root = math.sqrt(2.0 / math.pi)

    def up(n, piece):
        weight = loaded(n)

        def body(i, _):
            span = pl.ds(pl.multiple_of(i * tile, 128), tile)
            to = pl.ds(pl.multiple_of(piece * width + i * tile, 128), tile)
            v = nn(hidden_two[...], weight[:, span]) + bias_up[0:1, to]
            square = v * v
            bend = jnp.tanh(root * (v + 0.044715 * (v * square)))
            half = 0.5 * (1.0 + bend)
            act[:, to] = (v * half).astype(low)
            rise = root * (1.0 + (3.0 * 0.044715) * square)
            slope[:, to] = (half + 0.5 * v * (1.0 - bend * bend) * rise).astype(low)
            return 0

        lax.fori_loop(0, width // tile, body, 0)

    def down(n, piece):
        weight = loaded(n)

        def body(i, _):
            span = pl.ds(pl.multiple_of(i * tile, 128), tile)
            out = nn(act[:, piece * width : piece * width + width], weight[:, span])
            if piece == 0:
                total[:, span] = out + bias_down[0:1, span]
            else:
                total[:, span] += out
            return 0

        lax.fori_loop(0, width // tile, body, 0)

    mixed_result = hidden_one

    def finish_rows():
        gate_sum_ref[...] = jnp.zeros_like(gate_sum_ref)
        gate_sum_ref[3:4, :] = jnp.sum(small_out[...].astype(full), axis=0, keepdims=True)

        def body(span):
            slots = slots_col[span, 0:1]
            gate = select_rows(modulation_ref, slots, 5, width)
            out = total[span, :]
            mixed_result[span, :] = (middle[span, :] + gate * out).astype(low)
            product = out * cotangent_ref[span, :].astype(full)
            for slot in range(3):
                gate_sum_ref[slot : slot + 1, :] += jnp.sum(
                    jnp.where(slots == slot, product, 0.0), axis=0, keepdims=True
                )

        row_loop(0, rows, body)

    g.start_z(0)
    g.start_y(0)
    g.on_z(0, 1)
    g.on_z(0, 2)
    own2 = assemble(1)
    own2.start()
    for k in range(1, 16):
        bias_note(k).start()
    down_copy.start()
    own3.wait()
    own2.wait()
    bias_grid(0, 6)
    g.on_z(0, 3)
    g.start_z(1)
    bias_grid(6, 9)
    g.on_x(0, 1, 0)
    g.on_y(0, 0)
    inputs[0].wait()
    project_condition()
    g.on_y(0, 1)
    g.on_y(0, 2)
    share_condition()
    g.on_z(1, 1)
    bias_grid(9, 13)
    g.start_z(2)
    bias_grid(13, heads)
    g.on_y(0, 3)
    g.on_x(0, 2, 1)
    finish_condition()
    g.on_z(1, 2)
    g.on_x(0, 2, 0)
    g.on_x(0, 3, 0)
    inputs[1].wait()
    inputs[2].wait()
    norm_one(0, rows // 2)
    g.on_x(0, 1, 1)
    norm_one(rows // 2, rows)
    put(small_out, mlp_grad_out)
    turn(hidden_one, turned_one_out, 0)
    g.on_y(1, 1)
    g.on_x(0, 3, 1)
    g.on_z(1, 3)
    g.on_z(2, 1)
    g.on_core(0)
    a = fetch(w12(0))
    b = fetch(w12(width))
    project(a, 0)
    a = fetch(w12(2 * width))
    g.on_y(1, 2)
    project(b, 1)
    b = fetch(w12(3 * width))
    g.start_y(1)
    g.on_y(1, 3)
    project(a, 2)
    put(placed, placed_out)
    g.on_z(2, 3)
    mixed[...] = jnp.zeros_like(mixed)
    attend(0, 3)
    attend(3, 6)
    g.on_x(1, 2, 0)
    g.on_x(1, 1, 1)
    attend(6, 10)
    g.on_x(2, 1, 0)
    g.on_x(1, 3, 0)
    attend(10, 13)
    attend(13, heads)
    g.on_x(1, 2, 1)
    g.on_z(2, 2)
    g.on_x(1, 1, 0)
    g.on_y(1, 0)
    g.on_x(1, 3, 1)
    gather_back()
    turn(attended, turned_mix_out, 1)
    out_project(b)
    put(branch, branch_out)
    g.on_y(2, 1)
    g.on_core(1)
    g.start_y(2)
    norm_two()
    turn(hidden_two, turned_two_out, 2)
    put(middle, middle_out)
    a = fetch(w12(4 * width))
    b = fetch(w12(5 * width))
    g.on_y(2, 3)
    g.on_x(2, 3, 0)
    up(a, 0)
    a = fetch(w12(6 * width))
    up(b, 1)
    b = fetch(w12(7 * width))
    g.on_y(2, 2)
    up(a, 2)
    g.on_x(2, 2, 0)
    g.on_x(2, 1, 1)
    up(b, 3)
    put(slope, slope_out)
    g.on_x(2, 3, 1)
    for n in range(6):
        down_grad_tile(n)
    g.on_y(2, 0)
    g.on_x(2, 2, 1)
    for n in range(6, 12):
        down_grad_tile(n)
    g.on_core(2)
    down_copy.wait()
    pieces = feed // width
    a = fetch(full3_ref.at[pl.ds(0, width), :])
    for piece in range(pieces):
        if piece + 1 < pieces:
            b = fetch(full3_ref.at[pl.ds((piece + 1) * width, width), :])
        down(a, piece)
        a = b
    finish_rows()
    put(hidden_one, result_out)
    for cp in outs:
        cp.wait()
    turns[2].wait()
    finish_down_grad()
    weight_copy(heads - 2).wait()
    weight_copy(heads - 1).wait()
    for w in range(3):
        g.finish(w)
    for t, k in others:
        note(t, k).wait_send()
    for k in range(1, 16):
        bias_note(k).wait_send()
    for k in range(1, 8):
        share(k).wait_send()


def forward_pass(heads, *arrays):
    tokens, buckets = arrays[7], arrays[12]
    rows, width = tokens.shape
    feed = 4 * width
    places = buckets.shape[0]
    frames = 3 * places
    any_, vm = pl.BlockSpec(memory_space=pl.ANY), pl.BlockSpec(memory_space=pltpu.VMEM)
    V, D, S = pltpu.VMEM, pltpu.SemaphoreType.DMA, jax.ShapeDtypeStruct
    count = arrays[11].shape[1]
    padded = -(-count // 128) * 128
    shard = arrays[3].shape[0]
    return pl.pallas_call(
        functools.partial(forward_kernel, heads),
        out_shape=(
            S((width, 2 * feed), low),
            S((feed, width), low),
            S((frames, 3 * width), low),
            S((heads, 3, places, places), low),
            S((rows, width), full),
            S((rows, width), full),
            S((rows, feed), low),
            S((rows, width), low),
            S((rows, width), low),
            S((width, rows), low),
            S((width, rows), low),
            S((width, rows), low),
            S((feed // 2, width), low),
            S((feed // 2, width), low),
            S((32, 8, 128), full),
            S((4, 6 * width), full),
            S((8, width), full),
        ),
        in_specs=[any_ if i in (1, 7, 8) else vm for i in range(13)],
        out_specs=(any_,) * 14 + (vm,) * 3,
        scratch_shapes=[
            V((shard, 6 * width), low),
            V(tokens.shape, low),
            V(tokens.shape, low),
            V((16, 8, 128), full),
            V((8, 512), full),
            V((shard + 8, 2 * feed), low),
            V((rows, 128), jnp.int32),
            V((1, rows), jnp.int32),
            V((rows, 128), jnp.int32),
            V((heads, padded // 128, 128), full),
            V((shard + 8, 2 * feed), low),
            V((2 * shard, 2 * feed), low),
            V((2, 8, 24, width), full),
            V((8, 32, width), low),
            V((8, 24, width), full),
            V((7, 32, width), low),
            V((16, 8, 512), full),
            V((1, 3 * width), full),
            V((1, width), full),
            V((1, feed), full),
            V((1, width), full),
            V((heads, places, places), low),
            V((rows, width), low),
            V((frames, 3 * width), low),
            V((2, 3, places, places), low),
            V((frames, width), low),
            V((rows, width), low),
            V((rows, width), full),
            V((rows, width), full),
            V((rows, width), low),
            V((rows, feed), low),
            V((rows, feed), low),
            V((rows, width), full),
            V((rows, width), low),
            V((2, width, width), low),
            V((width, rows), low),
            V((2, 384, width), low),
            V((places, places), jnp.int32),
            V((frames, places), full),
            D((2, 16)),
            D((2, 16)),
            D((16,)),
            D((16,)),
            D((3,)),
            D((3,)),
            D((3,)),
            D((8,)),
            D((8,)),
            D((3, 23)),
            D((3, 23)),
            D((2,)),
            D((24,)),
            D((2,)),
            D((3,)),
            D((2,)),
            D((6,)),
            D((2,)),
            D((3,)),
        ],
        compiler_params=pltpu.CompilerParams(
            collective_id=0, has_side_effects=True, vmem_limit_bytes=63 * 2**20
        ),
    )(*arrays)


(
    LD,
    UG,
    D2S,
    D2A,
    D2B,
    HG,
    N2,
    DA,
    ATT,
    UP,
    T1,
    D1S,
    D1A,
    D1B,
    H,
    N1,
    MG,
    HI,
    VEC,
    MODG,
    COND,
    FINAL,
    WRITE,
    START_X,
    START_Y,
    START_E,
    START_F,
    ON_X,
    ON_Y,
    ON_Z,
) = range(30)


def aligned(value, size):
    return value if isinstance(value, int) else pl.multiple_of(value, size)


def scatter_part(x, w, part):
    unit = 768 if w < 2 else 96
    off, size = {
        "all": (0, 3),
        "ad": (x, 2),
        "a": (2 * x, 1),
        "other": (2 - 2 * x, 1),
    }[part]
    return unit * off, unit * size


class Scatter:
    def __init__(self, place, acc, over_x, over_y, over_z, ends, send, recv):
        self.p, self.sums = place, acc
        self.over_x, self.over_y, self.over_z, self.ends = over_x, over_y, over_z, ends
        self.send, self.recv = send, recv

    def acc(self, w, chip, part):
        off, size = scatter_part(self.p.x, w, part)
        if w < 2:
            rows = pl.ds(aligned(chip * 144, 16), 144)
            return self.sums[w].at[rows, pl.ds(aligned(off, 128), size)]
        return self.sums[2].at[pl.ds(aligned(chip * 288 + off, 16), size), :]

    def copy(self, w, slot, src, dst, device):
        return pltpu.make_async_remote_copy(
            src_ref=src,
            dst_ref=dst,
            send_sem=self.send.at[w, slot],
            recv_sem=self.recv.at[w, slot],
            device_id=device,
            device_id_type=MESH,
        )

    def x(self, w, j, yy):
        slot = 2 * (j - 1) + yy
        src = self.acc(w, self.p.chip(j, yy), "other")
        return self.copy(w, slot, src, self.over_x[w].at[slot], self.p.at(x=1))

    def y(self, w, j):
        if j == 0:
            return self.copy(
                w, 9, self.acc(w, self.p.chip(0, 1), "all"), self.ends[w].at[0], self.p.at(y=1)
            )
        src = self.acc(w, self.p.chip(j, 1), "ad")
        return self.copy(w, 5 + j, src, self.over_y[w].at[j - 1], self.p.at(y=1))

    def z(self, w, j):
        src = self.acc(w, self.p.chip(j, 0), "ad")
        return self.copy(w, 9 + j, src, self.over_z[w].at[j - 1], self.p.at(j=j))

    def f(self, w, part):
        src = self.acc(w, self.p.chip(0, 0), part)
        off, size = scatter_part(self.p.x, w, part)
        if w < 2:
            dst = self.ends[w].at[1, :, pl.ds(aligned(off, 128), size)]
        else:
            dst = self.ends[2].at[1, pl.ds(aligned(off, 16), size), :]
        return self.copy(w, 13 if part == "ad" else 14, src, dst, self.p.at(x=1))

    def add(self, w, chip, part, land):
        dst = self.acc(w, chip, part)
        step = 48

        def body(i, _):
            span = pl.ds(aligned(i * step, 16), step)
            dst[span, :] = dst[span, :] + land[span, :]
            return 0

        lax.fori_loop(0, dst.shape[0] // step, body, 0)

    def start_x(self, w, j):
        for yy in (1, 0):
            self.x(w, j, yy).start()

    def start_y(self, w):
        self.y(w, 0).start()

    def on_x(self, w, j, yy):
        self.x(w, j, yy).wait_recv()
        self.add(w, self.p.chip(j, yy), "a", self.over_x[w].at[2 * (j - 1) + yy])
        if yy == 1:
            self.y(w, j).start()

    def on_y(self, w, j):
        self.y(w, j).wait_recv()
        if j == 0:
            self.add(w, self.p.chip(0, 0), "all", self.ends[w].at[0])
        else:
            self.add(w, self.p.chip(j, 0), "ad", self.over_y[w].at[j - 1])
            self.z(w, j).start()

    def on_z(self, w, j):
        self.z(w, j).wait_recv()
        self.add(w, self.p.chip(0, 0), "ad", self.over_z[w].at[j - 1])

    def start_e(self, w):
        self.f(w, "other").start()

    def start_f(self, w):
        self.f(w, "ad").start()

    def finish(self, w):
        for j in (1, 2, 3):
            for yy in (0, 1):
                self.x(w, j, yy).wait_send()
            self.y(w, j).wait_send()
            self.z(w, j).wait_send()
        self.y(w, 0).wait_send()


def backward_kernel(
    heads,
    order,
    full12_ref,
    full3_ref,
    placed_in,
    weights_in,
    branch_in,
    middle_in,
    slope_in,
    mlp_grad_in,
    turned_one_in,
    turned_mix_in,
    turned_two_in,
    down_near_in,
    down_far_in,
    cotangent_in,
    tokens_in,
    mod_in,
    inbox_ref,
    modulation_ref,
    gate_sum_ref,
    segments_ref,
    positions_ref,
    buckets_ref,
    out_packed_ref,
    out_out_ref,
    out_up_ref,
    gmod_ref,
    tokens_grad_ref,
    spread_ref,
    grid_ref,
    grid_far_ref,
    out3_ref,
    vec_out_ref,
    gmod_sum_ref,
    cond_ref,
    acc0,
    acc1,
    acc3,
    x0,
    x1,
    x2,
    y0,
    y1,
    y2,
    z0,
    z1,
    z2,
    e0,
    e1,
    e2,
    slots3,
    turned,
    feed_ref,
    wide,
    total,
    middle,
    sib_end,
    vsum,
    vbuf,
    msum,
    mine_ref,
    cpart,
    hist,
    sums_row,
    buckets_t,
    slots_col,
    frame_row_ref,
    frame_col,
    send,
    recv,
    ssend,
    srecv,
    lsem,
    wsem,
    vsend,
    vrecv,
    msend,
    mrecv,
    csend,
    crecv,
    fsend,
    frecv,
    psem,
    gsem,
    hsem,
):
    place = Place()
    x, d, c, z = place.x, place.d, place.c, place.z
    rows, feed = feed_ref.shape
    width = total.shape[1]
    places = buckets_ref.shape[0]
    head_width = width // heads
    frames = 3 * places
    scale = head_width ** (-0.5)
    tile = 384
    barrier = pltpu.get_barrier_semaphore()
    for k in range(1, 16):
        pl.semaphore_signal(barrier, inc=1, device_id=(x, (d + k) % 16), device_id_type=MESH)
    pl.semaphore_signal(barrier, inc=1, device_id=place.at(x=1), device_id_type=MESH)

    def remote(src, dst, s, r, device):
        return pltpu.make_async_remote_copy(
            src_ref=src, dst_ref=dst, send_sem=s, recv_sem=r, device_id=device, device_id_type=MESH
        )

    s = Scatter(
        place, (acc0, acc1, acc3), (x0, x1, x2), (y0, y1, y2), (z0, z1, z2), (e0, e1, e2), send, recv
    )
    box = {}

    def local(n, src, dst):
        return pltpu.make_async_copy(src, dst, lsem.at[n])

    sent = []

    def slot_for(w, k, dst, side):
        if side:
            remote(slots3.at[0], dst, ssend.at[0], srecv.at[w, k], place.at(core=1)).wait_recv()
            return 0
        n = len(sent)
        if n >= 2:
            slot_free(n % 2)
        sent.append(n)
        return n % 2

    def slot_free(n):
        remote(slots3.at[n], slots3.at[n], ssend.at[n], ssend.at[n], place.at(core=1)).wait_send()

    def column_tile(side, w, k, which):
        core = 1 - c if side == 0 else c
        off = (1536 * (1 - x), 768, 1536 * x)[k]
        cols = pl.ds(aligned(core * (feed // 2) + off, 128), 2 * tile)
        dst = s.sums[w].at[:, pl.ds(aligned(off, 128), 2 * tile)]
        slot = slot_for(w, k, dst, side)
        half = width // 2

        def product(to, part):
            rows_of = pl.ds(part * half, half)
            if not which:
                return nn(turned[0, rows_of, :], feed_ref[:, cols])
            if k == 1:
                near = pl.ds(aligned(core * (feed // 2) + off, 128), tile)
                far = pl.ds(aligned(core * (feed // 2) + off + tile, 128), tile)
                return jnp.concatenate(
                    [
                        nn(turned[0, rows_of, :], feed_ref[:, near]),
                        nn(turned[core, rows_of, :], feed_ref[:, far]),
                    ],
                    axis=1,
                )
            left = jnp.where(off >= width, core, 0)
            return nn(turned[left, rows_of, :], feed_ref[:, cols])

        for part in (0, 1):
            span = pl.ds(part * half, half)
            value = product(None, part)
            if side:
                dst[span, :] = (value + dst[span, :].astype(full)).astype(low)
            else:
                slots3[slot, span, :] = value.astype(low)
        if not side:
            remote(slots3.at[slot], dst, ssend.at[slot], srecv.at[w, k], place.at(core=1)).start()

    loads = []

    def load_of(n):
        which, piece = loads[n]
        span = pl.ds(piece * width, width)
        src = full3_ref.at[span, :] if which else full12_ref.at[:, span]
        return pltpu.make_async_copy(src, wide.at[n % 2], wsem.at[n % 2])

    def fetch(src):
        loads.append(src)
        load_of(len(loads) - 1).start()

    def loaded(n):
        load_of(n).wait()
        return wide.at[n % 2]

    def w12(piece):
        return (0, piece)

    def w3(piece):
        return (1, piece)

    def tiles(body):
        def run(i, _):
            body(i * tile)
            return 0

        lax.fori_loop(0, width // tile, run, 0)

    def span_of(at, size=tile):
        return pl.ds(aligned(at, 128), size)

    def into_vec(row, value):
        for i in range(value.shape[1] // 128):
            vsum[row + i : row + i + 1, :] = value[:, 128 * i : 128 * i + 128]

    step = 64

    def row_loop(first, last, body):
        def run(i, _):
            body(pl.ds(aligned(i * step, step), step))
            return 0

        lax.fori_loop(first // step, last // step, run, 0)

    def piece_sums(row, slots, value):
        for slot in range(3):
            msum[row + slot : row + slot + 1, :] += jnp.sum(
                jnp.where(slots == slot, value, 0.0), axis=0, keepdims=True
            )

    def back_rows(normed, inverse, upstream):
        return inverse * (
            upstream
            - jnp.mean(upstream, axis=-1, keepdims=True)
            - normed * jnp.mean(upstream * normed, axis=-1, keepdims=True)
        )

    def slope_copy(piece):
        return local(
            4 + piece % 2, slope_in.at[:, pl.ds(piece * width, width)], box["slope"].at[piece % 2]
        )

    def first_copies():
        return [
            local(0, mlp_grad_in, box["mlp"]),
            local(1, branch_in, box["branch"]),
            local(2, middle_in, middle),
            local(3, cotangent_in, box["cotangent"]),
        ]

    def turned_copy(slot, src):
        return local(6 + slot, src, turned.at[slot])

    def step_ld():
        far = local(10, down_far_in, acc3)
        far.start()
        near = [
            local(11 + k, down_near_in.at[pl.ds(k * width, width), :], box["near"].at[k])
            for k in (0, 1)
        ]
        for cp in near:
            cp.start()
        copies = first_copies()
        copies[0].start()
        slope_copy(0).start()
        slope_copy(1).start()
        turned_copy(0, turned_two_in).start()
        for cp in copies[1:]:
            cp.start()
        msum[...] = jnp.zeros_like(msum)
        msum[9:12, :] = gate_sum_ref[0:3, :]
        into_vec(128 + 63, gate_sum_ref[3:4, :])
        frame_row_ref[...] = segments_ref[...] * places + positions_ref[...]
        slots_col[...] = jnp.broadcast_to(segments_ref[...], (128, rows)).T
        frame_col[...] = jnp.broadcast_to(frame_row_ref[...], (128, rows)).T
        pl.semaphore_wait(barrier, 16)
        far.wait()

        def add(i, _):
            span = pl.ds(aligned(i * 96, 96), 96)
            for k in (0, 1):
                to = pl.ds(aligned(k * width + i * 96, 96), 96)
                acc3[to, :] = acc3[to, :] + box["near"][k, span, :]
            return 0

        for cp in near:
            cp.wait()
        lax.fori_loop(0, width // 96, add, 0)
        fetch(w3(0))
        fetch(w3(1))
        copies[0].wait()

    def up_grad(n, piece):
        weight = loaded(n)
        slope_copy(piece).wait()
        slope = box["slope"].at[piece % 2]
        mlp_ref = box["mlp"]

        def body(at):
            value = nt(mlp_ref[...], weight[span_of(at), :]) * slope[:, span_of(at)].astype(full)
            rounded = value.astype(low)
            feed_ref[:, span_of(piece * width + at)] = rounded
            sums_row[0:1, span_of(at)] = jnp.sum(rounded.astype(full), axis=0, keepdims=True)

        tiles(body)
        into_vec(128 + 27 + 9 * piece, sums_row[0:1, :])
        if piece < 2:
            slope_copy(piece + 2).start()

    def step_ug(piece):
        up_grad(piece, piece)
        fetch(w3(piece + 2) if piece < 2 else w12(piece + 2))

    def hidden_grad(n, piece):
        weight = loaded(n)

        def body(at):
            value = nt(feed_ref[:, piece * width : piece * width + width], weight[span_of(at), :])
            if piece == 0:
                total[:, span_of(at)] = value
            else:
                total[:, span_of(at)] += value

        tiles(body)

    def step_hg(piece):
        hidden_grad(4 + piece, piece)
        if piece < 3:
            fetch((w12(6), w12(7), w12(3))[piece])

    def step_n2():
        for cp in first_copies()[1:]:
            cp.wait()
        branch_buf, cotangent_ref = box["branch"], box["cotangent"]
        sums_row[...] = jnp.zeros_like(sums_row)

        def norm_two(span):
            slots = slots_col[span, 0:1]
            normed, inverse = normalize_rows(middle[span, :])
            grad = total[span, :]
            grow = select_rows(modulation_ref, slots, 4, width)
            mid = cotangent_ref[span, :].astype(full) + back_rows(
                normed, inverse, grad * (1.0 + grow)
            )
            middle[span, :] = mid
            gate = select_rows(modulation_ref, slots, 2, width)
            rounded = (gate * mid).astype(low)
            feed_ref[span, 3 * width : 4 * width] = rounded
            sums_row[0:1, :] += jnp.sum(rounded.astype(full), axis=0, keepdims=True)
            piece_sums(0, slots, branch_buf[span, :] * mid)
            piece_sums(3, slots, grad)
            piece_sums(6, slots, grad * normed)

        row_loop(0, rows, norm_two)
        into_vec(128 + 18, sums_row[0:1, :])

    windows = head_windows(heads, head_width)

    def weights_copy(head):
        return pltpu.make_async_copy(
            weights_in.at[head], box["weights"].at[head % 2], psem.at[head % 2]
        )

    def grid_copy(head):
        return pltpu.make_async_copy(
            box["grid"].at[head % 2], grid_ref.at[head], gsem.at[head % 2]
        )

    def step_da():
        placed_copy = local(8, placed_in, box["placed"])
        placed_copy.start()
        weights_copy(0).start()
        weights_copy(1).start()
        turned_copy(0, turned_one_in).start()
        turned_copy(1, turned_mix_in).start()
        weight = loaded(8)
        up = box["up"]

        def body(at):
            value = nt(feed_ref[:, 3 * width :], weight[span_of(at), :])
            where = one_hot((frames, rows), 0, frame_row_ref[...])
            up[:, span_of(at)] = nn(where, value.astype(low)).astype(low)

        tiles(body)
        placed_copy.wait()

    def attend(first, last):
        placed, up, weights, grid_part = box["placed"], box["up"], box["weights"], box["grid"]
        for head in range(first, last):
            base, wide_at, offset = windows[head]
            mask = lane_mask(places, wide_at, offset, head_width)
            slot = head % 2
            weights_copy(head).wait()
            if head >= 2:
                grid_copy(head - 2).wait()
            for image in range(frames // places):
                at = slice(image * places, image * places + places)
                spans = [slice(p * width + base, p * width + base + wide_at) for p in range(3)]
                olds = [placed[at, span] for span in spans]
                query, key = [jnp.where(mask, t, jnp.zeros_like(t)) for t in olds[:2]]
                upstream = up[at, spans[0]]
                upstream = jnp.where(mask, upstream, jnp.zeros_like(upstream))
                shares = weights[slot, image]
                shares_f = shares.astype(full)
                share_grads = nt(olds[2], upstream)
                inner = jnp.sum(share_grads * shares_f, axis=0, keepdims=True)
                score_f = shares_f * (share_grads - inner)
                score = score_f.astype(low)
                if image == 0:
                    grid_part[slot] = score_f
                else:
                    grid_part[slot] += score_f
                grads = (
                    (tn(score, key) * scale).astype(low),
                    (nn(score, query) * scale).astype(low),
                    nn(shares, upstream).astype(low),
                )
                for span, old, grad in zip(spans, olds, grads):
                    placed[at, span] = jnp.where(mask, grad, old)
            grid_copy(head).start()
            if head + 2 < heads:
                weights_copy(head + 2).start()

    def step_up():
        grid_copy(heads - 2).wait()
        grid_copy(heads - 1).wait()
        grid_far_copy().start()
        fetch(w12(0))
        fetch(w12(1))
        placed = box["placed"]
        for piece in range(3):

            def body(at):
                back = one_hot((rows, frames), 1, frame_col[:, 0:1])
                span = span_of(piece * width + at)
                rounded = nn(back, placed[:, span]).astype(low)
                feed_ref[:, span] = rounded
                if piece != 1:
                    sums_row[0:1, span_of(at)] = jnp.sum(
                        rounded.astype(full), axis=0, keepdims=True
                    )

            tiles(body)
            if piece != 1:
                into_vec(128 + 9 * (piece // 2), sums_row[0:1, :])

    def step_t1():
        turned_copy(0, turned_one_in).wait()
        turned_copy(1, turned_mix_in).wait()
        local(9, tokens_in, box["tokens"]).start()

    def step_h(piece):
        hidden_grad(9 + piece, piece)
        if piece == 0:
            fetch(w12(2))

    def step_n1():
        local(9, tokens_in, box["tokens"]).wait()
        tokens_ref = box["tokens"]

        def norm_one(span):
            slots = slots_col[span, 0:1]
            normed, inverse = normalize_rows(tokens_ref[span, :].astype(full))
            grad = total[span, :]
            grow = select_rows(modulation_ref, slots, 1, width)
            middle[span, :] += back_rows(normed, inverse, grad * (1.0 + grow))
            piece_sums(16, slots, grad)
            piece_sums(19, slots, grad * normed)

        row_loop(0, rows, norm_one)
        put_tokens().start()
        mine_ref[...] = msum[...].astype(low)
        put_mine().start()

    def put_tokens():
        return local(13, middle, tokens_grad_ref)

    def put_mine():
        return local(14, mine_ref, spread_ref.at[row_of(0, place.chip(), 0)])

    def row_of(xx, chip, cc):
        return (x if xx == 0 else 1 - x) * 16 + chip * 2 + (c if cc == 0 else 1 - c)

    def spread(slot, row, device, src=None):
        return remote(
            spread_ref.at[row] if src is None else src,
            spread_ref.at[row],
            msend.at[slot],
            mrecv.at[slot],
            device,
        )

    def first(slot, device):
        return spread(slot, row_of(0, place.chip(), 0), device, mine_ref)

    def mz(j, r=False):
        if not r:
            return first(j, place.at(j=j))
        return spread(j, row_of(0, place.chip(j), 0), place.at(j=j))

    def my(j, r=False):
        if j == 0 and not r:
            return first(4, place.at(y=1))
        return spread(4 + j, row_of(0, place.chip(j, 1 if r else 0), 0), place.at(y=1))

    def mx(j, yy, r=False):
        if j == 0 and yy == 0 and not r:
            return first(8, place.at(x=1))
        row = row_of(1 if r else 0, place.chip(j, yy), 0)
        return spread(8 + 2 * j + yy, row, place.at(x=1))

    def ms(xx, j, yy, r=False):
        slot = 16 + xx * 8 + 2 * j + yy
        if xx == 0 and j == 0 and yy == 0 and not r:
            return first(slot, place.at(core=1))
        return spread(slot, row_of(xx, place.chip(j, yy), 1 if r else 0), place.at(core=1))

    def step_mg(n):
        if n == 0:
            for j in (1, 2, 3):
                mz(j).start()
            my(0).start()
            mx(0, 0).start()
            ms(0, 0, 0).start()
        elif n == 1:
            for j in (1, 2, 3):
                mz(j, True).wait_recv()
                my(j).start()
                mx(j, 0).start()
                ms(0, j, 0).start()
        elif n == 2:
            for j in range(4):
                my(j, True).wait_recv()
                mx(j, 1).start()
                ms(0, j, 1).start()
        elif n == 3:
            for yy in (0, 1):
                for j in range(4):
                    mx(j, yy, True).wait_recv()
                    ms(1, j, yy).start()
        else:
            for xx in (0, 1):
                for yy in (0, 1):
                    for j in range(4):
                        ms(xx, j, yy, True).wait_recv()

    def vcopy(n):
        if n < 3:
            device = (place.at(core=1), place.at(x=1), place.at(y=1))[n]
            return remote(vsum, vbuf.at[n], vsend.at[n], vrecv.at[n], device)
        return remote(vsum, vbuf.at[3 + z], vsend.at[n], vrecv.at[n], place.at(j=n - 2))

    def varrive(j):
        remote(
            vsum, vbuf.at[3 + place.zz(j)], vsend.at[2 + j], vrecv.at[2 + j], place.at(j=j)
        ).wait_recv()

    def step_v(n):
        if n == 0:
            vsum[0:128, :] = hist[...]
            vcopy(0).start()
        elif n < 4:
            vcopy(n - 1).wait()
            vsum[...] += vbuf[n - 1]
            if n < 3:
                vcopy(n).start()
            else:
                for j in (1, 2, 3):
                    vcopy(2 + j).start()
                vbuf[3 + z] = vsum[...]
        else:
            for j in (1, 2, 3):
                varrive(j)
            vec_out_ref[...] = vbuf[3] + vbuf[4] + vbuf[5] + vbuf[6]

    half_places = places // 2

    def grid_far_copy():
        span = pl.ds(aligned((1 - c) * half_places, 8), half_places)
        return remote(
            grid_ref.at[:, span, :], grid_far_ref, hsem.at[2], hsem.at[3], place.at(core=1)
        )

    def hist_copies(n):
        span = 16
        near = pl.ds(aligned(c * half_places + n * span, 8), span)
        far = pl.ds(n * span, span)
        return [
            pltpu.make_async_copy(
                grid_ref.at[:, near, :], box["hist"].at[n % 2, 0], hsem.at[n % 2]
            ),
            pltpu.make_async_copy(
                grid_far_ref.at[:, far, :], box["hist"].at[n % 2, 1], hsem.at[4 + n % 2]
            ),
        ]

    def step_hi(quarter):
        if quarter == 0:
            grid_far_copy().wait()
            buckets_t[...] = buckets_ref[...].T
            hist[...] = jnp.zeros_like(hist)
            for cp in hist_copies(0):
                cp.start()
        for n in (2 * quarter, 2 * quarter + 1):
            if n + 1 < 8:
                for cp in hist_copies(n + 1):
                    cp.start()
            for cp in hist_copies(n):
                cp.wait()

            def body(a8, _):
                base = aligned(a8 * 8, 8)
                at = pl.ds(aligned(c * half_places + n * 16 + base, 8), 8)
                index8 = buckets_t[at, :]
                values8 = box["hist"][n % 2, 0, :, pl.ds(base, 8), :]
                values8 = values8 + box["hist"][n % 2, 1, :, pl.ds(base, 8), :]
                out = hist[...]
                for a in range(8):
                    index = index8[a : a + 1, :]
                    lower, upper = index & 127, index >> 7
                    mask = lax.broadcasted_iota(jnp.int32, (8, places), 0) == upper
                    values = jnp.where(mask[None], values8[:, a : a + 1, :], 0.0)
                    left = values.reshape(heads * 8, places).astype(low)
                    right = one_hot((128, places), 0, lower)
                    out += nt(left, right)
                hist[...] = out
                return 0

            lax.fori_loop(0, 2, body, 0)

    def step_modg():
        pieces_ref, mod_ref = box["pieces"], box["mod"]
        get_pieces = local(15, spread_ref, pieces_ref)
        get_mod = local(16, mod_in, mod_ref)
        put_mine().wait()
        get_pieces.start()
        get_mod.start()

        def place_rows(p, devices):
            base = 3 * (p - 2) if p >= 2 else 3 * p
            shape = (devices * 16, devices * 8)
            r = lax.broadcasted_iota(jnp.int32, shape, 0)
            q = lax.broadcasted_iota(jnp.int32, shape, 1)
            same = (r // 16 == q // 8) & (r % 16 - base == q % 8) & (q % 8 < 3)
            return same.astype(full).astype(low)

        activated = inbox_ref[...].reshape(256, 128).astype(low)
        put_three().wait()
        get_pieces.wait()
        get_mod.wait()
        cond_total = jnp.zeros((128, mod_ref.shape[0]), full)
        puts = []
        for p in range(6):
            half = 0 if p >= 2 else 16
            span = slice(width * p, width * p + width)
            pieces = pieces_ref[:, half : half + 16, :].reshape(512, width)
            where = place_rows(p, 32)
            left = nn(where, activated).astype(low)
            total[72 * p : 72 * p + 72, :] = tn(left, pieces)[0:72]
            puts.append(
                local(17 + p, total.at[pl.ds(72 * p, 72), :], gmod_ref.at[:, pl.ds(width * p, width)])
            )
            puts[-1].start()
            ones = jnp.sum(where.astype(full), axis=1, keepdims=True).astype(low)
            gmod_sum_ref[:, span] = tn(jnp.broadcast_to(ones, (512, 128)), pieces)[0:8]
            mine = pieces_ref[pl.ds(x * 16, 16), half : half + 16, :].reshape(256, width)
            cond_rows = tn(place_rows(p, 16), mine).astype(low)
            cond_total += nt(cond_rows, mod_ref[:, span])
        cpart[:, :, 0 : mod_ref.shape[0]] = cond_total.reshape(16, 8, mod_ref.shape[0])
        for cp in puts:
            cp.wait()

    def ccopy(k, r=False):
        dest = (d + k) % 16
        src = (d + 16 - k) % 16
        return remote(
            cpart.at[dest], cond_ref.at[src if r else d], csend.at[k], crecv.at[k], (x, dest)
        )

    def put_three():
        return local(23, total.at[pl.ds(0, 288), :], out3_ref)

    def end_copy(w):
        chip = place.chip(0, 0)
        return remote(
            s.acc(w, chip, "all"), sib_end.at[w], fsend.at[w], frecv.at[w], place.at(core=1)
        )

    def step_final(w):
        s.f(w, "other").wait()
        s.f(w, "ad").wait()
        chip = place.chip(0, 0)
        if w == 2:
            rows3 = pl.ds(aligned(chip * 288, 16), 288)
            total[0:288, :] = acc3[rows3, :].astype(full) + e2[1].astype(full)
            put_three().start()
        else:
            s.add(w, chip, "all", s.ends[w].at[1])
            end_copy(w).start()

    def out_piece(at):
        stage, row = (middle, 72 * at) if at < 7 else (total, 432)
        if at < 3:
            to = out_packed_ref.at[:, pl.ds(width * at, width)]
        elif at == 3:
            to = out_out_ref
        else:
            to = out_up_ref.at[:, pl.ds(width * (at - 4), width)]
        return local(24 + at, stage.at[pl.ds(row, 72), :], to)

    def step_write(w):
        if w == 1:
            put_tokens().wait()
        end_copy(w).wait()
        own_rows = pl.ds(aligned(place.chip(0, 0) * 144, 16), 144)

        def value(half, span):
            mine = s.sums[w][own_rows, span].astype(full)
            theirs = sib_end[w, :, span].astype(full)
            both = jnp.where(c == half, mine, theirs)
            return jnp.where(c == 0, both[0:72], both[72:144])

        part_width = feed // 16
        for piece in range(4):
            at = 4 * w + piece
            stage, row = (middle, 72 * at) if at < 7 else (total, 432)
            if w == 0:
                start = width * (piece % 2)
                stage[row : row + 72, :] = value(piece // 2, slice(start, start + width))
            else:
                for n in range(4):
                    start = part_width * (2 * piece + n // 2)
                    stage[row : row + 72, part_width * n : part_width * (n + 1)] = value(
                        n % 2, slice(start, start + part_width)
                    )
            out_piece(at).start()

    def perform(e):
        name, rest = e[0], e[1:]
        if name == UG:
            step_ug(*rest)
        elif name == D2S:
            turned_copy(0, turned_two_in).wait()
            for k in range(3):
                column_tile(0, 1, k, False)
        elif name == D2A:
            column_tile(1, 1, 0, False)
        elif name == D2B:
            for k in (1, 2):
                column_tile(1, 1, k, False)
        elif name == D1S:
            for k in range(3):
                column_tile(0, 0, k, True)
        elif name == D1A:
            column_tile(1, 0, 0, True)
        elif name == D1B:
            for k in (1, 2):
                column_tile(1, 0, k, True)
        elif name == ATT:
            attend(*rest)
        elif name == COND:
            for k in range(1, 16):
                ccopy(k).start()
            cond_ref[d] = cpart[d]
        else:
            table[name](*rest)

    table = {
        START_X: s.start_x,
        START_Y: s.start_y,
        START_E: s.start_e,
        START_F: s.start_f,
        ON_X: s.on_x,
        ON_Y: s.on_y,
        ON_Z: s.on_z,
        LD: step_ld,
        HG: step_hg,
        N2: step_n2,
        DA: step_da,
        UP: step_up,
        T1: step_t1,
        H: step_h,
        N1: step_n1,
        MG: step_mg,
        VEC: step_v,
        HI: step_hi,
        MODG: step_modg,
        FINAL: step_final,
        WRITE: step_write,
    }
    V = pltpu.VMEM
    scopes = {
        LD: {
            "slope": V((2, rows, width), low),
            "branch": V((rows, width), full),
            "mlp": V((rows, width), low),
            "cotangent": V((rows, width), low),
        },
        DA: {
            "placed": V((frames, 3 * width), low),
            "up": V((frames, width), low),
            "weights": V((2, 3, places, places), low),
            "grid": V((2, places, places), full),
        },
        T1: {"tokens": V((rows, width), low)},
        HI: {"hist": V((2, 2, heads, 16, places), full)},
        MODG: {"pieces": V((32, 32, width), low), "mod": V(mod_in.shape, low)},
    }
    lasts = {LD: (N2,), DA: (UP,), T1: (N1,), HI: (HI, 3), MODG: (MODG,)}
    at = 0
    while at < len(order):
        name = order[at][0]
        if name not in scopes:
            perform(order[at])
            at += 1
            continue
        end = at
        while order[end] != lasts[name]:
            end += 1
        parts = list(scopes[name])

        def scope(*refs):
            box.update(zip(parts, refs))
            if "slope" in parts:
                box["near"] = wide
            for e in order[at : end + 1]:
                perform(e)

        pl.run_scoped(scope, *[scopes[name][k] for k in parts])
        at = end + 1
    for k in range(1, 16):
        ccopy(k, True).wait_recv()
        ccopy(k).wait_send()
    for n in range(8):
        out_piece(n).wait()
    for n in range(2):
        slot_free(n)
    for j in (1, 2, 3):
        vcopy(2 + j).wait_send()
        mz(j).wait_send()
    for j in range(4):
        my(j).wait_send()
        for yy in (0, 1):
            mx(j, yy).wait_send()
            for xx in (0, 1):
                ms(xx, j, yy).wait_send()
    for w in range(3):
        s.finish(w)


backward_order = (
    (LD,),
    (START_Y, 2,),
    (START_X, 2, 2,),
    (UG, 0,),
    (UG, 1,),
    (UG, 2,),
    (ON_X, 2, 2, 1,),
    (UG, 3,),
    (START_X, 2, 1,),
    (D2S,),
    (START_X, 2, 3,),
    (D2A,),
    (ON_X, 2, 1, 1,),
    (D2B,),
    (ON_X, 2, 2, 0,),
    (HG, 0,),
    (ON_Y, 2, 2,),
    (HG, 1,),
    (START_X, 1, 2,),
    (HG, 2,),
    (START_X, 1, 3,),
    (ON_X, 2, 3, 1,),
    (START_X, 1, 1,),
    (HG, 3,),
    (ON_Y, 2, 0,),
    (START_E, 2,),
    (N2,),
    (DA,),
    (ON_X, 1, 2, 1,),
    (ON_X, 1, 2, 0,),
    (ON_X, 2, 1, 0,),
    (ON_Y, 2, 1,),
    (ON_X, 2, 3, 0,),
    (ON_Y, 2, 3,),
    (ATT, 0, 2,),
    (ATT, 2, 4,),
    (ATT, 4, 6,),
    (ON_Z, 2, 1,),
    (ON_Z, 2, 2,),
    (ATT, 6, 8,),
    (ATT, 8, 10,),
    (ON_X, 1, 3, 1,),
    (ON_X, 1, 1, 1,),
    (ON_Y, 1, 2,),
    (ON_X, 1, 3, 0,),
    (ATT, 10, 12,),
    (ON_Z, 2, 3,),
    (ATT, 12, 14,),
    (START_F, 2,),
    (ATT, 14, 16,),
    (UP,),
    (START_Y, 1,),
    (T1,),
    (ON_Y, 1, 3,),
    (D1S,),
    (D1A,),
    (START_X, 0, 2,),
    (D1B,),
    (ON_X, 1, 1, 0,),
    (H, 0,),
    (START_X, 0, 1,),
    (H, 1,),
    (ON_X, 0, 2, 1,),
    (H, 2,),
    (ON_Y, 1, 1,),
    (N1,),
    (START_X, 0, 3,),
    (ON_X, 0, 1, 1,),
    (MG, 0,),
    (ON_X, 0, 2, 0,),
    (HI, 0,),
    (ON_Z, 1, 2,),
    (ON_Y, 0, 2,),
    (ON_Y, 1, 0,),
    (START_E, 1,),
    (ON_Z, 1, 1,),
    (ON_X, 0, 3, 1,),
    (MG, 1,),
    (ON_Z, 1, 3,),
    (HI, 1,),
    (START_F, 1,),
    (START_Y, 0,),
    (ON_X, 0, 1, 0,),
    (HI, 2,),
    (HI, 3,),
    (VEC, 0,),
    (ON_Y, 0, 1,),
    (ON_X, 0, 3, 0,),
    (VEC, 1,),
    (ON_Y, 0, 3,),
    (MG, 2,),
    (ON_Z, 0, 2,),
    (MG, 3,),
    (VEC, 2,),
    (ON_Z, 0, 1,),
    (FINAL, 2,),
    (VEC, 3,),
    (ON_Y, 0, 0,),
    (START_E, 0,),
    (FINAL, 1,),
    (ON_Z, 0, 3,),
    (START_F, 0,),
    (MG, 4,),
    (MODG,),
    (COND,),
    (WRITE, 1,),
    (VEC, 4,),
    (FINAL, 0,),
    (WRITE, 0,),
)


def backward_pass(heads, big, small):
    any_, vm = pl.BlockSpec(memory_space=pl.ANY), pl.BlockSpec(memory_space=pltpu.VMEM)
    V, D, S = pltpu.VMEM, pltpu.SemaphoreType.DMA, jax.ShapeDtypeStruct
    rows, width = big[-3].shape
    feed = 4 * width
    places = small[-1].shape[0]
    flat = V((3, 144, 1536), low)
    tall = V((3, 192, width), low)
    return pl.pallas_call(
        functools.partial(backward_kernel, heads, backward_order),
        out_shape=(
            S((72, 3 * width), full),
            S((72, width), full),
            S((72, feed), full),
            S((72, 6 * width), full),
            S((rows, width), full),
            S((32, 32, width), low),
            S((heads, places, places), full),
            S((heads, places // 2, places), full),
            S((288, width), full),
            S((200, 128), full),
            S((8, 6 * width), full),
            S((16, 8, 128), full),
        ),
        in_specs=[any_] * len(big) + [vm] * len(small),
        out_specs=(any_,) * 9 + (vm,) * 3,
        scratch_shapes=[
            V((width, 2 * width), low),
            V((width, 2 * width), low),
            V((2 * width, width), low),
            V((6, 144, 768), low),
            V((6, 144, 768), low),
            V((6, 96, width), low),
            flat,
            flat,
            tall,
            flat,
            flat,
            tall,
            V((2, 144, 2 * width), low),
            V((2, 144, 2 * width), low),
            V((2, 288, width), low),
            V((2, width, 768), low),
            V((2, width, rows), low),
            V((rows, feed), low),
            V((2, width, width), low),
            V((rows, width), full),
            V((rows, width), full),
            V((2, 144, 2 * width), low),
            V((200, 128), full),
            V((7, 200, 128), full),
            V((32, width), full),
            V((32, width), low),
            V((16, 8, 128), full),
            V((128, 128), full),
            V((8, width), full),
            V((places, places), jnp.int32),
            V((rows, 128), jnp.int32),
            V((1, rows), jnp.int32),
            V((rows, 128), jnp.int32),
            D((3, 15)),
            D((3, 15)),
            D((2,)),
            D((3, 6)),
            D((32,)),
            D((2,)),
            D((6,)),
            D((6,)),
            D((32,)),
            D((32,)),
            D((16,)),
            D((16,)),
            D((2,)),
            D((2,)),
            D((2,)),
            D((2,)),
            D((6,)),
        ],
        compiler_params=pltpu.CompilerParams(
            collective_id=1, has_side_effects=True, vmem_limit_bytes=64 * 2**20
        ),
    )(*big, *small)


def shards(
    tokens,
    condition,
    segments,
    positions,
    buckets,
    modulator,
    modulator_bias,
    projector,
    projector_bias,
    position_table,
    output_weight,
    output_bias,
    up_weight,
    up_bias,
    down_weight,
    down_bias,
    cotangent,
):
    heads, bucket_count = position_table.shape
    image_tokens = buckets.shape[0]
    rows, model_width = tokens.shape[1], tokens.shape[2]
    images = condition.shape[1]
    shard = modulator.shape[0]
    feed_width = up_weight.shape[1]
    dp_index = lax.axis_index("dp")
    stream_index = lax.axis_index("stream")
    low = jnp.bfloat16
    full = jnp.float32

    def gather(part):
        return lax.all_gather(part, "dp", axis=0, tiled=True)

    inputs = tokens[0].astype(full)
    slot_ids, places = segments[0], positions[0]
    silu_value, silu_back = jax.vjp(jax.nn.silu, condition[0].astype(full))
    activated = silu_value.astype(low)
    activated_both = lax.all_gather(activated, ("stream", "dp"), axis=0, tiled=True)
    slots = activated_both.shape[0]
    activated_own = lax.dynamic_slice(activated_both, (0, dp_index * shard), (slots, shard))
    stream_slots = slots // 2
    partial = jnp.dot(
        lax.dynamic_slice(activated_own, (stream_index * stream_slots, 0), (stream_slots, shard)),
        modulator,
        preferred_element_type=full,
    )
    bias_parts = (modulator_bias, projector_bias, output_bias, up_bias, down_bias)
    bias_all = lax.all_gather(jnp.concatenate(bias_parts), "dp", axis=0)
    bias_full = []
    start = 0
    for part in bias_parts:
        bias_full.append(bias_all[:, start : start + part.shape[0]].reshape(-1).astype(full))
        start += part.shape[0]
    modulation = (
        lax.psum_scatter(partial, "dp", scatter_dimension=0, tiled=True) + bias_full[0]
    )
    projector_all = gather(projector)
    output_all = gather(output_weight)
    up_all = gather(up_weight)
    down_all = gather(down_weight)
    grid = bias_grid(position_table, buckets)
    local = slot_ids[:, None]
    per_token = jnp.where(
        local == 0, modulation[0:1], jnp.where(local == 1, modulation[1:2], modulation[2:3])
    )
    shift_attn, scale_attn, gate_attn, shift_mlp, scale_mlp, gate_mlp = jnp.split(
        per_token, 6, axis=1
    )
    normed_one, inverse_one = normalize(inputs)
    hidden_one = (normed_one * (1.0 + scale_attn) + shift_attn).astype(low)
    packed_bias = jnp.concatenate(
        [bias_full[1][:model_width], jnp.zeros((model_width,), full), bias_full[1][model_width:]]
    )
    packed = (
        jnp.dot(hidden_one, projector_all, preferred_element_type=full) + packed_bias
    ).astype(low)
    attended, placed, weights = attend_forward(packed, slot_ids, places, grid)
    branch_attn = jnp.dot(attended, output_all, preferred_element_type=full) + bias_full[2]
    middle = inputs + gate_attn * branch_attn
    normed_two, inverse_two = normalize(middle)
    hidden_two = (normed_two * (1.0 + scale_mlp) + shift_mlp).astype(low)
    up_output = jnp.dot(hidden_two, up_all, preferred_element_type=full) + bias_full[3]
    activation, gelu_back = jax.vjp(lambda v: jax.nn.gelu(v, approximate=True), up_output)
    activation_low = activation.astype(low)
    branch_mlp = jnp.dot(activation_low, down_all, preferred_element_type=full) + bias_full[4]
    result = (middle + gate_mlp * branch_mlp).astype(low)

    upstream = cotangent[0].astype(full)
    mlp_grad = (gate_mlp * upstream).astype(low)
    gate_mlp_grad = branch_mlp * upstream

    def scatter(grad):
        part = lax.psum_scatter(grad.astype(low), "dp", scatter_dimension=0, tiled=True)
        return lax.psum(part, "stream").astype(full)

    down_grad = scatter(
        jnp.einsum("tf,td->fd", activation_low, mlp_grad, preferred_element_type=full)
    )
    activation_grad = jnp.einsum("td,fd->tf", mlp_grad, down_all, preferred_element_type=full)
    up_grad_low = gelu_back(activation_grad)[0].astype(low)
    up_grad = scatter(
        jnp.einsum("td,tf->df", hidden_two, up_grad_low, preferred_element_type=full)
    )
    hidden_two_grad = jnp.einsum(
        "tf,df->td", up_grad_low, up_all, preferred_element_type=full
    )
    middle_grad = upstream + normalize_back(
        normed_two, inverse_two, hidden_two_grad * (1.0 + scale_mlp)
    )
    attn_grad = (gate_attn * middle_grad).astype(low)
    gate_attn_grad = branch_attn * middle_grad
    output_grad = scatter(
        jnp.einsum("td,te->de", attended, attn_grad, preferred_element_type=full)
    )
    attended_grad = jnp.einsum(
        "te,de->td", attn_grad, output_all, preferred_element_type=full
    ).astype(low)
    packed_grad, grid_grad = attend_backward(placed, weights, attended_grad, slot_ids, places)
    projector_grad = scatter(
        jnp.einsum("td,te->de", hidden_one, packed_grad, preferred_element_type=full)
    )
    table_grad = table_histogram(grid_grad, buckets, bucket_count)
    packed_sums = jnp.sum(packed_grad.astype(full), axis=0)
    sums = (
        table_grad.reshape(-1),
        packed_sums[:model_width],
        packed_sums[2 * model_width :],
        jnp.sum(attn_grad.astype(full), axis=0),
        jnp.sum(up_grad_low.astype(full), axis=0),
        jnp.sum(mlp_grad.astype(full), axis=0),
    )
    small = lax.psum(jnp.concatenate(sums), ("stream", "dp"))
    table_count = heads * bucket_count
    table_total = small[:table_count].reshape(heads, bucket_count)
    bias_grads = []
    start = table_count
    for part in bias_parts[1:]:
        size = part.shape[0]
        bias_grads.append(lax.dynamic_slice(small, (start + dp_index * size,), (size,)))
        start += size * (model_width // shard)
    hidden_one_grad = jnp.einsum(
        "te,de->td", packed_grad, projector_all, preferred_element_type=full
    )
    inputs_grad = middle_grad + normalize_back(
        normed_one, inverse_one, hidden_one_grad * (1.0 + scale_attn)
    )
    token_mod_grad = jnp.concatenate(
        [
            hidden_one_grad,
            hidden_one_grad * normed_one,
            gate_attn_grad,
            hidden_two_grad,
            hidden_two_grad * normed_two,
            gate_mlp_grad,
        ],
        axis=1,
    )
    modulation_grad = jnp.stack(
        [jnp.sum(jnp.where(local == slot, token_mod_grad, 0.0), axis=0) for slot in range(images)]
    ).astype(low)
    modulation_grad_both = lax.all_gather(modulation_grad, ("stream", "dp"), axis=0, tiled=True)
    modulator_grad = jnp.einsum(
        "id,ie->de", activated_own, modulation_grad_both, preferred_element_type=full
    )
    bias_width = modulator_bias.shape[0]
    modulator_bias_grad = jnp.sum(
        lax.dynamic_slice(
            modulation_grad_both, (0, dp_index * bias_width), (slots, bias_width)
        ).astype(full),
        axis=0,
    )
    activated_part = jnp.einsum(
        "ie,de->id",
        lax.dynamic_slice(
            modulation_grad_both, (stream_index * stream_slots, 0), (stream_slots, 6 * model_width)
        ),
        modulator,
        preferred_element_type=full,
    )
    activated_grad = (
        lax.all_to_all(
            activated_part.reshape(-1, images, shard), "dp", split_axis=0, concat_axis=0, tiled=True
        )
        .transpose(1, 0, 2)
        .reshape(images, model_width)
    )
    condition_grad = silu_back(activated_grad)[0]
    return (
        result[None],
        inputs_grad[None],
        condition_grad[None],
        modulator_grad,
        modulator_bias_grad,
        projector_grad,
        bias_grads[0],
        table_total,
        output_grad,
        bias_grads[1],
        up_grad,
        bias_grads[2],
        down_grad,
        bias_grads[3],
    )


def own_shards(
    tokens,
    condition,
    segments,
    positions,
    buckets,
    modulator,
    modulator_bias,
    projector,
    projector_bias,
    position_table,
    output_weight,
    output_bias,
    up_weight,
    up_bias,
    down_weight,
    down_bias,
    cotangent,
):
    heads, bucket_count = position_table.shape
    image_tokens = buckets.shape[0]
    rows, model_width = tokens.shape[1], tokens.shape[2]
    images = condition.shape[1]
    shard = modulator.shape[0]
    devices = model_width // shard
    chips = devices // 2
    dp_index = lax.axis_index("dp")
    full = jnp.float32
    (
        full12,
        full3,
        placed,
        weights,
        branch,
        middle,
        slope,
        result,
        mlp_grad,
        turned_one,
        turned_mix,
        turned_two,
        down_near,
        down_far,
        inbox,
        modulation,
        gate_sums,
    ) = forward_pass(
        heads,
        condition[0],
        modulator,
        jnp.concatenate([modulator_bias, projector_bias, output_bias, up_bias, down_bias])[None],
        projector,
        output_weight,
        up_weight,
        down_weight,
        tokens[0],
        cotangent[0],
        segments,
        positions,
        position_table,
        buckets,
    )
    (
        projector_grad,
        output_grad,
        up_grad,
        modulator_grad,
        inputs_grad,
        _,
        _,
        _,
        down_grad,
        small,
        modulator_sums,
        cond_parts,
    ) = backward_pass(
        heads,
        (
            full12,
            full3,
            placed,
            weights,
            branch,
            middle,
            slope,
            mlp_grad,
            turned_one,
            turned_mix,
            turned_two,
            down_near,
            down_far,
            cotangent[0],
            tokens[0],
            modulator,
        ),
        (inbox, modulation, gate_sums, segments, positions, buckets),
    )
    small = small.reshape(-1)
    table_count = 128 * 128
    table_total = small[:table_count].reshape(heads, -1)[:, :bucket_count]
    bias_grads = []
    start = table_count
    for part in (projector_bias, output_bias, up_bias, down_bias):
        size = part.shape[0]
        at = dp_index * size
        if size == 4 * shard:
            at = (dp_index % 2) * chips * size + (dp_index // 2) * size
        bias_grads.append(lax.dynamic_slice(small, (start + at,), (size,)))
        start += size * devices
    bias_width = modulator_bias.shape[0]
    modulator_bias_grad = lax.dynamic_slice(
        modulator_sums, (0, dp_index * bias_width), (1, bias_width)
    )[0]
    activated_grad = (
        cond_parts[:, :images, :shard].transpose(1, 0, 2).reshape(images, model_width)
    )
    _, silu_back = jax.vjp(jax.nn.silu, condition[0].astype(full))
    condition_grad = silu_back(activated_grad)[0]
    return (
        result[None],
        inputs_grad[None],
        condition_grad[None],
        modulator_grad,
        modulator_bias_grad,
        projector_grad,
        bias_grads[0],
        table_total,
        output_grad,
        bias_grads[1],
        up_grad,
        bias_grads[2],
        down_grad,
        bias_grads[3],
    )


def solution(mesh):
    in_specs = (
        P("stream", "dp", None),
        P("stream", "dp", None),
        P("stream", "dp"),
        P("stream", "dp"),
        P(),
        P("dp", None),
        P("dp"),
        P("dp", None),
        P("dp"),
        P(),
        P("dp", None),
        P("dp"),
        P("dp", None),
        P("dp"),
        P("dp", None),
        P("dp"),
        P("stream", "dp", None),
    )
    out_specs = (
        P("stream", "dp", None),
        P("stream", "dp", None),
        P("stream", "dp", None),
        P("dp", None),
        P("dp"),
        P("dp", None),
        P("dp"),
        P(),
        P("dp", None),
        P("dp"),
        P("dp", None),
        P("dp"),
        P("dp", None),
        P("dp"),
    )
    own = dict(mesh.shape) == {'stream': 2, 'dp': 16}
    return jax.shard_map(own_shards if own else shards, mesh=mesh, in_specs=in_specs, out_specs=out_specs, check_vma=False)
```
